256 devices in a mesh: gy: 8 (over y, core), gx: 32 (over z, x).
Axes of the slice: x: 4, y: 4, z: 8, core: 2. Of those that a mesh axis runs over, the one named last changes fastest.
Arguments:
- tokens: bfloat16 [128, 96, 4096], P('gy', None, 'gx'), may hold values from -6 to 6
- in_weight: bfloat16 [96, 419], replicated, may hold values from -0.625 to 0.625
- conv_weight: float32 [3, 3, 224], replicated, may hold values from -2 to 2
- conv_bias: float32 [224], replicated, may hold values from -0.5 to 0.5
- step_bias: float32 [3], replicated, may hold values from -4 to -2
- decay_log: float32 [3], replicated, may hold values from -7.7 to 0, as said below
- skip_gain: float32 [3], replicated, may hold values from 0.5 to 1.5
- norm_gain: float32 [192], replicated, may hold values from 0.1 to 1.9
- out_weight: bfloat16 [192, 96], replicated, may hold values from -0.4375 to 0.4375
Outputs:
- layer_out: bfloat16 [128, 96, 4096], P('gy', None, 'gx')
The draws below stay inside these ranges and needn't reach their ends.
Inputs may be any that keep to these rules, and one draw needn't show every extreme that they name: `decay_log`: one value a head.
All inputs are finite; a program needn't handle non-finite values.
Results may differ from the reference program's by a relative error of at most 0.00325.
The reference program's roundings to bfloat16 on the way (of `projected`, `activated` and `normed`) count: a program that leaves them out, or rounds other values in their place, can miss the bound.
Values may be sent and summed in bfloat16 or wider, within the bound.
No kernel may reach another device: no remote copies, remote signals or barrier semaphores. Data moves between devices by JAX's collectives and lax.ppermute only.
A program may use at most 128 MiB of HBM per device.

```python
import math
import jax
import jax.numpy as jnp
from jax import lax

D = 96
INNER = 192
STATE = 16
HEAD_DIM = 64
HEADS = 3
CONV_CH = 224
PROJ = 419
ROWS = 128
COLS = 4096


def draw_decay_log(key, part):
    key = jax.random.fold_in(key, 7)
    lowest, highest = (math.log(0.002), math.log(1.0))
    return jax.random.uniform(key, (HEADS,), jnp.float32, lowest, highest)


def level_of(stream_key, dims, pieces, smallest, high):
    gain, own = 1.0, jax.random.fold_in(stream_key, 6)
    for axis_at, shards_of in pieces:
        heights = jnp.exp(jax.random.uniform(jax.random.fold_in(own, axis_at), (shards_of,), jnp.float32, smallest / len(pieces), high / len(pieces)))
        gain = gain * jnp.repeat(heights, dims[axis_at] // shards_of).reshape([-1 if axis == axis_at else 1 for axis in range(len(dims))])
    return gain


def noise(stream_key, shape, width, bound, pieces=(), kind=jnp.bfloat16):
    array = width * jax.random.normal(stream_key, shape, jnp.float32)
    if pieces:
        array = array * level_of(stream_key, shape, pieces, -0.22, 0.18)
    return jnp.clip(array, -bound, bound).astype(kind)


def setup_inputs(seed: int = 0) -> dict:
    splits = jax.random.split(jax.random.key(seed), 10)
    tokens = noise(splits[0], (ROWS, D, COLS), 1.0, 6.0, ((0, 8), (2, 32)))
    in_weight = noise(splits[1], (D, PROJ), D ** -0.5, 0.625)
    conv_weight = noise(splits[2], (3, 3, CONV_CH), 9 ** -0.5, 2.0, (), jnp.float32)
    conv_bias = jnp.clip(jax.random.uniform(splits[3], (CONV_CH,), jnp.float32, -0.5, 0.5), -0.5, 0.5)
    step_bias = jnp.clip(jax.random.uniform(splits[4], (HEADS,), jnp.float32, -4.0, -2.0), -4.0, -2.0)
    decay_log = draw_decay_log(jax.random.fold_in(splits[9], 71), 0)
    skip_gain = jnp.clip(jax.random.uniform(splits[6], (HEADS,), jnp.float32, 0.5, 1.5), 0.5, 1.5)
    norm_gain = jnp.clip(1.0 + 0.18 * jax.random.normal(splits[7], (INNER,), jnp.float32), 0.1, 1.9)
    out_weight = noise(splits[8], (INNER, D), INNER ** -0.5, 0.4375)
    return dict(tokens=tokens, in_weight=in_weight, conv_weight=conv_weight, conv_bias=conv_bias, step_bias=step_bias, decay_log=decay_log, skip_gain=skip_gain, norm_gain=norm_gain, out_weight=out_weight)


norm_eps = 1e-05

def reference(tokens, in_weight, conv_weight, conv_bias, step_bias, decay_log, skip_gain, norm_gain, out_weight):
    highest = lax.Precision.HIGHEST
    projected = jnp.einsum('rdc,dk->rkc', tokens.astype(jnp.float32), in_weight.astype(jnp.float32), precision=highest).astype(jnp.bfloat16)
    conv_in = projected[:, INNER:INNER + CONV_CH, :].astype(jnp.float32)
    padded = jnp.pad(conv_in, ((1, 1), (0, 0), (1, 1)))
    summed = jnp.zeros((ROWS, CONV_CH, COLS), jnp.float32) + conv_bias[None, :, None]
    for shift_row in range(3):
        for shift_col in range(3):
            summed = summed + conv_weight[shift_row, shift_col][None, :, None] * padded[shift_row:shift_row + ROWS, :, shift_col:shift_col + COLS]
    activated = jax.nn.silu(summed).astype(jnp.bfloat16)
    step_raw = projected[:, INNER + CONV_CH:, :].astype(jnp.float32)
    step_size = jax.nn.softplus(step_raw + step_bias[None, :, None])
    log_decay = -jnp.exp(decay_log)[None, :, None] * step_size
    inner_x = activated[:, :INNER, :].astype(jnp.float32).reshape(ROWS, HEADS, HEAD_DIM, COLS)
    input_map = activated[:, INNER:INNER + STATE, :].astype(jnp.float32)
    output_map = activated[:, INNER + STATE:, :].astype(jnp.float32)
    scaled_x = step_size[:, :, None, :] * inner_x
    gate_vals = projected[:, :INNER, :]

    def combine(earlier, later):
        return (earlier[0] * later[0], later[0][..., None, None] * earlier[1] + later[1])

    def advance(row_state, item):
        decay_col, scaled_col, input_col, output_col, inner_col, gate_col = item
        decay_now = jnp.exp(decay_col)
        row_state = decay_now[:, :, None, None] * row_state + scaled_col[:, :, :, None] * input_col[:, None, None, :]
        _, column_state = lax.associative_scan(combine, (decay_now, row_state), axis=0)
        mixed = jnp.einsum('rhpn,rn->rhp', column_state, output_col, precision=highest)
        mixed = mixed + skip_gain[None, :, None] * inner_col
        mixed = mixed.reshape(ROWS, INNER)
        gated = mixed * jax.nn.silu(gate_col.astype(jnp.float32))
        normed = gated * lax.rsqrt(lax.optimization_barrier(jnp.mean(gated * gated, axis=1, keepdims=True)) + norm_eps) * norm_gain[None, :]
        result = jnp.dot(normed.astype(jnp.bfloat16), out_weight, preferred_element_type=jnp.float32).astype(jnp.bfloat16)
        return (row_state, result)
    start = jnp.zeros((ROWS, HEADS, HEAD_DIM, STATE), jnp.float32)
    items = (jnp.moveaxis(log_decay, 2, 0), jnp.moveaxis(scaled_x, 3, 0), jnp.moveaxis(input_map, 2, 0), jnp.moveaxis(output_map, 2, 0), jnp.moveaxis(inner_x, 3, 0), jnp.moveaxis(gate_vals, 2, 0))
    _, stacked = lax.scan(advance, start, items)
    return jnp.transpose(stacked, (1, 2, 0))
```

```python
import jax
import jax.numpy as jnp
from jax import lax
from jax.experimental import pallas as pl
from jax.experimental.pallas import tpu as pltpu
from jax.sharding import PartitionSpec as P

f32, bf16 = jnp.float32, jnp.bfloat16
norm_eps = 1e-05
ROWS, COLS, WIDTH, LANES = 16, 128, 96, 128
BLOCK, BLOCKS = 16, 8
VMEM = 56 * 1024 * 1024


def silu(v):
    return v / (1.0 + jnp.exp(-v))


def split(v):
    high = v.astype(bf16)
    return high, (v - high.astype(f32)).astype(bf16)


def dot(a, b, dims):
    return lax.dot_general(a, b, (dims, ((), ())), preferred_element_type=f32)


def lane_iota():
    return lax.broadcasted_iota(jnp.int32, (8, LANES), 1)


def fold_sublanes(parts):
    place = lax.broadcasted_iota(jnp.int32, (8, LANES), 0)
    step = 1
    while len(parts) > 1:
        first = (place & step) == 0
        parts = [
            jnp.where(first, a, b) + pltpu.roll(jnp.where(first, b, a), 8 - step, 0)
            for a, b in zip(parts[0::2], parts[1::2])
        ]
        step *= 2
    return parts[0]


def entry_kernel(
    tok, up, down, left, right, weight, taps, vec, xdt, decay, act, gate, bct, ends, proj
):
    lanes = lane_iota()

    def place_row(index, tokens):
        out = dot(tokens, weight[:, 0:384], ((0,), (0,))).astype(bf16).astype(f32)
        for g in range(3):
            proj[index, g, 8:136, :] = out[:, g * 128 : g * 128 + 128]

    place_row(0, up[0:WIDTH, :])
    place_row(ROWS + 1, down[0:WIDTH, :])

    def own_row(r, carry):
        out = dot(tok[r], weight[...], ((0,), (0,))).astype(bf16)
        for g in range(3):
            proj[r + 1, g, 8:136, :] = out[:, g * 128 : g * 128 + 128].astype(f32)
        for g in range(2):
            gate[r, g] = out[:, 640 + g * 128 : 768 + g * 128]
            raw = out[:, 384 + g * 128 : 512 + g * 128].astype(f32) + vec[g, 0:1, :]
            step = jnp.maximum(raw, 0.0) + jnp.log1p(jnp.exp(-jnp.abs(raw)))
            xdt[r, g] = step
        return carry

    lax.fori_loop(0, ROWS, own_row, 0)
    for side, at in ((left, 7), (right, 136)):
        out = dot(side[...], weight[:, 0:384], ((1,), (0,))).astype(bf16).astype(f32)
        for g in range(3):
            proj[:, g, at, :] = out[0 : ROWS + 2, g * 128 : g * 128 + 128]

    row_at = lax.broadcasted_iota(jnp.int32, (COLS, COLS), 0)
    col_at = lax.broadcasted_iota(jnp.int32, (COLS, COLS), 1)
    later = jnp.where(col_at > row_at, 1.0, 0.0).astype(bf16)
    later = jnp.concatenate([later, later], axis=1)

    def conv_row(r, carry):
        parts = []
        for g in range(3):
            acc = jnp.broadcast_to(taps[g, 9:10, :], (COLS, LANES))
            for a in range(3):
                for b in range(3):
                    k = a * 3 + b
                    acc = acc + taps[g, k : k + 1, :] * proj[r + a, g, 7 + b : 135 + b, :]
            parts.append(silu(acc).astype(bf16))
        turned = parts[2].astype(f32).T[0:32, :]
        bct[r] = turned
        b_pair = turned[0:16, :].astype(bf16)
        b_pair = jnp.concatenate([b_pair, b_pair], axis=1)
        states, totals = [], []
        for g in range(2):
            act[r, g] = parts[g]
            step = xdt[r, g]
            log_decay = vec[g, 1:2, :] * step
            scaled = step * parts[g].astype(f32)
            xdt[r, g] = scaled
            decay[r, g] = jnp.exp(log_decay)
            suffix = dot(later, jnp.concatenate(split(log_decay), axis=0), ((1,), (0,)))
            totals.append(jnp.exp(suffix[0:1, :] + log_decay[0:1, :]))
            weighted = scaled * jnp.exp(suffix)
            states.append(dot(b_pair, jnp.concatenate(split(weighted), axis=0), ((1,), (0,))))
        third = jnp.where(lanes < 64, states[1][0:8, :], states[1][8:16, :])
        rest = jnp.concatenate(totals + [jnp.zeros((2, LANES), f32)], axis=0)
        ends[2 * r] = jnp.concatenate([states[0][0:8, :], third[0:4, :], rest], axis=0)
        ends[2 * r + 1] = jnp.concatenate([states[0][8:16, :], third[4:8, :], rest], axis=0)
        return carry

    lax.fori_loop(0, ROWS, conv_row, 0)


def row_prefix_kernel(parts, out):
    count = parts.shape[0]
    first = jnp.zeros((8, LANES), f32)
    second = jnp.zeros((8, LANES), f32)
    for s in range(count):
        out[s, 0:8, :] = first
        out[s, 8:16, :] = second
        first = parts[s, 12:13, :] * first + parts[s, 0:8, :]
        second = parts[s, 13:14, :] * second + parts[s, 8:16, :]


def scan_kernel(xdt, decay, bct, carry, local, bottom):
    lanes = lane_iota()
    low = lanes < 64

    def group(rg, _):
        begin = []
        for i in range(4):
            r = rg * 4 + i
            begin.append(carry[2 * r, 0:8, :])
            begin.append(carry[2 * r + 1, 0:8, :])
            begin.append(
                jnp.concatenate([carry[2 * r, 8:12, :], carry[2 * r + 1, 8:12, :]], axis=0)
            )

        def block(cb, state):
            state = list(state)
            base = cb * BLOCK
            maps = [pltpu.roll(bct[rg * 4 + i], COLS - base, 1) for i in range(4)]
            for j in range(BLOCK):
                c = base + j
                cols = [
                    jnp.where(rg == 0, 0.0, bottom[cb, j * 24 + 8 * q : j * 24 + 8 * q + 8, :])
                    for q in range(3)
                ]
                reads = []
                for i in range(4):
                    r = rg * 4 + i
                    wide = [
                        jnp.broadcast_to(maps[i][8 * q : 8 * q + 8, j : j + 1], (8, LANES))
                        for q in range(4)
                    ]
                    b_third = jnp.where(low, wide[0], wide[1])
                    c_third = jnp.where(low, wide[2], wide[3])
                    x = [xdt[r, g, pl.ds(c, 8, stride=0), :] for g in range(2)]
                    d = [decay[r, g, pl.ds(c, 8, stride=0), :] for g in range(2)]
                    for q, (g, b) in enumerate(((0, wide[0]), (0, wide[1]), (1, b_third))):
                        state[3 * i + q] = d[g] * state[3 * i + q] + x[g] * b
                        cols[q] = d[g] * cols[q] + state[3 * i + q]
                    reads.append(wide[2] * cols[0] + wide[3] * cols[1])
                    reads.append(c_third * cols[2])
                for q in range(3):
                    bottom[cb, j * 24 + 8 * q : j * 24 + 8 * q + 8, :] = cols[q]
                local[rg, :, c, :] = fold_sublanes(reads)
            return tuple(state)

        lax.fori_loop(0, BLOCKS, block, tuple(begin))
        return 0

    lax.fori_loop(0, 4, group, 0)

    def totals(cb, _):
        base = pl.multiple_of(cb * BLOCK, BLOCK)
        for g in range(2):
            product = decay[0, g, pl.ds(base, BLOCK), :]
            for r in range(1, ROWS):
                product = product * decay[r, g, pl.ds(base, BLOCK), :]
            bottom[cb, 384 + 16 * g : 400 + 16 * g, :] = product
        return 0

    lax.fori_loop(0, BLOCKS, totals, 0)


def col_prefix_kernel(parts, out):
    def column(j, _):
        state = [jnp.zeros((8, LANES), f32) for _ in range(3)]
        base = pl.multiple_of(j * 24, 8)
        for s in range(BLOCKS):
            d = [parts[s, pl.ds(384 + 16 * g + j, 8, stride=0), :] for g in range(2)]
            for q in range(3):
                out[s, pl.ds(base + 8 * q, 8), :] = state[q]
                state[q] = d[q // 2] * state[q] + parts[s, pl.ds(base + 8 * q, 8), :]
        return 0

    lax.fori_loop(0, BLOCK, column, 0)


def exit_kernel(states, bct, local, decay, act, gate, vec, weight, out, carried):
    lanes = lane_iota()
    low = lanes < 64

    def group(rg, _):
        def block(cb, _):
            base = cb * BLOCK
            maps = [pltpu.roll(bct[rg * 4 + i, 16:32, :], COLS - base, 1) for i in range(4)]
            for j in range(BLOCK):
                cols = [states[cb, j * 24 + 8 * q : j * 24 + 8 * q + 8, :] for q in range(3)]
                reads = []
                for i in range(4):
                    wide = [
                        jnp.broadcast_to(maps[i][8 * q : 8 * q + 8, j : j + 1], (8, LANES))
                        for q in range(2)
                    ]
                    reads.append(wide[0] * cols[0] + wide[1] * cols[1])
                    reads.append(jnp.where(low, wide[0], wide[1]) * cols[2])
                carried[rg, :, base + j, :] = fold_sublanes(reads)
            return 0

        lax.fori_loop(0, BLOCKS, block, 0)
        return 0

    lax.fori_loop(0, 4, group, 0)

    reach = [jnp.ones((COLS, LANES), f32)] * 2
    for r in range(ROWS):
        gated = []
        for g in range(2):
            s = (r % 4) * 2 + g
            reach[g] = reach[g] * decay[r, g]
            mixed = local[r // 4, s] + reach[g] * carried[r // 4, s]
            if g == 1:
                mixed = mixed + pltpu.roll(mixed, 64, 1)
            mixed = mixed + vec[g, 2:3, :] * act[r, g].astype(f32)
            gated.append(mixed * silu(gate[r, g].astype(f32)))
        total = jnp.sum(gated[0] * gated[0] + gated[1] * gated[1], axis=1, keepdims=True)
        scale = lax.rsqrt(total * (1.0 / 192) + norm_eps)
        normed = [(gated[g] * scale * vec[g, 3:4, :]).astype(bf16) for g in range(2)]
        result = dot(weight[...], jnp.concatenate(normed, axis=1), ((1,), (1,)))
        out[r] = result.astype(bf16)


def call(kernel, shapes, scratch, *operands):
    return pl.pallas_call(
        kernel,
        out_shape=[jax.ShapeDtypeStruct(s, t) for s, t in shapes],
        scratch_shapes=scratch,
        compiler_params=pltpu.CompilerParams(vmem_limit_bytes=VMEM),
    )(*operands)


def steps(axis):
    count = lax.axis_size(axis)
    up = [(i, i + 1) for i in range(count - 1)]
    return up, [(j, i) for i, j in up]


def on_device(
    tokens,
    in_weight,
    conv_weight,
    conv_bias,
    step_bias,
    decay_log,
    skip_gain,
    norm_gain,
    out_weight,
):
    to_right, to_left = steps("gx")
    to_down, to_up = steps("gy")
    left = lax.ppermute(tokens[:, :, COLS - 1], "gx", to_right)
    right = lax.ppermute(tokens[:, :, 0], "gx", to_left)

    def edge(r):
        rest = jnp.stack([left[r], right[r]])
        return jnp.concatenate([tokens[r], jnp.pad(rest, ((0, 14), (0, 32)))], axis=0)

    above = lax.ppermute(edge(ROWS - 1), "gy", to_down)
    below = lax.ppermute(edge(0), "gy", to_up)

    def beside(at, own):
        rows = [above[at : at + 1, :WIDTH], own, below[at : at + 1, :WIDTH]]
        return jnp.pad(jnp.concatenate(rows, axis=0), ((0, 14), (0, 0)))

    def zeros(*shape):
        return jnp.zeros(shape, bf16)

    conv = in_weight[:, 192:416]
    wide = [
        conv[:, :192],
        conv[:, 128:192],
        conv[:, 192:],
        zeros(WIDTH, 96),
        jnp.repeat(in_weight[:, 416:], 64, axis=1),
        jnp.repeat(in_weight[:, 418:], 64, axis=1),
        in_weight[:, :192],
        zeros(WIDTH, 64),
    ]
    weight = jnp.concatenate(wide, axis=1)
    taps = jnp.concatenate([conv_weight.reshape(9, 224), conv_bias[None]], axis=0)
    taps = jnp.concatenate(
        [taps[:, :192], taps[:, 128:192], taps[:, 192:], jnp.zeros((10, 96), f32)], axis=1
    )
    taps = jnp.pad(taps.reshape(10, 3, 128).transpose(1, 0, 2), ((0, 0), (0, 6), (0, 0)))

    def by_head(v):
        return jnp.repeat(jnp.concatenate([v, v[2:]]), 64)

    vec = jnp.stack(
        [
            by_head(step_bias),
            by_head(-jnp.exp(decay_log)),
            by_head(skip_gain),
            jnp.pad(norm_gain, (0, 64)),
        ]
    )
    vec = jnp.pad(vec.reshape(4, 2, 128).transpose(1, 0, 2), ((0, 0), (0, 4), (0, 0)))
    out_turned = jnp.pad(out_weight.T, ((0, 0), (0, 64)))

    plane = (ROWS, 2, COLS, LANES)
    xdt, decay, act, gate, bct, ends = call(
        entry_kernel,
        [
            (plane, f32),
            (plane, f32),
            (plane, bf16),
            (plane, bf16),
            ((ROWS, 32, COLS), f32),
            ((2 * ROWS, 16, LANES), f32),
        ],
        [pltpu.VMEM((ROWS + 2, 3, 144, LANES), f32)],
        tokens,
        above,
        below,
        beside(96, left),
        beside(97, right),
        weight,
        taps,
        vec,
    )
    ends = lax.all_to_all(ends, "gx", 0, 0)
    (carry,) = call(row_prefix_kernel, [((2 * ROWS, 16, LANES), f32)], [], ends)
    carry = lax.all_to_all(carry, "gx", 0, 0)
    local, bottom = call(
        scan_kernel,
        [((4, 8, COLS, LANES), f32), ((BLOCKS, 416, LANES), f32)],
        [],
        xdt,
        decay,
        bct,
        carry,
    )
    bottom = lax.all_to_all(bottom, "gy", 0, 0)
    (states,) = call(col_prefix_kernel, [((BLOCKS, 384, LANES), f32)], [], bottom)
    states = lax.all_to_all(states, "gy", 0, 0)
    (out,) = call(
        exit_kernel,
        [((ROWS, WIDTH, COLS), bf16)],
        [pltpu.VMEM((4, 8, COLS, LANES), f32)],
        states,
        bct,
        local,
        decay,
        act,
        gate,
        vec,
        out_turned,
    )
    return out


def solution(mesh):
    return jax.shard_map(
        on_device,
        mesh=mesh,
        in_specs=(P("gy", None, "gx"), P(), P(), P(), P(), P(), P(), P(), P()),
        out_specs=P("gy", None, "gx"),
        check_vma=False,
    )
```

```python
import functools

import jax
import jax.numpy as jnp
from jax import lax
from jax.experimental import pallas as pl
from jax.experimental.pallas import tpu as pltpu
from jax.sharding import PartitionSpec as P

f32, bf16 = jnp.float32, jnp.bfloat16
norm_eps = 1e-05
ROWS, COLS, WIDTH, LANES = 16, 128, 96, 128
INNER, STATE, HALF = 192, 16, 64
BLOCK, BLOCKS, GROUP = 16, 8, 4
HALVED, CHIPS = BLOCKS // 2, 4
PIECE, PIECE_OUT = (BLOCK * 26, LANES), (BLOCK * 24, LANES)
PLANE = (ROWS, 2, COLS, LANES)
VMEM = 12 * 1024 * 1024


def silu(v):
    return v / (1.0 + jnp.exp(-v))


def split(v):
    high = v.astype(bf16)
    return high, (v - high.astype(f32)).astype(bf16)


def dot(a, b, dims):
    return lax.dot_general(a, b, (dims, ((), ())), preferred_element_type=f32)


def low_lanes(rows=8):
    return lax.broadcasted_iota(jnp.int32, (rows, LANES), 1) < HALF


def by_head(values, g):
    if g == 1:
        return jnp.full((1, LANES), values[2], f32)
    return jnp.where(low_lanes(1), values[0], values[1])


def fold_sublanes(parts):
    place = lax.broadcasted_iota(jnp.int32, (8, LANES), 0)
    step = 1
    while len(parts) > 1:
        first = (place & step) == 0
        parts = [
            jnp.where(first, a, b) + pltpu.roll(jnp.where(first, b, a), 8 - step, 0)
            for a, b in zip(parts[0::2], parts[1::2])
        ]
        step *= 2
    return parts[0]


def each_row(body, together):
    def some(k, carry):
        for i in range(together):
            body(k * together + i)
        return carry

    lax.fori_loop(0, ROWS // together, some, 0)


def spread(values, q, j):
    return jnp.broadcast_to(values[8 * q : 8 * q + 8, j : j + 1], (8, LANES))


def entry_kernel(
    tok,
    above,
    below,
    left,
    right,
    in_weight,
    conv_weight,
    conv_bias,
    step_bias,
    decay_log,
    xdt,
    decay,
    act,
    gate,
    bct,
    cmap,
    ends,
    proj,
    weight,
    taps,
    compact,
    totals,
):
    source = in_weight[...].astype(f32)
    chan_b, chan_c = source[:, 384:400], source[:, 400:416]
    step_w = [jnp.broadcast_to(source[:, 416 + h : 417 + h], (WIDTH, HALF)) for h in range(3)]
    wide = [
        source[:, 192:384],
        chan_c,
        chan_c,
        chan_b,
        jnp.zeros((WIDTH, 16), f32),
        step_w[0],
        step_w[1],
        step_w[2],
        step_w[2],
        source[:, 0:192],
        jnp.zeros((WIDTH, HALF), f32),
    ]
    weight[...] = jnp.concatenate(wide, axis=1).astype(bf16)
    step_turned = jnp.concatenate([source[:, 416:419], jnp.zeros((WIDTH, 125), f32)], axis=1)
    step_turned = step_turned.T[0:8, :].astype(bf16)
    for ref, at, size in ((conv_weight, 0, 9), (conv_bias, 9, 1)):
        v = ref[...]
        taps[0, at : at + size, :] = v[:, 0:128]
        tail = [v[:, 128:192], v[:, 208:224], v[:, 208:224], v[:, 192:208]]
        taps[1, at : at + size, :] = jnp.concatenate(tail + [jnp.zeros((size, 16), f32)], axis=1)

    def conv_part(tokens, dims):
        return dot(tokens, weight[:, 0:256], dims).astype(bf16).astype(f32)

    def softplus(v):
        return jnp.maximum(v, 0.0) + jnp.log1p(jnp.exp(-jnp.abs(v)))

    for at, ref in ((0, above), (ROWS + 1, below)):
        out = conv_part(ref[0:WIDTH, :], ((0,), (0,)))
        sides = conv_part(ref[WIDTH:, 0:WIDTH], ((1,), (0,)))
        for g in range(2):
            proj[at, g, 8:136, :] = out[:, g * 128 : g * 128 + 128]
            proj[at, g, 7:8, :] = sides[0:1, g * 128 : g * 128 + 128]
            proj[at, g, 136:137, :] = sides[1:2, g * 128 : g * 128 + 128]
    for ref, at in ((left, 7), (right, 136)):
        out = conv_part(ref[...], ((1,), (0,)))
        for g in range(2):
            proj[1 : ROWS + 1, g, at, :] = out[:, g * 128 : g * 128 + 128]

    def own_row(r):
        out = dot(tok[r], weight[...], ((0,), (0,))).astype(bf16)
        compact[r] = dot(step_turned, tok[r], ((1,), (0,))).astype(bf16).astype(f32)
        for g in range(2):
            proj[r + 1, g, 8:136, :] = out[:, g * 128 : g * 128 + 128].astype(f32)
            gate[r, g] = out[:, 512 + g * 128 : 640 + g * 128]
            raw = out[:, 256 + g * 128 : 384 + g * 128].astype(f32) + by_head(step_bias, g)
            xdt[r, g] = softplus(raw)

    each_row(own_row, 4)

    head = lax.broadcasted_iota(jnp.int32, (8, LANES), 0)

    def head_rows(ref):
        return jnp.where(head == 0, ref[0], jnp.where(head == 1, ref[1], ref[2]))

    step = softplus(compact[...] + head_rows(step_bias))
    log_decay = (-jnp.exp(head_rows(decay_log)) * step).reshape(ROWS * 8, LANES)
    log_decay = jnp.concatenate(split(log_decay), axis=1)
    from_at = lax.broadcasted_iota(jnp.int32, (2 * COLS, COLS), 0) & (COLS - 1)
    to_at = lax.broadcasted_iota(jnp.int32, (2 * COLS, COLS), 1)
    later = jnp.where(from_at > to_at, 1.0, 0.0).astype(bf16)
    suffix = dot(log_decay, later, ((1,), (0,)))
    whole = dot(log_decay, jnp.ones((2 * COLS, COLS), bf16), ((1,), (0,)))
    compact[...] = step * jnp.exp(suffix).reshape(ROWS, 8, LANES)
    totals[...] = jnp.exp(whole).reshape(ROWS, 8, LANES)
    rate = [-jnp.exp(by_head(decay_log, g)) for g in range(2)]

    def conv_row(r):
        parts = []
        for g in range(2):
            acc = jnp.broadcast_to(taps[g, 9:10, :], (COLS, LANES))
            for a in range(3):
                for b in range(3):
                    k = a * 3 + b
                    acc = acc + taps[g, k : k + 1, :] * proj[r + a, g, 7 + b : 135 + b, :]
            parts.append(silu(acc).astype(bf16).astype(f32))
        turned = parts[1].T
        chan_b = turned[96:112, :]
        bct[r, 0:16, :] = chan_b
        bct[r, 16:32, :] = turned[64:80, :]
        other = pltpu.roll(parts[1], HALF, 1)
        cmap[:, r, :] = other
        parts[1] = jnp.where(low_lanes(COLS), parts[1], other)
        for g in range(2):
            act[r, g] = parts[g].astype(bf16)
            step = xdt[r, g]
            xdt[r, g] = step * parts[g]
            decay[r, g] = jnp.exp(rate[g] * step)
        weighted = [compact[r, h : h + 1, :] * chan_b for h in range(3)]
        weighted = jnp.concatenate(split(jnp.concatenate(weighted, axis=0)), axis=0)
        inner = jnp.concatenate([act[r, 0], act[r, 1]], axis=1)
        state = dot(weighted, inner, ((1,), (0,)))
        state = state[0:48, :] + state[48:96, :]
        low = low_lanes(16)
        first = jnp.where(low, state[0:16, 0:128], state[16:32, 0:128])
        third = jnp.where(low_lanes(), state[32:40, 128:256], state[40:48, 128:256])
        total = jnp.where(low_lanes(1), totals[r, 0:1, :], totals[r, 1:2, :])
        rest = jnp.concatenate([total, totals[r, 2:3, :], jnp.zeros((2, LANES), f32)], axis=0)
        ends[2 * r] = jnp.concatenate([first[0:8, :], third[0:4, :], rest], axis=0)
        ends[2 * r + 1] = jnp.concatenate([first[8:16, :], third[4:8, :], rest], axis=0)

    each_row(conv_row, 2)


def row_prefix_kernel(parts, out):
    count = parts.shape[0]
    first = jnp.zeros((8, LANES), f32)
    second = jnp.zeros((8, LANES), f32)
    for s in range(count):
        out[s, 0:8, :] = first
        out[s, 8:16, :] = second
        first = parts[s, 12:13, :] * first + parts[s, 0:8, :]
        second = parts[s, 13:14, :] * second + parts[s, 8:16, :]


def starts(carry, r):
    third = jnp.concatenate([carry[2 * r, 8:12, :], carry[2 * r + 1, 8:12, :]], axis=0)
    return [carry[2 * r, 0:8, :], carry[2 * r + 1, 0:8, :], third]


def bottom_kernel(xdt, decay, bct, carry, mine, theirs, hold):
    core = lax.axis_index("gy") % 2
    low = low_lanes()
    begin = []
    for r in range(ROWS):
        begin += starts(carry, r)

    def block(cb, state):
        state = list(state)
        base = pl.multiple_of(cb * BLOCK, BLOCK)
        maps = [pltpu.roll(bct[r, 0:16, :], COLS - base, 1) for r in range(ROWS)]
        for j in range(BLOCK):
            cols = [jnp.zeros((8, LANES), f32)] * 3
            for r in range(ROWS):
                wide = [spread(maps[r], q, j) for q in range(2)]
                wide.append(jnp.where(low, wide[0], wide[1]))
                x = [xdt[r, g, pl.ds(base + j, 8, stride=0), :] for g in range(2)]
                d = [decay[r, g, pl.ds(base + j, 8, stride=0), :] for g in range(2)]
                for q in range(3):
                    g = q // 2
                    state[3 * r + q] = d[g] * state[3 * r + q] + x[g] * wide[q]
                    cols[q] = d[g] * cols[q] + state[3 * r + q]
            for q in range(3):
                hold[j * 24 + 8 * q : j * 24 + 8 * q + 8, :] = cols[q]
        for g in range(2):
            product = decay[0, g, pl.ds(base, BLOCK), :]
            for r in range(1, ROWS):
                product = product * decay[r, g, pl.ds(base, BLOCK), :]
            hold[384 + 16 * g : 400 + 16 * g, :] = product

        @pl.when(cb // HALVED == core)
        def _():
            mine[cb % HALVED] = hold[...]

        @pl.when(cb // HALVED != core)
        def _():
            theirs[cb % HALVED] = hold[...]

        return tuple(state)

    lax.fori_loop(0, BLOCKS, block, tuple(begin))


def local_kernel(begins, xdt, decay, bct, carry, act, gate, skip_gain, *refs):
    if begins:
        track_in, gated_out, reach_out, track, local = refs
        track[...] = track_in[...]
    else:
        gated_out, reach_out, track, local = refs
        track[...] = jnp.zeros_like(track)
    low = low_lanes()

    def group(at, _):
        rg = begins // GROUP + at
        begin = []
        for i in range(GROUP):
            begin += starts(carry, rg * GROUP + i)

        def block(cb, state):
            state = list(state)
            base = cb * BLOCK
            maps = [pltpu.roll(bct[rg * GROUP + i], COLS - base, 1) for i in range(GROUP)]
            for j in range(BLOCK):
                cols = [track[cb, j * 24 + 8 * q : j * 24 + 8 * q + 8, :] for q in range(3)]
                reads = []
                for i in range(GROUP):
                    r = rg * GROUP + i
                    wide = [spread(maps[i], q, j) for q in range(4)]
                    b_all = [wide[0], wide[1], jnp.where(low, wide[0], wide[1])]
                    x = [xdt[r, g, pl.ds(base + j, 8, stride=0), :] for g in range(2)]
                    d = [decay[r, g, pl.ds(base + j, 8, stride=0), :] for g in range(2)]
                    for q in range(3):
                        g = q // 2
                        state[3 * i + q] = d[g] * state[3 * i + q] + x[g] * b_all[q]
                        cols[q] = d[g] * cols[q] + state[3 * i + q]
                    reads.append(wide[2] * cols[0] + wide[3] * cols[1])
                    reads.append(jnp.where(low, wide[2], wide[3]) * cols[2])
                for q in range(3):
                    track[cb, j * 24 + 8 * q : j * 24 + 8 * q + 8, :] = cols[q]
                local[at, :, base + j, :] = fold_sublanes(reads)
            return tuple(state)

        lax.fori_loop(0, BLOCKS, block, tuple(begin))
        return 0

    lax.fori_loop(0, ROWS // 2 // GROUP, group, 0)
    reach = [jnp.ones((COLS, LANES), f32)] * 2
    for r in range(begins):
        for g in range(2):
            reach[g] = reach[g] * decay[r, g]
    for i in range(ROWS // 2):
        r = begins + i
        for g in range(2):
            reach[g] = reach[g] * decay[r, g]
            mixed = local[i // GROUP, (i % GROUP) * 2 + g]
            if g == 1:
                mixed = mixed + pltpu.roll(mixed, HALF, 1)
            mixed = mixed + by_head(skip_gain, g) * act[r, g].astype(f32)
            gating = silu(gate[r, g].astype(f32))
            gated_out[i, g] = mixed * gating
            reach_out[i, g] = reach[g] * gating


def place():
    gy = lax.axis_index("gy")
    return gy % 2, gy // 2


def rows_of(j, q):
    return pl.ds(pl.multiple_of(j * 24 + 8 * q, 8), 8)


def decay_of(j, q):
    return pl.ds(BLOCK * (24 + q // 2) + j, 8, stride=0)


def join_kernel(mine, theirs, *outs):
    core, chip = place()
    for k, out in enumerate(outs):
        piece = (chip + k) % CHIPS

        def column(j, _):
            for q in range(3):
                a, b = mine[piece, rows_of(j, q), :], theirs[piece, rows_of(j, q), :]
                da, db = mine[piece, decay_of(j, q), :], theirs[piece, decay_of(j, q), :]
                out[rows_of(j, q), :] = jnp.where(core == 0, db * a + b, da * b + a)
            return 0

        lax.fori_loop(0, BLOCK, column, 0, unroll=4)
        rest = pl.ds(BLOCK * 24, BLOCK * 2)
        out[rest, :] = mine[piece, rest, :] * theirs[piece, rest, :]


def col_prefix_kernel(*refs):
    parts, outs, held, ready = refs[:CHIPS], refs[CHIPS : 2 * CHIPS], refs[-2], refs[-1]
    _, chip = place()
    for k, part in enumerate(parts):
        held[(chip + CHIPS - k) % CHIPS] = part[...]

    def column(j, _):
        for q in range(3):
            state = jnp.zeros((8, LANES), f32)
            for s in range(CHIPS):
                ready[s, rows_of(j, q), :] = state
                state = held[s, decay_of(j, q), :] * state + held[s, rows_of(j, q), :]
        return 0

    lax.fori_loop(0, BLOCK, column, 0, unroll=4)
    for k, out in enumerate(outs):
        out[...] = ready[(chip + k) % CHIPS]


def share_kernel(*refs):
    parts, (mine, theirs, own, other) = refs[:CHIPS], refs[CHIPS:]
    core, chip = place()
    for k, part in enumerate(parts):
        piece = (chip + CHIPS - k) % CHIPS

        def column(j, _):
            for q in range(3):
                upper = part[rows_of(j, q), :]
                a, b = mine[piece, rows_of(j, q), :], theirs[piece, rows_of(j, q), :]
                da, db = mine[piece, decay_of(j, q), :], theirs[piece, decay_of(j, q), :]
                lower = jnp.where(core == 0, da * upper + a, db * upper + b)
                own[piece, rows_of(j, q), :] = jnp.where(core == 0, upper, lower)
                other[piece, rows_of(j, q), :] = jnp.where(core == 0, lower, upper)
            return 0

        lax.fori_loop(0, BLOCK, column, 0, unroll=4)


def exit_kernel(
    own, other, cmap, gated_a, reach_a, gated_b, reach_b, norm_gain, out_weight, out, carried
):
    low = low_lanes()
    core, _ = place()

    def block(k, _, states, half):
        for j in range(BLOCK):
            first, second, third = [
                states[k, j * 24 + 8 * q : j * 24 + 8 * q + 8, :] for q in range(3)
            ]
            turned = pltpu.roll(third, HALF, 1)
            right = [jnp.where(low, third, turned), jnp.where(low, turned, third)]
            whole = jnp.concatenate(
                [
                    jnp.concatenate([first, second], axis=0),
                    jnp.concatenate(right, axis=0),
                ],
                axis=1,
            )
            c = ((core ^ half) * HALVED + k) * BLOCK + j
            reads = cmap[c][:, 0:32].astype(bf16)
            result = dot(reads, jnp.concatenate(split(whole), axis=0), ((1,), (0,)))
            for g in range(2):
                carried[:, g, c, :] = result[:, g * 128 : g * 128 + 128]
        return 0

    for half, states in enumerate((own, other)):
        lax.fori_loop(0, HALVED, functools.partial(block, states=states, half=half), 0)
    turned = out_weight[...].astype(f32).T
    weight = jnp.concatenate([turned, jnp.zeros((WIDTH, HALF), f32)], axis=1).astype(bf16)
    pad = jnp.zeros((1, HALF), f32)
    gain = [norm_gain[:, 0:128], jnp.concatenate([norm_gain[:, 128:192], pad], axis=1)]

    def row(r, begins, gated, reach):
        i = r - begins
        parts = [gated[i, g] + reach[i, g] * carried[r, g] for g in range(2)]
        total = jnp.sum(parts[0] * parts[0] + parts[1] * parts[1], axis=1, keepdims=True)
        scale = lax.rsqrt(total * (1.0 / INNER) + norm_eps)
        normed = [(parts[g] * scale * gain[g]).astype(bf16) for g in range(2)]
        result = dot(weight, jnp.concatenate(normed, axis=1), ((1,), (1,)))
        out[r] = result.astype(bf16)

    for begins, gated, reach in ((0, gated_a, reach_a), (ROWS // 2, gated_b, reach_b)):

        def some(k, carry):
            for i in range(4):
                row(begins + 4 * k + i, begins, gated, reach)
            return carry

        lax.fori_loop(0, ROWS // 8, some, 0)


def call(kernel, spaces, shapes, scratch, *operands, after=()):
    kinds = {"v": pltpu.VMEM, "s": pltpu.SMEM, "h": pl.ANY}
    first, waits = len(operands), len(after)
    spaces, operands = spaces + "h" * waits, operands + tuple(after)

    def inner(*refs):
        kernel(*refs[:first], *refs[first + waits :])

    return pl.pallas_call(
        inner,
        in_specs=[pl.BlockSpec(memory_space=kinds[k]) for k in spaces],
        out_specs=[pl.BlockSpec(memory_space=kinds[k]) for _, _, k in shapes],
        out_shape=[jax.ShapeDtypeStruct(s, t) for s, t, _ in shapes],
        scratch_shapes=scratch,
        compiler_params=pltpu.CompilerParams(vmem_limit_bytes=VMEM),
    )(*operands)


def steps(axis):
    count = lax.axis_size(axis)
    up = [(i, i + 1) for i in range(count - 1)]
    return up, [(j, i) for i, j in up]


def on_device(
    tokens,
    in_weight,
    conv_weight,
    conv_bias,
    step_bias,
    decay_log,
    skip_gain,
    norm_gain,
    out_weight,
):
    to_right, to_left = steps("gx")
    to_down, to_up = steps("gy")
    left = lax.ppermute(tokens[:, :, COLS - 1], "gx", to_right)
    right = lax.ppermute(tokens[:, :, 0], "gx", to_left)

    def edge(r):
        rest = jnp.pad(jnp.stack([left[r], right[r]]), ((0, 14), (0, LANES - WIDTH)))
        return jnp.concatenate([tokens[r], rest], axis=0)

    above = lax.ppermute(edge(ROWS - 1), "gy", to_down)
    below = lax.ppermute(edge(0), "gy", to_up)
    vmem = pltpu.VMEM
    xdt, decay, act, gate, bct, cmap, ends = call(
        entry_kernel,
        "vvvvvvvvss",
        [
            (PLANE, f32, "v"),
            (PLANE, f32, "v"),
            (PLANE, bf16, "v"),
            (PLANE, bf16, "v"),
            ((ROWS, 32, COLS), f32, "v"),
            ((COLS, ROWS, LANES), f32, "v"),
            ((2 * ROWS, 16, LANES), f32, "v"),
        ],
        [
            vmem((ROWS + 2, 2, 144, LANES), f32),
            vmem((WIDTH, 768), bf16),
            vmem((2, 16, LANES), f32),
            vmem((ROWS, 8, LANES), f32),
            vmem((ROWS, 8, LANES), f32),
        ],
        tokens,
        above,
        below,
        left,
        right,
        in_weight,
        conv_weight.reshape(9, 224),
        conv_bias.reshape(1, 224),
        step_bias,
        decay_log,
    )
    ends = lax.all_to_all(ends, "gx", 0, 0)
    (carry,) = call(row_prefix_kernel, "v", [((2 * ROWS, 16, LANES), f32, "v")], [], ends)
    carry = lax.all_to_all(carry, "gx", 0, 0)
    piece, piece_out = (PIECE, f32, "v"), (PIECE_OUT, f32, "v")
    halves = ((HALVED,) + PIECE, f32, "v")
    mine, theirs = call(
        bottom_kernel, "vvvv", [halves] * 2, [vmem(PIECE, f32)], xdt, decay, bct, carry
    )
    gy_count = lax.axis_size("gy")
    swap = [(i, i ^ 1) for i in range(gy_count)]
    ahead = [[(i, (i + 2 * k) % gy_count) for i in range(gy_count)] for k in range(CHIPS)]

    def rotate(pieces):
        return [pieces[0]] + [lax.ppermute(pieces[k], "gy", ahead[k]) for k in range(1, CHIPS)]

    theirs = lax.ppermute(theirs, "gy", swap)
    joined = call(join_kernel, "vv", [piece] * CHIPS, [], mine, theirs)
    pieces = rotate(joined)
    half = (ROWS // 2,) + PLANE[1:]
    local_scratch = vmem((ROWS // 2 // GROUP, 8, COLS, LANES), f32)
    inner = (xdt, decay, bct, carry, act, gate, skip_gain)
    gated_a, reach_a, track = call(
        functools.partial(local_kernel, 0),
        "vvvvvvs",
        [(half, f32, "v"), (half, f32, "v"), ((BLOCKS,) + PIECE_OUT, f32, "v")],
        [local_scratch],
        *inner,
        after=joined[:1],
    )
    pieces = call(
        col_prefix_kernel,
        "vvvv",
        [piece_out] * CHIPS,
        [vmem((CHIPS,) + PIECE, f32), vmem((CHIPS,) + PIECE_OUT, f32)],
        *pieces,
        after=(track,),
    )
    above_chip = pieces[0]
    pieces = rotate(pieces)
    gated_b, reach_b = call(
        functools.partial(local_kernel, ROWS // 2),
        "vvvvvvsv",
        [(half, f32, "v"), (half, f32, "v")],
        [vmem((BLOCKS,) + PIECE_OUT, f32), local_scratch],
        *inner,
        track,
        after=(above_chip,),
    )
    halves_out = ((HALVED,) + PIECE_OUT, f32, "v")
    own, other = call(
        share_kernel, "vvvvvv", [halves_out] * 2, [], *pieces, mine, theirs, after=(gated_b,)
    )
    other = lax.ppermute(other, "gy", swap)
    (out,) = call(
        exit_kernel,
        "vvvvvvvvv",
        [((ROWS, WIDTH, COLS), bf16, "v")],
        [vmem(PLANE, f32)],
        own,
        other,
        cmap,
        gated_a,
        reach_a,
        gated_b,
        reach_b,
        norm_gain.reshape(1, INNER),
        out_weight,
    )
    return out


def solution(mesh):
    return jax.shard_map(
        on_device,
        mesh=mesh,
        in_specs=(P("gy", None, "gx"), P(), P(), P(), P(), P(), P(), P(), P()),
        out_specs=P("gy", None, "gx"),
        check_vma=False,
    )
```

```python
import functools

import jax
import jax.numpy as jnp
from jax import lax
from jax.experimental import pallas as pl
from jax.experimental.pallas import tpu as pltpu
from jax.sharding import PartitionSpec as P

f32, bf16 = jnp.float32, jnp.bfloat16
norm_eps = 1e-05
ROWS, COLS, WIDTH, LANES = 16, 128, 96, 128
INNER, STATE, HALF = 192, 16, 64
BLOCK, BLOCKS = 16, 8
HALVED, CHIPS = BLOCKS // 2, 4
PIECE, PIECE_OUT = (BLOCK * 26, LANES), (BLOCK * 24, LANES)
PLANE = (ROWS, 2, COLS, LANES)
VMEM = 12 * 1024 * 1024


def silu(v):
    return v / (1.0 + jnp.exp(-v))


def split(v):
    high = v.astype(bf16)
    return high, (v - high.astype(f32)).astype(bf16)


def dot(a, b, dims):
    return lax.dot_general(a, b, (dims, ((), ())), preferred_element_type=f32)


def low_lanes(rows=8):
    return lax.broadcasted_iota(jnp.int32, (rows, LANES), 1) < HALF


def by_head(values, g):
    if g == 1:
        return jnp.full((1, LANES), values[2], f32)
    return jnp.where(low_lanes(1), values[0], values[1])


def fold_sublanes(parts):
    place = lax.broadcasted_iota(jnp.int32, (8, LANES), 0)
    step = 1
    while len(parts) > 1:
        first = (place & step) == 0
        parts = [
            jnp.where(first, a, b) + pltpu.roll(jnp.where(first, b, a), 8 - step, 0)
            for a, b in zip(parts[0::2], parts[1::2])
        ]
        step *= 2
    return parts[0]


def each_row(body, together):
    def some(k, carry):
        for i in range(together):
            body(k * together + i)
        return carry

    lax.fori_loop(0, ROWS // together, some, 0)


def spread(values, q, j):
    return jnp.broadcast_to(values[8 * q : 8 * q + 8, j : j + 1], (8, LANES))


def softplus(v):
    return jnp.maximum(v, 0.0) + jnp.log1p(jnp.exp(-jnp.abs(v)))


def project_kernel(
    tok, in_weight, step_bias, decay_log, inner, gate, steps, compact, totals, conv_w, weight
):
    source = in_weight[...].astype(f32)
    chan_b, chan_c = source[:, 384:400], source[:, 400:416]
    step_w = [jnp.broadcast_to(source[:, 416 + h : 417 + h], (WIDTH, HALF)) for h in range(3)]
    wide = [
        source[:, 192:384],
        chan_c,
        chan_c,
        chan_b,
        jnp.zeros((WIDTH, 16), f32),
        step_w[0],
        step_w[1],
        step_w[2],
        step_w[2],
        source[:, 0:192],
        jnp.zeros((WIDTH, HALF), f32),
    ]
    weight[...] = jnp.concatenate(wide, axis=1).astype(bf16)
    conv_w[...] = weight[:, 0:256]
    step_turned = jnp.concatenate([source[:, 416:419], jnp.zeros((WIDTH, 125), f32)], axis=1)
    step_turned = step_turned.T[0:8, :].astype(bf16)

    def own_row(r):
        out = dot(tok[r], weight[...], ((0,), (0,))).astype(bf16)
        compact[r] = dot(step_turned, tok[r], ((1,), (0,))).astype(bf16).astype(f32)
        for g in range(2):
            inner[r, g] = out[:, g * 128 : g * 128 + 128]
            gate[r, g] = out[:, 512 + g * 128 : 640 + g * 128]
            raw = out[:, 256 + g * 128 : 384 + g * 128].astype(f32) + by_head(step_bias, g)
            steps[r, g] = softplus(raw)

    each_row(own_row, 4)

    head = lax.broadcasted_iota(jnp.int32, (8, LANES), 0)

    def head_rows(ref):
        return jnp.where(head == 0, ref[0], jnp.where(head == 1, ref[1], ref[2]))

    step = softplus(compact[...] + head_rows(step_bias))
    log_decay = (-jnp.exp(head_rows(decay_log)) * step).reshape(ROWS * 8, LANES)
    log_decay = jnp.concatenate(split(log_decay), axis=1)
    from_at = lax.broadcasted_iota(jnp.int32, (2 * COLS, COLS), 0) & (COLS - 1)
    to_at = lax.broadcasted_iota(jnp.int32, (2 * COLS, COLS), 1)
    later = jnp.where(from_at > to_at, 1.0, 0.0).astype(bf16)
    suffix = dot(log_decay, later, ((1,), (0,)))
    whole = dot(log_decay, jnp.ones((2 * COLS, COLS), bf16), ((1,), (0,)))
    compact[...] = step * jnp.exp(suffix).reshape(ROWS, 8, LANES)
    totals[...] = jnp.exp(whole).reshape(ROWS, 8, LANES)


def entry_kernel(
    inner,
    above,
    below,
    left,
    right,
    steps,
    compact,
    totals,
    conv_w,
    conv_weight,
    conv_bias,
    decay_log,
    xdt,
    decay,
    act,
    bct,
    cmap,
    *refs,
):
    ends_out, (proj, taps, ends) = refs[:CHIPS], refs[CHIPS:]
    for ref, at, size in ((conv_weight, 0, 9), (conv_bias, 9, 1)):
        v = ref[...]
        taps[0, at : at + size, :] = v[:, 0:128]
        tail = [v[:, 128:192], v[:, 208:224], v[:, 208:224], v[:, 192:208]]
        taps[1, at : at + size, :] = jnp.concatenate(tail + [jnp.zeros((size, 16), f32)], axis=1)

    def conv_part(tokens, dims):
        return dot(tokens, conv_w[...], dims).astype(bf16).astype(f32)

    for at, ref in ((0, above), (ROWS + 1, below)):
        out = conv_part(ref[...], ((0,), (0,)))
        for g in range(2):
            proj[at, g, 8:136, :] = out[:, g * 128 : g * 128 + 128]
    for ref, at in ((left, 7), (right, 136)):
        out = conv_part(ref[...], ((1,), (0,)))
        for g in range(2):
            proj[:, g, at, :] = out[0 : ROWS + 2, g * 128 : g * 128 + 128]

    def own_row(r):
        for g in range(2):
            proj[r + 1, g, 8:136, :] = inner[r, g].astype(f32)

    each_row(own_row, 4)
    rate = [-jnp.exp(by_head(decay_log, g)) for g in range(2)]

    def conv_row(r):
        parts = []
        for g in range(2):
            acc = jnp.broadcast_to(taps[g, 9:10, :], (COLS, LANES))
            for a in range(3):
                for b in range(3):
                    k = a * 3 + b
                    acc = acc + taps[g, k : k + 1, :] * proj[r + a, g, 7 + b : 135 + b, :]
            parts.append(silu(acc).astype(bf16).astype(f32))
        turned = parts[1].T
        chan_b = turned[96:112, :]
        bct[r, 0:16, :] = chan_b
        bct[r, 16:32, :] = turned[64:80, :]
        other = pltpu.roll(parts[1], HALF, 1)
        cmap[:, r, :] = other
        parts[1] = jnp.where(low_lanes(COLS), parts[1], other)
        for g in range(2):
            act[r, g] = parts[g].astype(bf16)
            step = steps[r, g]
            xdt[r, g] = step * parts[g]
            decay[r, g] = jnp.exp(rate[g] * step)
        weighted = [compact[r, h : h + 1, :] * chan_b for h in range(3)]
        weighted = jnp.concatenate(split(jnp.concatenate(weighted, axis=0)), axis=0)
        inner_x = jnp.concatenate([act[r, 0], act[r, 1]], axis=1)
        state = dot(weighted, inner_x, ((1,), (0,)))
        state = state[0:48, :] + state[48:96, :]
        first = jnp.where(low_lanes(16), state[0:16, 0:128], state[16:32, 0:128])
        third = jnp.where(low_lanes(), state[32:40, 128:256], state[40:48, 128:256])
        total = jnp.where(low_lanes(1), totals[r, 0:1, :], totals[r, 1:2, :])
        rest = jnp.concatenate([total, totals[r, 2:3, :], jnp.zeros((2, LANES), f32)], axis=0)
        quarter, at = r // 4, (r % 4) * 2
        ends[quarter, at] = jnp.concatenate([first[0:8, :], third[0:4, :], rest], axis=0)
        ends[quarter, at + 1] = jnp.concatenate([first[8:16, :], third[4:8, :], rest], axis=0)

    each_row(conv_row, 2)
    member, _ = line()
    for k, out in enumerate(ends_out):
        out[...] = ends[(member + k) % CHIPS]


def line():
    gx = lax.axis_index("gx")
    return gx % 4, gx // 4


def part_of(ref, i, at=None):
    box = ref if at is None else ref.at[at]
    return (box[i, 0:8, :], box[i, 8:16, :]), (box[i, 12:13, :], box[i, 13:14, :])


def put(ref, i, tiles, decays=None):
    ref[i, 0:8, :] = tiles[0]
    ref[i, 8:16, :] = tiles[1]
    if decays is not None:
        ref[i, 12:13, :] = decays[0]
        ref[i, 13:14, :] = decays[1]


def chain(tiles, step):
    return [d * a + b for a, b, d in zip(tiles, *step)]


def product(a, b):
    return [u * v for u, v in zip(a, b)]


def members_kernel(*refs):
    parts, (out, held) = refs[:CHIPS], refs[CHIPS:]
    member, _ = line()
    for k, part in enumerate(parts):
        held[(member + CHIPS - k) % CHIPS] = part[...]
    for i in range(8):
        tiles, decays = part_of(held, i, 0)
        for m in range(1, CHIPS):
            step = part_of(held, i, m)
            tiles, decays = chain(tiles, step), product(decays, step[1])
        put(out, i, tiles, decays)


def pair_kernel(mine, theirs, out):
    _, z = line()
    odd = z % 2 == 1
    for i in range(8):
        a, b = part_of(mine, i), part_of(theirs, i)
        after, before = chain(b[0], a), chain(a[0], b)
        tiles = [jnp.where(odd, u, v) for u, v in zip(after, before)]
        put(out, i, tiles, product(a[1], b[1]))


def carry_kernel(near, mid, far, theirs, *refs):
    parts, outs, held = refs[:CHIPS], refs[CHIPS : 2 * CHIPS], refs[-1]
    member, z = line()
    odd = z % 2 == 1
    for k, part in enumerate(parts):
        held[(member + CHIPS - k) % CHIPS] = part[...]
    for i in range(8):
        tiles = part_of(far, i)[0]
        for part in (mid, near):
            tiles = chain(tiles, part_of(part, i))
        tiles = [jnp.where(odd, u, v) for u, v in zip(chain(tiles, part_of(theirs, i)), tiles)]
        for m in range(CHIPS):
            step = part_of(held, i, m)
            put(held.at[m], i, tiles)
            tiles = chain(tiles, step)
    for k, out in enumerate(outs):
        out[...] = held[(member + k) % CHIPS]


def starts(carry, r):
    third = jnp.concatenate([carry[2 * r, 8:12, :], carry[2 * r + 1, 8:12, :]], axis=0)
    return [carry[2 * r, 0:8, :], carry[2 * r + 1, 0:8, :], third]


def bottom_kernel(xdt, decay, bct, *refs):
    parts, (mine, theirs, carry, hold) = refs[:CHIPS], refs[CHIPS:]
    core = lax.axis_index("gy") % 2
    member, _ = line()
    for k, part in enumerate(parts):
        carry[pl.ds((member + CHIPS - k) % CHIPS * 8, 8)] = part[...]
    low = low_lanes()
    begin = []
    for r in range(ROWS):
        begin += starts(carry, r)

    def block(cb, state):
        state = list(state)
        base = pl.multiple_of(cb * BLOCK, BLOCK)
        maps = [pltpu.roll(bct[r, 0:16, :], COLS - base, 1) for r in range(ROWS)]
        for j in range(BLOCK):
            cols = [jnp.zeros((8, LANES), f32)] * 3
            for r in range(ROWS):
                wide = [spread(maps[r], q, j) for q in range(2)]
                wide.append(jnp.where(low, wide[0], wide[1]))
                x = [xdt[r, g, pl.ds(base + j, 8, stride=0), :] for g in range(2)]
                d = [decay[r, g, pl.ds(base + j, 8, stride=0), :] for g in range(2)]
                for q in range(3):
                    g = q // 2
                    state[3 * r + q] = d[g] * state[3 * r + q] + x[g] * wide[q]
                    cols[q] = d[g] * cols[q] + state[3 * r + q]
            for q in range(3):
                hold[j * 24 + 8 * q : j * 24 + 8 * q + 8, :] = cols[q]
        for g in range(2):
            product = decay[0, g, pl.ds(base, BLOCK), :]
            for r in range(1, ROWS):
                product = product * decay[r, g, pl.ds(base, BLOCK), :]
            hold[384 + 16 * g : 400 + 16 * g, :] = product

        @pl.when(cb // HALVED == core)
        def _():
            mine[cb % HALVED] = hold[...]

        @pl.when(cb // HALVED != core)
        def _():
            theirs[cb % HALVED] = hold[...]

        return tuple(state)

    lax.fori_loop(0, BLOCKS, block, tuple(begin))


def gating_kernel(decay, gate, gating, reach):
    along = [jnp.ones((COLS, LANES), f32)] * 2

    def some(k, along):
        along = list(along)
        for i in range(4):
            r = k * 4 + i
            for g in range(2):
                along[g] = along[g] * decay[r, g]
                gated = silu(gate[r, g].astype(f32))
                gating[r, g] = gated
                reach[r, g] = along[g] * gated
        return tuple(along)

    lax.fori_loop(0, ROWS // 4, some, tuple(along))


def local_kernel(begins, xdt, decay, bct, carry, act, gating, skip_gain, *refs):
    if begins:
        track_in, gated, local = refs
    else:
        gated, track, local = refs
    low = low_lanes()
    count = ROWS // 2
    begin = []
    for i in range(count):
        begin += starts(carry, begins + i)

    def block(cb, state):
        state = list(state)
        base = cb * BLOCK
        maps = [pltpu.roll(bct[begins + i], COLS - base, 1) for i in range(count)]
        for j in range(BLOCK):
            if begins:
                cols = [track_in[cb, j * 24 + 8 * q : j * 24 + 8 * q + 8, :] for q in range(3)]
            else:
                cols = [jnp.zeros((8, LANES), f32)] * 3
            reads = []
            for i in range(count):
                r = begins + i
                wide = [spread(maps[i], q, j) for q in range(4)]
                b_all = [wide[0], wide[1], jnp.where(low, wide[0], wide[1])]
                x = [xdt[r, g, pl.ds(base + j, 8, stride=0), :] for g in range(2)]
                d = [decay[r, g, pl.ds(base + j, 8, stride=0), :] for g in range(2)]
                for q in range(3):
                    g = q // 2
                    state[3 * i + q] = d[g] * state[3 * i + q] + x[g] * b_all[q]
                    cols[q] = d[g] * cols[q] + state[3 * i + q]
                reads.append(wide[2] * cols[0] + wide[3] * cols[1])
                reads.append(jnp.where(low, wide[2], wide[3]) * cols[2])
            if not begins:
                for q in range(3):
                    track[cb, j * 24 + 8 * q : j * 24 + 8 * q + 8, :] = cols[q]
            for k in range(2):
                local[k, :, base + j, :] = fold_sublanes(reads[8 * k : 8 * k + 8])
        return tuple(state)

    lax.fori_loop(0, BLOCKS, block, tuple(begin))
    for i in range(count):
        r = begins + i
        for g in range(2):
            mixed = local[i // 4, (i % 4) * 2 + g]
            if g == 1:
                mixed = mixed + pltpu.roll(mixed, HALF, 1)
            mixed = mixed + by_head(skip_gain, g) * act[r, g].astype(f32)
            gated[i, g] = mixed * gating[r, g]


def place():
    gy = lax.axis_index("gy")
    return gy % 2, gy // 2


def rows_of(j, q):
    return pl.ds(pl.multiple_of(j * 24 + 8 * q, 8), 8)


def decay_of(j, q):
    return pl.ds(BLOCK * (24 + q // 2) + j, 8, stride=0)


def join_kernel(mine, theirs, *outs):
    core, chip = place()
    for k, out in enumerate(outs):
        piece = (chip + k) % CHIPS

        def column(j, _):
            for q in range(3):
                a, b = mine[piece, rows_of(j, q), :], theirs[piece, rows_of(j, q), :]
                da, db = mine[piece, decay_of(j, q), :], theirs[piece, decay_of(j, q), :]
                out[rows_of(j, q), :] = jnp.where(core == 0, db * a + b, da * b + a)
            return 0

        lax.fori_loop(0, BLOCK, column, 0, unroll=4)
        rest = pl.ds(BLOCK * 24, BLOCK * 2)
        out[rest, :] = mine[piece, rest, :] * theirs[piece, rest, :]


def col_prefix_kernel(*refs):
    parts, outs, held, ready = refs[:CHIPS], refs[CHIPS : 2 * CHIPS], refs[-2], refs[-1]
    _, chip = place()
    for k, part in enumerate(parts):
        held[(chip + CHIPS - k) % CHIPS] = part[...]

    def column(j, _):
        for q in range(3):
            state = jnp.zeros((8, LANES), f32)
            for s in range(CHIPS):
                ready[s, rows_of(j, q), :] = state
                state = held[s, decay_of(j, q), :] * state + held[s, rows_of(j, q), :]
        return 0

    lax.fori_loop(0, BLOCK, column, 0, unroll=4)
    for k, out in enumerate(outs):
        out[...] = ready[(chip + k) % CHIPS]


def share_kernel(*refs):
    parts, (mine, theirs, own, other) = refs[:CHIPS], refs[CHIPS:]
    core, chip = place()
    for k, part in enumerate(parts):
        piece = (chip + CHIPS - k) % CHIPS

        def column(j, _):
            for q in range(3):
                upper = part[rows_of(j, q), :]
                a, b = mine[piece, rows_of(j, q), :], theirs[piece, rows_of(j, q), :]
                da, db = mine[piece, decay_of(j, q), :], theirs[piece, decay_of(j, q), :]
                lower = jnp.where(core == 0, da * upper + a, db * upper + b)
                own[piece, rows_of(j, q), :] = jnp.where(core == 0, upper, lower)
                other[piece, rows_of(j, q), :] = jnp.where(core == 0, lower, upper)
            return 0

        lax.fori_loop(0, BLOCK, column, 0, unroll=4)


def reads_kernel(states, cmap, carried, *, half):
    low = low_lanes()
    core, _ = place()

    def block(k, _):
        for j in range(BLOCK):
            first, second, third = [
                states[k, j * 24 + 8 * q : j * 24 + 8 * q + 8, :] for q in range(3)
            ]
            turned = pltpu.roll(third, HALF, 1)
            right = [jnp.where(low, third, turned), jnp.where(low, turned, third)]
            whole = jnp.concatenate(
                [
                    jnp.concatenate([first, second], axis=0),
                    jnp.concatenate(right, axis=0),
                ],
                axis=1,
            )
            at = k * BLOCK + j
            reads = cmap[(core ^ half) * HALF + at][:, 0:32].astype(bf16)
            result = dot(reads, jnp.concatenate(split(whole), axis=0), ((1,), (0,)))
            for g in range(2):
                carried[:, g, at, :] = result[:, g * 128 : g * 128 + 128]
        return 0

    lax.fori_loop(0, HALVED, block, 0)


def exit_kernel(
    own, other, cmap, gated_a, gated_b, reach, norm_gain, out_weight, out, carried
):
    core, _ = place()
    reads_kernel(other, cmap, carried, half=1)
    turned = out_weight[...].astype(f32).T
    weight = jnp.concatenate([turned, jnp.zeros((WIDTH, HALF), f32)], axis=1).astype(bf16)
    pad = jnp.zeros((1, HALF), f32)
    gain = [norm_gain[:, 0:128], jnp.concatenate([norm_gain[:, 128:192], pad], axis=1)]

    def row(r, begins, gated):
        i = r - begins
        parts = []
        for g in range(2):
            a, b = own[r, g], carried[r, g]
            both = [jnp.where(core == 0, a, b), jnp.where(core == 0, b, a)]
            parts.append(gated[i, g] + reach[r, g] * jnp.concatenate(both, axis=0))
        total = jnp.sum(parts[0] * parts[0] + parts[1] * parts[1], axis=1, keepdims=True)
        scale = lax.rsqrt(total * (1.0 / INNER) + norm_eps)
        normed = [(parts[g] * scale * gain[g]).astype(bf16) for g in range(2)]
        result = dot(weight, jnp.concatenate(normed, axis=1), ((1,), (1,)))
        out[r] = result.astype(bf16)

    for begins, gated in ((0, gated_a), (ROWS // 2, gated_b)):

        def some(k, carry):
            for i in range(4):
                row(begins + 4 * k + i, begins, gated)
            return carry

        lax.fori_loop(0, ROWS // 8, some, 0)


def call(kernel, spaces, shapes, scratch, *operands, after=()):
    kinds = {"v": pltpu.VMEM, "s": pltpu.SMEM, "h": pl.ANY}
    first, waits = len(operands), len(after)
    spaces, operands = spaces + "h" * waits, operands + tuple(after)

    def inner(*refs):
        kernel(*refs[:first], *refs[first + waits :])

    return pl.pallas_call(
        inner,
        in_specs=[pl.BlockSpec(memory_space=kinds[k]) for k in spaces],
        out_specs=[pl.BlockSpec(memory_space=kinds[k]) for _, _, k in shapes],
        out_shape=[jax.ShapeDtypeStruct(s, t) for s, t, _ in shapes],
        scratch_shapes=scratch,
        compiler_params=pltpu.CompilerParams(vmem_limit_bytes=VMEM),
    )(*operands)


def steps(axis):
    count = lax.axis_size(axis)
    up = [(i, i + 1) for i in range(count - 1)]
    return up, [(j, i) for i, j in up]


def on_device(
    tokens,
    in_weight,
    conv_weight,
    conv_bias,
    step_bias,
    decay_log,
    skip_gain,
    norm_gain,
    out_weight,
):
    to_right, to_left = steps("gx")
    to_down, to_up = steps("gy")
    above = lax.ppermute(tokens[ROWS - 1], "gy", to_down)
    below = lax.ppermute(tokens[0], "gy", to_up)

    def edge(c):
        column = [above[None, :, c], tokens[:, :, c], below[None, :, c]]
        return jnp.concatenate(column, axis=0)

    last, first = edge(COLS - 1), edge(0)
    left = lax.ppermute(last, "gx", to_right)
    right = lax.ppermute(first, "gx", to_left)
    vmem = pltpu.VMEM
    rows8 = ((ROWS, 8, LANES), f32, "v")
    inner, gate, step, compact, totals, conv_w = call(
        project_kernel,
        "vvss",
        [(PLANE, bf16, "v"), (PLANE, bf16, "v"), (PLANE, f32, "v"), rows8, rows8]
        + [((WIDTH, 256), bf16, "v")],
        [vmem((WIDTH, 768), bf16)],
        tokens,
        in_weight,
        step_bias,
        decay_log,
        after=(last,),
    )
    packet = ((8, 16, LANES), f32, "v")
    quarters = vmem((CHIPS,) + packet[0], f32)
    xdt, decay, act, bct, cmap, *ends = call(
        entry_kernel,
        "vvvvvvvvvvvs",
        [
            (PLANE, f32, "v"),
            (PLANE, f32, "v"),
            (PLANE, bf16, "v"),
            ((ROWS, 32, COLS), f32, "v"),
            ((COLS, ROWS, LANES), f32, "v"),
        ]
        + [packet] * CHIPS,
        [vmem((ROWS + 2, 2, 144, LANES), f32), vmem((2, 16, LANES), f32), quarters],
        inner,
        above,
        below,
        left,
        right,
        step,
        compact,
        totals,
        conv_w,
        conv_weight.reshape(9, 224),
        conv_bias.reshape(1, 224),
        decay_log,
    )
    gx_count = lax.axis_size("gx")

    def members(pieces):
        moved = [pieces[0]] * CHIPS
        for k in (2, 1, 3):
            pairs = [(i, i // 4 * 4 + (i + k) % 4) for i in range(gx_count)]
            moved[k] = lax.ppermute(pieces[k], "gx", pairs)
        return moved

    gating, reach = call(
        gating_kernel, "vv", [(PLANE, f32, "v")] * 2, [], decay, gate, after=ends[:1]
    )
    ends = members(ends)
    (whole,) = call(members_kernel, "vvvv", [packet], [quarters], *ends, after=(reach,))
    beside = lax.ppermute(whole, "gx", [(i, i ^ 4) for i in range(gx_count)])
    (both,) = call(pair_kernel, "vv", [packet], [], whole, beside)
    mid, near, far = [
        lax.ppermute(both, "gx", [(i, i + 8 * k) for i in range(gx_count - 8 * k)])
        for k in (2, 1, 3)
    ]
    carries = call(
        carry_kernel, "v" * 8, [packet] * CHIPS, [quarters], near, mid, far, beside, *ends
    )
    carries = members(carries)
    piece, piece_out = (PIECE, f32, "v"), (PIECE_OUT, f32, "v")
    halves = ((HALVED,) + PIECE, f32, "v")
    mine, theirs, carry = call(
        bottom_kernel,
        "v" * 7,
        [halves, halves, ((2 * ROWS, 16, LANES), f32, "v")],
        [vmem(PIECE, f32)],
        xdt,
        decay,
        bct,
        *carries,
    )
    gy_count = lax.axis_size("gy")
    swap = [(i, i ^ 1) for i in range(gy_count)]
    ahead = [[(i, (i + 2 * k) % gy_count) for i in range(gy_count)] for k in range(CHIPS)]

    def rotate(pieces):
        moved = [pieces[0]] * CHIPS
        for k in (2, 1, 3):
            moved[k] = lax.ppermute(pieces[k], "gy", ahead[k])
        return moved

    theirs = lax.ppermute(theirs, "gy", swap)
    joined = call(join_kernel, "vv", [piece] * CHIPS, [], mine, theirs)
    pieces = rotate(joined)
    half = ((ROWS // 2,) + PLANE[1:], f32, "v")
    local_scratch = vmem((2, 8, COLS, LANES), f32)
    inner = (xdt, decay, bct, carry, act, gating, skip_gain)
    gated_a, track = call(
        functools.partial(local_kernel, 0),
        "vvvvvvs",
        [half, ((BLOCKS,) + PIECE_OUT, f32, "v")],
        [local_scratch],
        *inner,
        after=joined[:1],
    )
    pieces = call(
        col_prefix_kernel,
        "vvvv",
        [piece_out] * CHIPS,
        [vmem((CHIPS,) + PIECE, f32), vmem((CHIPS,) + PIECE_OUT, f32)],
        *pieces,
        after=(track,),
    )
    above_chip = pieces[0]
    pieces = rotate(pieces)
    (gated_b,) = call(
        functools.partial(local_kernel, ROWS // 2),
        "vvvvvvsv",
        [half],
        [local_scratch],
        *inner,
        track,
        after=(above_chip,),
    )
    halves_out = ((HALVED,) + PIECE_OUT, f32, "v")
    own, other = call(
        share_kernel, "vvvvvv", [halves_out] * 2, [], *pieces, mine, theirs, after=(gated_b,)
    )
    sent = other
    other = lax.ppermute(sent, "gy", swap)
    half_plane = (ROWS, 2, HALF, LANES)
    (own,) = call(
        functools.partial(reads_kernel, half=0),
        "vv",
        [(half_plane, f32, "v")],
        [],
        own,
        cmap,
        after=(sent,),
    )
    (out,) = call(
        exit_kernel,
        "vvvvvvvv",
        [((ROWS, WIDTH, COLS), bf16, "v")],
        [vmem(half_plane, f32)],
        own,
        other,
        cmap,
        gated_a,
        gated_b,
        reach,
        norm_gain.reshape(1, INNER),
        out_weight,
    )
    return out


def solution(mesh):
    return jax.shard_map(
        on_device,
        mesh=mesh,
        in_specs=(P("gy", None, "gx"), P(), P(), P(), P(), P(), P(), P(), P()),
        out_specs=P("gy", None, "gx"),
        check_vma=False,
    )
```

```python
import functools

import jax
import jax.numpy as jnp
from jax import lax
from jax.experimental import pallas as pl
from jax.experimental.pallas import tpu as pltpu
from jax.sharding import PartitionSpec as P

f32, bf16 = jnp.float32, jnp.bfloat16
norm_eps = 1e-05
ROWS, COLS, WIDTH, LANES = 16, 128, 96, 128
INNER, STATE, HALF = 192, 16, 64
BLOCK, BLOCKS = 16, 8
HALVED, CHIPS = BLOCKS // 2, 4
PIECE, PIECE_OUT = (BLOCK * 26, LANES), (BLOCK * 24, LANES)
PLANE = (ROWS, 2, COLS, LANES)
VMEM = 12 * 1024 * 1024


def silu(v):
    return v / (1.0 + jnp.exp(-v))


def split(v):
    high = v.astype(bf16)
    return high, (v - high.astype(f32)).astype(bf16)


def dot(a, b, dims):
    return lax.dot_general(a, b, (dims, ((), ())), preferred_element_type=f32)


def low_lanes(rows=8):
    return lax.broadcasted_iota(jnp.int32, (rows, LANES), 1) < HALF


def by_head(values, g):
    if g == 1:
        return jnp.full((1, LANES), values[2], f32)
    return jnp.where(low_lanes(1), values[0], values[1])


def fold_sublanes(parts):
    place = lax.broadcasted_iota(jnp.int32, (8, LANES), 0)
    step = 1
    while len(parts) > 1:
        first = (place & step) == 0
        parts = [
            jnp.where(first, a, b) + pltpu.roll(jnp.where(first, b, a), 8 - step, 0)
            for a, b in zip(parts[0::2], parts[1::2])
        ]
        step *= 2
    return parts[0]


def each_row(body, together):
    def some(k, carry):
        for i in range(together):
            body(k * together + i)
        return carry

    lax.fori_loop(0, ROWS // together, some, 0)


def spread(values, q, j):
    return jnp.broadcast_to(values[8 * q : 8 * q + 8, j : j + 1], (8, LANES))


def softplus(v):
    return jnp.maximum(v, 0.0) + jnp.log1p(jnp.exp(-jnp.abs(v)))


def project_kernel(
    tok,
    in_weight,
    conv_weight,
    conv_bias,
    step_bias,
    decay_log,
    inner,
    gate,
    steps,
    compact,
    totals,
    conv_w,
    taps,
    weight,
):
    load_taps(conv_weight, conv_bias, taps)
    source = in_weight[...].astype(f32)
    chan_b, chan_c = source[:, 384:400], source[:, 400:416]
    step_w = [jnp.broadcast_to(source[:, 416 + h : 417 + h], (WIDTH, HALF)) for h in range(3)]
    wide = [
        source[:, 192:384],
        chan_c,
        chan_c,
        chan_b,
        jnp.zeros((WIDTH, 16), f32),
        step_w[0],
        step_w[1],
        step_w[2],
        step_w[2],
        source[:, 0:192],
        jnp.zeros((WIDTH, HALF), f32),
    ]
    weight[...] = jnp.concatenate(wide, axis=1).astype(bf16)
    conv_w[...] = weight[:, 0:256]
    step_turned = jnp.concatenate([source[:, 416:419], jnp.zeros((WIDTH, 125), f32)], axis=1)
    step_turned = step_turned.T[0:8, :].astype(bf16)

    def own_row(r):
        out = dot(tok[r], weight[...], ((0,), (0,))).astype(bf16)
        compact[r] = dot(step_turned, tok[r], ((1,), (0,))).astype(bf16).astype(f32)
        for g in range(2):
            inner[r, g] = out[:, g * 128 : g * 128 + 128]
            gate[r, g] = out[:, 512 + g * 128 : 640 + g * 128]
            raw = out[:, 256 + g * 128 : 384 + g * 128].astype(f32) + by_head(step_bias, g)
            steps[r, g] = softplus(raw)

    each_row(own_row, 4)

    head = lax.broadcasted_iota(jnp.int32, (8, LANES), 0)

    def head_rows(ref):
        return jnp.where(head == 0, ref[0], jnp.where(head == 1, ref[1], ref[2]))

    step = softplus(compact[...] + head_rows(step_bias))
    log_decay = (-jnp.exp(head_rows(decay_log)) * step).reshape(ROWS * 8, LANES)
    log_decay = jnp.concatenate(split(log_decay), axis=1)
    from_at = lax.broadcasted_iota(jnp.int32, (2 * COLS, COLS), 0) & (COLS - 1)
    to_at = lax.broadcasted_iota(jnp.int32, (2 * COLS, COLS), 1)
    later = jnp.where(from_at > to_at, 1.0, 0.0).astype(bf16)
    suffix = dot(log_decay, later, ((1,), (0,)))
    whole = dot(log_decay, jnp.ones((2 * COLS, COLS), bf16), ((1,), (0,)))
    compact[...] = step * jnp.exp(suffix).reshape(ROWS, 8, LANES)
    totals[...] = jnp.exp(whole).reshape(ROWS, 8, LANES)


def pack_kernel(tok, left, right, *outs):
    for out, r in zip(outs, (ROWS - 1, 0)):
        sides = [left[r : r + 1, :].astype(f32), right[r : r + 1, :].astype(f32)]
        sides = jnp.concatenate(sides + [jnp.zeros((14, WIDTH), f32)], axis=0)
        sides = jnp.concatenate([sides, jnp.zeros((16, LANES - WIDTH), f32)], axis=1)
        out[0:WIDTH, :] = tok[r]
        out[WIDTH:, :] = sides.astype(bf16)


def load_taps(conv_weight, conv_bias, taps):
    for k in range(10):
        v = conv_bias[...] if k == 9 else conv_weight[k // 3, k % 3 : k % 3 + 1, :]
        taps[0, k : k + 1, :] = v[:, 0:128]
        tail = [v[:, 128:192], v[:, 208:224], v[:, 208:224], v[:, 192:208]]
        taps[1, k : k + 1, :] = jnp.concatenate(tail + [jnp.zeros((1, 16), f32)], axis=1)


def conv_part(tokens, conv_w, dims):
    return dot(tokens, conv_w[...], dims).astype(bf16).astype(f32)


def put_sides(left, right, conv_w, proj, begins, first, count):
    for ref, at in ((left, 7), (right, 136)):
        out = conv_part(ref[...], conv_w, ((1,), (0,)))
        for g in range(2):
            proj[first : first + count, g, at, :] = out[
                begins : begins + count, g * 128 : g * 128 + 128
            ]


def conv_row(proj, taps, at):
    parts = []
    for g in range(2):
        acc = jnp.broadcast_to(taps[g, 9:10, :], (COLS, LANES))
        for a in range(3):
            for b in range(3):
                k = a * 3 + b
                acc = acc + taps[g, k : k + 1, :] * proj[at + a, g, 7 + b : 135 + b, :]
        parts.append(silu(acc).astype(bf16).astype(f32))
    return parts


def finish_row(parts, steps, compact, totals, xdt, act, bct, ends):
    turned = parts[1].T
    chan_b = turned[96:112, :]
    bct[0:16, :] = chan_b
    bct[16:32, :] = turned[64:80, :]
    other = pltpu.roll(parts[1], HALF, 1)
    whole = [parts[0], jnp.where(low_lanes(COLS), parts[1], other)]
    for g in range(2):
        act[g] = whole[g].astype(bf16)
        xdt[g] = steps[g] * whole[g]
    weighted = [compact[h : h + 1, :] * chan_b for h in range(3)]
    weighted = jnp.concatenate(split(jnp.concatenate(weighted, axis=0)), axis=0)
    inner_x = jnp.concatenate(whole, axis=1).astype(bf16)
    state = dot(weighted, inner_x, ((1,), (0,)))
    state = state[0:48, :] + state[48:96, :]
    first = jnp.where(low_lanes(16), state[0:16, 0:128], state[16:32, 0:128])
    third = jnp.where(low_lanes(), state[32:40, 128:256], state[40:48, 128:256])
    total = jnp.where(low_lanes(1), totals[0:1, :], totals[1:2, :])
    rest = jnp.concatenate([total, totals[2:3, :], jnp.zeros((2, LANES), f32)], axis=0)
    ends[0] = jnp.concatenate([first[0:8, :], third[0:4, :], rest], axis=0)
    ends[1] = jnp.concatenate([first[8:16, :], third[4:8, :], rest], axis=0)
    return other


def inside_kernel(
    inner,
    left,
    right,
    steps,
    compact,
    totals,
    conv_w,
    taps,
    decay_log,
    xdt,
    decay,
    act,
    bct,
    cmap,
    ends,
    proj,
):
    put_sides(left, right, conv_w, proj, 0, 0, ROWS)
    rate = [-jnp.exp(by_head(decay_log, g)) for g in range(2)]

    def own_row(r):
        for g in range(2):
            proj[r, g, 8:136, :] = inner[r, g].astype(f32)
            decay[r, g] = jnp.exp(rate[g] * steps[r, g])

    each_row(own_row, 4)

    def some(k, carry):
        for i in range(2):
            r = 1 + 2 * k + i
            parts = conv_row(proj, taps, r - 1)
            refs = [ref.at[r] for ref in (steps, compact, totals, xdt, act, bct)]
            cmap[:, r, :] = finish_row(parts, *refs, ends.at[pl.ds(2 * r, 2)])
        return carry

    lax.fori_loop(0, ROWS // 2 - 1, some, 0)


def edge_kernel(
    inner,
    above,
    below,
    left,
    right,
    steps,
    compact,
    totals,
    conv_w,
    taps,
    cmap_in,
    ends,
    xdt,
    act,
    bct,
    cmap,
    *refs,
):
    ends_out, (proj, held) = refs[:CHIPS], refs[CHIPS:]
    put_sides(left, right, conv_w, proj, 0, 1, 2)
    put_sides(left, right, conv_w, proj, ROWS - 2, 3, 2)
    for at, ref in ((0, above), (5, below)):
        out = conv_part(ref[0:WIDTH, :], conv_w, ((0,), (0,)))
        sides = conv_part(ref[WIDTH:, 0:WIDTH], conv_w, ((1,), (0,)))
        for g in range(2):
            proj[at, g, 8:136, :] = out[:, g * 128 : g * 128 + 128]
            proj[at, g, 7:8, :] = sides[0:1, g * 128 : g * 128 + 128]
            proj[at, g, 136:137, :] = sides[1:2, g * 128 : g * 128 + 128]
    for at, r in ((1, 0), (2, 1), (3, ROWS - 2), (4, ROWS - 1)):
        for g in range(2):
            proj[at, g, 8:136, :] = inner[r, g].astype(f32)
    held[...] = ends[...]
    cmap[...] = cmap_in[...]
    for e, r in enumerate((0, ROWS - 1)):
        parts = conv_row(proj, taps, 3 * e)
        own = [ref.at[r] for ref in (steps, compact, totals)]
        mine = [ref.at[e] for ref in (xdt, act, bct)]
        cmap[:, r, :] = finish_row(parts, *own, *mine, held.at[pl.ds(2 * r, 2)])
    member, _ = line()
    for k, out in enumerate(ends_out):
        out[...] = held[pl.ds((member + k) % CHIPS * 8, 8)]


def row_of(pair, r):
    inside, edge = pair
    if r in (0, ROWS - 1):
        return edge.at[0 if r == 0 else 1]
    return inside.at[r]


def line():
    gx = lax.axis_index("gx")
    return gx % 4, gx // 4


def part_of(ref, i, at=None):
    box = ref if at is None else ref.at[at]
    return (box[i, 0:8, :], box[i, 8:16, :]), (box[i, 12:13, :], box[i, 13:14, :])


def put(ref, i, tiles, decays=None):
    ref[i, 0:8, :] = tiles[0]
    ref[i, 8:16, :] = tiles[1]
    if decays is not None:
        ref[i, 12:13, :] = decays[0]
        ref[i, 13:14, :] = decays[1]


def chain(tiles, step):
    return [d * a + b for a, b, d in zip(tiles, *step)]


def product(a, b):
    return [u * v for u, v in zip(a, b)]


def members_kernel(*refs):
    parts, (out, held) = refs[:CHIPS], refs[CHIPS:]
    member, _ = line()
    for k, part in enumerate(parts):
        held[(member + CHIPS - k) % CHIPS] = part[...]
    for i in range(8):
        tiles, decays = part_of(held, i, 0)
        for m in range(1, CHIPS):
            step = part_of(held, i, m)
            tiles, decays = chain(tiles, step), product(decays, step[1])
        put(out, i, tiles, decays)


def pair_kernel(mine, theirs, out):
    _, z = line()
    odd = z % 2 == 1
    for i in range(8):
        a, b = part_of(mine, i), part_of(theirs, i)
        after, before = chain(b[0], a), chain(a[0], b)
        tiles = [jnp.where(odd, u, v) for u, v in zip(after, before)]
        put(out, i, tiles, product(a[1], b[1]))


def carry_kernel(near, mid, far, theirs, *refs):
    parts, outs, held = refs[:CHIPS], refs[CHIPS : 2 * CHIPS], refs[-1]
    member, z = line()
    odd = z % 2 == 1
    for k, part in enumerate(parts):
        held[(member + CHIPS - k) % CHIPS] = part[...]
    for i in range(8):
        tiles = part_of(far, i)[0]
        for part in (mid, near):
            tiles = chain(tiles, part_of(part, i))
        tiles = [jnp.where(odd, u, v) for u, v in zip(chain(tiles, part_of(theirs, i)), tiles)]
        for m in range(CHIPS):
            step = part_of(held, i, m)
            put(held.at[m], i, tiles)
            tiles = chain(tiles, step)
    for k, out in enumerate(outs):
        out[...] = held[(member + k) % CHIPS]


def starts(carry, r):
    third = jnp.concatenate([carry[2 * r, 8:12, :], carry[2 * r + 1, 8:12, :]], axis=0)
    return [carry[2 * r, 0:8, :], carry[2 * r + 1, 0:8, :], third]


def bottom_kernel(xdt_in, xdt_edge, decay, bct_in, bct_edge, *refs, half):
    if half:
        state_in, bottom = refs
        begin = [state_in[i] for i in range(3 * ROWS)]
    else:
        bottom, state_out = refs
        begin = [jnp.zeros((8, LANES), f32)] * (3 * ROWS)
    low = low_lanes()
    xdt = [row_of((xdt_in, xdt_edge), r) for r in range(ROWS)]
    bct = [row_of((bct_in, bct_edge), r) for r in range(ROWS)]

    def block(k, state):
        state = list(state)
        base = pl.multiple_of((half * HALVED + k) * BLOCK, BLOCK)
        maps = [pltpu.roll(bct[r][0:16, :], COLS - base, 1) for r in range(ROWS)]
        for j in range(BLOCK):
            cols = [jnp.zeros((8, LANES), f32)] * 3
            for r in range(ROWS):
                wide = [spread(maps[r], q, j) for q in range(2)]
                wide.append(jnp.where(low, wide[0], wide[1]))
                x = [xdt[r][g, pl.ds(base + j, 8, stride=0), :] for g in range(2)]
                d = [decay[r, g, pl.ds(base + j, 8, stride=0), :] for g in range(2)]
                for q in range(3):
                    g = q // 2
                    state[3 * r + q] = d[g] * state[3 * r + q] + x[g] * wide[q]
                    cols[q] = d[g] * cols[q] + state[3 * r + q]
            for q in range(3):
                bottom[k, j * 24 + 8 * q : j * 24 + 8 * q + 8, :] = cols[q]
        for g in range(2):
            whole = decay[0, g, pl.ds(base, BLOCK), :]
            for r in range(1, ROWS):
                whole = whole * decay[r, g, pl.ds(base, BLOCK), :]
            bottom[k, 384 + 16 * g : 400 + 16 * g, :] = whole
        return tuple(state)

    state = lax.fori_loop(0, HALVED, block, tuple(begin))
    if not half:
        for i in range(3 * ROWS):
            state_out[i] = state[i]


def weight_kernel(steps, decay, decay_log, coef):
    row_at = lax.broadcasted_iota(jnp.int32, (COLS, 2 * COLS), 0)
    col_at = lax.broadcasted_iota(jnp.int32, (COLS, 2 * COLS), 1) & (COLS - 1)
    upto = jnp.where(col_at <= row_at, 1.0, 0.0).astype(bf16)
    rate = [-jnp.exp(by_head(decay_log, g)) for g in range(2)]
    rate = jnp.concatenate(rate, axis=1)

    def some(k, below):
        below = list(below)
        for i in range(4):
            r = ROWS - 1 - (k * 4 + i)
            along = rate * jnp.concatenate([steps[r, 0], steps[r, 1]], axis=1)
            along = dot(upto, jnp.concatenate(split(along), axis=0), ((1,), (0,)))
            along = jnp.exp(along)
            for g in range(2):
                coef[r, g] = along[:, g * 128 : g * 128 + 128] * below[g]
                below[g] = below[g] * decay[r, g]
        return tuple(below)

    lax.fori_loop(0, ROWS // 4, some, (jnp.ones((COLS, LANES), f32),) * 2)


def add_kernel(coef, left_half, right_half, *refs):
    parts, (mine, theirs, carry, hold) = refs[:CHIPS], refs[CHIPS:]
    core, _ = place()
    member, _ = line()
    for k, part in enumerate(parts):
        carry[pl.ds((member + CHIPS - k) % CHIPS * 8, 8)] = part[...]
    for r in range(ROWS):
        hold[3 * r], hold[3 * r + 1], hold[3 * r + 2] = starts(carry, r)

    def block(k, _, source, out, base):
        for at in range(0, BLOCK, 4):
            sums = [
                source[k, 24 * j + 8 * q : 24 * j + 8 * q + 8, :]
                for j in range(at, at + 4)
                for q in range(3)
            ]
            for r in range(ROWS):
                tiles = [hold[3 * r + q] for q in range(3)]
                for j in range(4):
                    c = base + k * BLOCK + at + j
                    w = [coef[r, g, pl.ds(c, 8, stride=0), :] for g in range(2)]
                    for q in range(3):
                        sums[3 * j + q] = sums[3 * j + q] + w[q // 2] * tiles[q]
            for j in range(4):
                for q in range(3):
                    row = 24 * (at + j) + 8 * q
                    out[k, row : row + 8, :] = sums[3 * j + q]
        out[k, 384:416, :] = source[k, 384:416, :]
        return 0

    def both(outs):
        for half, source in enumerate((left_half, right_half)):
            run = functools.partial(block, source=source, out=outs[half], base=half * HALF)
            lax.fori_loop(0, HALVED, run, 0)

    @pl.when(core == 0)
    def _():
        both((mine, theirs))

    @pl.when(core != 0)
    def _():
        both((theirs, mine))


def gating_kernel(decay, gate, gating, reach):
    along = [jnp.ones((COLS, LANES), f32)] * 2

    def some(k, along):
        along = list(along)
        for i in range(4):
            r = k * 4 + i
            for g in range(2):
                along[g] = along[g] * decay[r, g]
                gated = silu(gate[r, g].astype(f32))
                gating[r, g] = gated
                reach[r, g] = along[g] * gated
        return tuple(along)

    lax.fori_loop(0, ROWS // 4, some, tuple(along))


def local_kernel(
    begins,
    xdt_in,
    xdt_edge,
    decay,
    bct_in,
    bct_edge,
    carry,
    act_in,
    act_edge,
    gating,
    skip_gain,
    *refs,
):
    if begins:
        track_in, gated, local = refs
    else:
        gated, track, local = refs
    low = low_lanes()
    xdt = [row_of((xdt_in, xdt_edge), r) for r in range(ROWS)]
    bct = [row_of((bct_in, bct_edge), r) for r in range(ROWS)]
    act = [row_of((act_in, act_edge), r) for r in range(ROWS)]
    count = ROWS // 2
    begin = []
    for i in range(count):
        begin += starts(carry, begins + i)

    def block(cb, state):
        state = list(state)
        base = cb * BLOCK
        maps = [pltpu.roll(bct[begins + i][...], COLS - base, 1) for i in range(count)]
        for j in range(BLOCK):
            if begins:
                cols = [track_in[cb, j * 24 + 8 * q : j * 24 + 8 * q + 8, :] for q in range(3)]
            else:
                cols = [jnp.zeros((8, LANES), f32)] * 3
            reads = []
            for i in range(count):
                r = begins + i
                wide = [spread(maps[i], q, j) for q in range(4)]
                b_all = [wide[0], wide[1], jnp.where(low, wide[0], wide[1])]
                x = [xdt[r][g, pl.ds(base + j, 8, stride=0), :] for g in range(2)]
                d = [decay[r, g, pl.ds(base + j, 8, stride=0), :] for g in range(2)]
                for q in range(3):
                    g = q // 2
                    state[3 * i + q] = d[g] * state[3 * i + q] + x[g] * b_all[q]
                    cols[q] = d[g] * cols[q] + state[3 * i + q]
                reads.append(wide[2] * cols[0] + wide[3] * cols[1])
                reads.append(jnp.where(low, wide[2], wide[3]) * cols[2])
            if not begins:
                for q in range(3):
                    track[cb, j * 24 + 8 * q : j * 24 + 8 * q + 8, :] = cols[q]
            for k in range(2):
                local[k, :, base + j, :] = fold_sublanes(reads[8 * k : 8 * k + 8])
        return tuple(state)

    lax.fori_loop(0, BLOCKS, block, tuple(begin))
    for i in range(count):
        r = begins + i
        for g in range(2):
            mixed = local[i // 4, (i % 4) * 2 + g]
            if g == 1:
                mixed = mixed + pltpu.roll(mixed, HALF, 1)
            mixed = mixed + by_head(skip_gain, g) * act[r][g].astype(f32)
            gated[i, g] = mixed * gating[r, g]


def place():
    gy = lax.axis_index("gy")
    return gy % 2, gy // 2


def rows_of(j, q):
    return pl.ds(pl.multiple_of(j * 24 + 8 * q, 8), 8)


def decay_of(j, q):
    return pl.ds(BLOCK * (24 + q // 2) + j, 8, stride=0)


def join_kernel(mine, theirs, *outs):
    core, chip = place()
    for k, out in enumerate(outs):
        piece = (chip + k) % CHIPS

        def column(j, _):
            for q in range(3):
                a, b = mine[piece, rows_of(j, q), :], theirs[piece, rows_of(j, q), :]
                da, db = mine[piece, decay_of(j, q), :], theirs[piece, decay_of(j, q), :]
                out[rows_of(j, q), :] = jnp.where(core == 0, db * a + b, da * b + a)
            return 0

        lax.fori_loop(0, BLOCK, column, 0, unroll=4)
        rest = pl.ds(BLOCK * 24, BLOCK * 2)
        out[rest, :] = mine[piece, rest, :] * theirs[piece, rest, :]


def col_prefix_kernel(*refs):
    parts, outs, held, ready = refs[:CHIPS], refs[CHIPS : 2 * CHIPS], refs[-2], refs[-1]
    _, chip = place()
    for k, part in enumerate(parts):
        held[(chip + CHIPS - k) % CHIPS] = part[...]

    def column(j, _):
        for q in range(3):
            state = jnp.zeros((8, LANES), f32)
            for s in range(CHIPS):
                ready[s, rows_of(j, q), :] = state
                state = held[s, decay_of(j, q), :] * state + held[s, rows_of(j, q), :]
        return 0

    lax.fori_loop(0, BLOCK, column, 0, unroll=4)
    for k, out in enumerate(outs):
        out[...] = ready[(chip + k) % CHIPS]


def share_kernel(*refs):
    parts, (mine, theirs, own, other) = refs[:CHIPS], refs[CHIPS:]
    core, chip = place()
    for k, part in enumerate(parts):
        piece = (chip + CHIPS - k) % CHIPS

        def column(j, _):
            for q in range(3):
                upper = part[rows_of(j, q), :]
                a, b = mine[piece, rows_of(j, q), :], theirs[piece, rows_of(j, q), :]
                da, db = mine[piece, decay_of(j, q), :], theirs[piece, decay_of(j, q), :]
                lower = jnp.where(core == 0, da * upper + a, db * upper + b)
                own[piece, rows_of(j, q), :] = jnp.where(core == 0, upper, lower)
                other[piece, rows_of(j, q), :] = jnp.where(core == 0, lower, upper)
            return 0

        lax.fori_loop(0, BLOCK, column, 0, unroll=4)


def reads_kernel(states, cmap, carried, *, half):
    low = low_lanes()
    core, _ = place()

    def block(k, _):
        for j in range(BLOCK):
            first, second, third = [
                states[k, j * 24 + 8 * q : j * 24 + 8 * q + 8, :] for q in range(3)
            ]
            turned = pltpu.roll(third, HALF, 1)
            right = [jnp.where(low, third, turned), jnp.where(low, turned, third)]
            whole = jnp.concatenate(
                [
                    jnp.concatenate([first, second], axis=0),
                    jnp.concatenate(right, axis=0),
                ],
                axis=1,
            )
            at = k * BLOCK + j
            reads = cmap[(core ^ half) * HALF + at][:, 0:32].astype(bf16)
            result = dot(reads, jnp.concatenate(split(whole), axis=0), ((1,), (0,)))
            for g in range(2):
                carried[:, g, at, :] = result[:, g * 128 : g * 128 + 128]
        return 0

    lax.fori_loop(0, HALVED, block, 0)


def exit_kernel(
    own, other, cmap, gated_a, gated_b, reach, norm_gain, out_weight, out, carried
):
    core, _ = place()
    reads_kernel(other, cmap, carried, half=1)
    turned = out_weight[...].astype(f32).T
    weight = jnp.concatenate([turned, jnp.zeros((WIDTH, HALF), f32)], axis=1).astype(bf16)
    pad = jnp.zeros((1, HALF), f32)
    gain = [norm_gain[:, 0:128], jnp.concatenate([norm_gain[:, 128:192], pad], axis=1)]

    def row(r, begins, gated):
        i = r - begins
        parts = []
        for g in range(2):
            a, b = own[r, g], carried[r, g]
            both = [jnp.where(core == 0, a, b), jnp.where(core == 0, b, a)]
            parts.append(gated[i, g] + reach[r, g] * jnp.concatenate(both, axis=0))
        total = jnp.sum(parts[0] * parts[0] + parts[1] * parts[1], axis=1, keepdims=True)
        scale = lax.rsqrt(total * (1.0 / INNER) + norm_eps)
        normed = [(parts[g] * scale * gain[g]).astype(bf16) for g in range(2)]
        result = dot(weight, jnp.concatenate(normed, axis=1), ((1,), (1,)))
        out[r] = result.astype(bf16)

    for begins, gated in ((0, gated_a), (ROWS // 2, gated_b)):

        def some(k, carry):
            for i in range(4):
                row(begins + 4 * k + i, begins, gated)
            return carry

        lax.fori_loop(0, ROWS // 8, some, 0)


def call(kernel, spaces, shapes, scratch, *operands, after=()):
    kinds = {"v": pltpu.VMEM, "s": pltpu.SMEM, "h": pl.ANY}
    first, waits = len(operands), len(after)
    spaces, operands = spaces + "h" * waits, operands + tuple(after)

    def inner(*refs):
        kernel(*refs[:first], *refs[first + waits :])

    return pl.pallas_call(
        inner,
        in_specs=[pl.BlockSpec(memory_space=kinds[k]) for k in spaces],
        out_specs=[pl.BlockSpec(memory_space=kinds[k]) for _, _, k in shapes],
        out_shape=[jax.ShapeDtypeStruct(s, t) for s, t, _ in shapes],
        scratch_shapes=scratch,
        compiler_params=pltpu.CompilerParams(vmem_limit_bytes=VMEM),
    )(*operands)


def steps(axis):
    count = lax.axis_size(axis)
    up = [(i, i + 1) for i in range(count - 1)]
    return up, [(j, i) for i, j in up]


def on_device(
    tokens,
    in_weight,
    conv_weight,
    conv_bias,
    step_bias,
    decay_log,
    skip_gain,
    norm_gain,
    out_weight,
):
    to_right, to_left = steps("gx")
    to_down, to_up = steps("gy")
    last, first = tokens[:, :, COLS - 1], tokens[:, :, 0]
    left = lax.ppermute(last, "gx", to_right)
    right = lax.ppermute(first, "gx", to_left)
    vmem = pltpu.VMEM
    rows8 = ((ROWS, 8, LANES), f32, "v")
    inner, gate, step, compact, totals, conv_w, taps = call(
        project_kernel,
        "vvvvss",
        [(PLANE, bf16, "v"), (PLANE, bf16, "v"), (PLANE, f32, "v"), rows8, rows8]
        + [((WIDTH, 256), bf16, "v"), ((2, 16, LANES), f32, "v")],
        [vmem((WIDTH, 768), bf16)],
        tokens,
        in_weight,
        conv_weight,
        conv_bias.reshape(1, 224),
        step_bias,
        decay_log,
        after=(last, first),
    )
    edge_row = ((WIDTH + 16, LANES), bf16, "v")
    down_row, up_row = call(
        pack_kernel, "vvv", [edge_row] * 2, [], tokens, left, right, after=(conv_w,)
    )
    above = lax.ppermute(down_row, "gy", to_down)
    below = lax.ppermute(up_row, "gy", to_up)
    packet = ((8, 16, LANES), f32, "v")
    quarters = vmem((CHIPS,) + packet[0], f32)
    all_ends = ((2 * ROWS, 16, LANES), f32, "v")
    cells = ((COLS, ROWS, LANES), f32, "v")
    xdt, decay, act, bct, cmap, ends = call(
        inside_kernel,
        "v" * 8 + "s",
        [
            (PLANE, f32, "v"),
            (PLANE, f32, "v"),
            (PLANE, bf16, "v"),
            ((ROWS, 32, COLS), f32, "v"),
            cells,
            all_ends,
        ],
        [vmem((ROWS, 2, 144, LANES), f32)],
        inner,
        left,
        right,
        step,
        compact,
        totals,
        conv_w,
        taps,
        decay_log,
        after=(up_row, down_row),
    )
    two = (2,) + PLANE[1:]
    xdt_edge, act_edge, bct_edge, cmap, *ends = call(
        edge_kernel,
        "v" * 12,
        [(two, f32, "v"), (two, bf16, "v"), ((2, 32, COLS), f32, "v"), cells]
        + [packet] * CHIPS,
        [vmem((6, 2, 144, LANES), f32), vmem(all_ends[0], f32)],
        inner,
        above,
        below,
        left,
        right,
        step,
        compact,
        totals,
        conv_w,
        taps,
        cmap,
        ends,
    )
    scanned = (xdt, xdt_edge, decay, bct, bct_edge)
    gx_count = lax.axis_size("gx")

    def members(pieces):
        moved = [pieces[0]] * CHIPS
        for k in (2, 1, 3):
            pairs = [(i, i // 4 * 4 + (i + k) % 4) for i in range(gx_count)]
            moved[k] = lax.ppermute(pieces[k], "gx", pairs)
        return moved

    piece, piece_out = (PIECE, f32, "v"), (PIECE_OUT, f32, "v")
    halves = ((HALVED,) + PIECE, f32, "v")
    tiles = ((3 * ROWS, 8, LANES), f32, "v")
    sent = ends[:1]
    left_half, middle = call(
        functools.partial(bottom_kernel, half=0),
        "vvvvv",
        [halves, tiles],
        [],
        *scanned,
        after=sent,
    )
    ends = members(ends)
    (whole,) = call(members_kernel, "vvvv", [packet], [quarters], *ends, after=(middle,))
    beside = lax.ppermute(whole, "gx", [(i, i ^ 4) for i in range(gx_count)])
    gating, reach = call(
        gating_kernel, "vv", [(PLANE, f32, "v")] * 2, [], decay, gate, after=(whole,)
    )
    (both,) = call(pair_kernel, "vv", [packet], [], whole, beside, after=(reach,))
    (right_half,) = call(
        functools.partial(bottom_kernel, half=1),
        "vvvvvv",
        [halves],
        [],
        *scanned,
        middle,
        after=(both,),
    )
    mid, near, far = [
        lax.ppermute(both, "gx", [(i, i + 8 * k) for i in range(gx_count - 8 * k)])
        for k in (2, 1, 3)
    ]
    carries = call(
        carry_kernel, "v" * 8, [packet] * CHIPS, [quarters], near, mid, far, beside, *ends,
        after=(right_half,),
    )
    (coef,) = call(
        weight_kernel, "vvs", [(PLANE, f32, "v")], [], step, decay, decay_log, after=carries[:1]
    )
    carries = members(carries)
    mine, theirs, carry = call(
        add_kernel,
        "v" * 7,
        [halves, halves, ((2 * ROWS, 16, LANES), f32, "v")],
        [vmem(tiles[0], f32)],
        coef,
        left_half,
        right_half,
        *carries,
    )
    gy_count = lax.axis_size("gy")
    swap = [(i, i ^ 1) for i in range(gy_count)]
    ahead = [[(i, (i + 2 * k) % gy_count) for i in range(gy_count)] for k in range(CHIPS)]

    def rotate(pieces):
        moved = [pieces[0]] * CHIPS
        for k in (2, 1, 3):
            moved[k] = lax.ppermute(pieces[k], "gy", ahead[k])
        return moved

    theirs = lax.ppermute(theirs, "gy", swap)
    joined = call(join_kernel, "vv", [piece] * CHIPS, [], mine, theirs)
    pieces = rotate(joined)
    half = ((ROWS // 2,) + PLANE[1:], f32, "v")
    local_scratch = vmem((2, 8, COLS, LANES), f32)
    inner = (*scanned, carry, act, act_edge, gating, skip_gain)
    gated_a, track = call(
        functools.partial(local_kernel, 0),
        "v" * 9 + "s",
        [half, ((BLOCKS,) + PIECE_OUT, f32, "v")],
        [local_scratch],
        *inner,
        after=joined[:1],
    )
    pieces = call(
        col_prefix_kernel,
        "vvvv",
        [piece_out] * CHIPS,
        [vmem((CHIPS,) + PIECE, f32), vmem((CHIPS,) + PIECE_OUT, f32)],
        *pieces,
        after=(track,),
    )
    above_chip = pieces[0]
    pieces = rotate(pieces)
    (gated_b,) = call(
        functools.partial(local_kernel, ROWS // 2),
        "v" * 9 + "sv",
        [half],
        [local_scratch],
        *inner,
        track,
        after=(above_chip,),
    )
    halves_out = ((HALVED,) + PIECE_OUT, f32, "v")
    own, other = call(
        share_kernel, "vvvvvv", [halves_out] * 2, [], *pieces, mine, theirs, after=(gated_b,)
    )
    sent = other
    other = lax.ppermute(sent, "gy", swap)
    half_plane = (ROWS, 2, HALF, LANES)
    (own,) = call(
        functools.partial(reads_kernel, half=0),
        "vv",
        [(half_plane, f32, "v")],
        [],
        own,
        cmap,
        after=(sent,),
    )
    (out,) = call(
        exit_kernel,
        "vvvvvvvv",
        [((ROWS, WIDTH, COLS), bf16, "v")],
        [vmem(half_plane, f32)],
        own,
        other,
        cmap,
        gated_a,
        gated_b,
        reach,
        norm_gain.reshape(1, INNER),
        out_weight,
    )
    return out


def solution(mesh):
    return jax.shard_map(
        on_device,
        mesh=mesh,
        in_specs=(P("gy", None, "gx"), P(), P(), P(), P(), P(), P(), P(), P()),
        out_specs=P("gy", None, "gx"),
        check_vma=False,
    )
```

```python
import functools

import jax
import jax.numpy as jnp
from jax import lax
from jax.experimental import pallas as pl
from jax.experimental.pallas import tpu as pltpu
from jax.sharding import PartitionSpec as P

f32, bf16 = jnp.float32, jnp.bfloat16
norm_eps = 1e-05
ROWS, COLS, WIDTH, LANES = 16, 128, 96, 128
INNER, STATE, HALF = 192, 16, 64
BLOCK, BLOCKS = 16, 8
HALVED, CHIPS = BLOCKS // 2, 4
PIECE, PIECE_OUT = (BLOCK * 26, LANES), (BLOCK * 24, LANES)
PLANE = (ROWS, 2, COLS, LANES)
VMEM = 12 * 1024 * 1024


def silu(v):
    return v / (1.0 + jnp.exp(-v))


def split(v):
    high = v.astype(bf16)
    return high, (v - high.astype(f32)).astype(bf16)


def dot(a, b, dims):
    return lax.dot_general(a, b, (dims, ((), ())), preferred_element_type=f32)


def low_lanes(rows=8):
    return lax.broadcasted_iota(jnp.int32, (rows, LANES), 1) < HALF


def by_head(values, g):
    if g == 1:
        return jnp.full((1, LANES), values[2], f32)
    return jnp.where(low_lanes(1), values[0], values[1])


def fold_sublanes(parts):
    place = lax.broadcasted_iota(jnp.int32, (8, LANES), 0)
    step = 1
    while len(parts) > 1:
        first = (place & step) == 0
        parts = [
            jnp.where(first, a, b) + pltpu.roll(jnp.where(first, b, a), 8 - step, 0)
            for a, b in zip(parts[0::2], parts[1::2])
        ]
        step *= 2
    return parts[0]


def each_row(body, together):
    def some(k, carry):
        for i in range(together):
            body(k * together + i)
        return carry

    lax.fori_loop(0, ROWS // together, some, 0)


def spread(values, q, j):
    return jnp.broadcast_to(values[8 * q : 8 * q + 8, j : j + 1], (8, LANES))


def softplus(v):
    return jnp.maximum(v, 0.0) + jnp.log1p(jnp.exp(-jnp.abs(v)))


def project_kernel(
    tok,
    in_weight,
    conv_weight,
    conv_bias,
    step_bias,
    decay_log,
    inner,
    steps,
    compact,
    totals,
    conv_w,
    taps,
    weight,
):
    load_taps(conv_weight, conv_bias, taps)
    source = in_weight[...].astype(f32)
    chan_b, chan_c = source[:, 384:400], source[:, 400:416]
    step_w = [jnp.broadcast_to(source[:, 416 + h : 417 + h], (WIDTH, HALF)) for h in range(3)]
    wide = [
        source[:, 192:384],
        chan_c,
        chan_c,
        chan_b,
        jnp.zeros((WIDTH, 16), f32),
        step_w[0],
        step_w[1],
        step_w[2],
        step_w[2],
    ]
    weight[...] = jnp.concatenate(wide, axis=1).astype(bf16)
    conv_w[...] = weight[:, 0:256]
    step_turned = jnp.concatenate([source[:, 416:419], jnp.zeros((WIDTH, 125), f32)], axis=1)
    step_turned = step_turned.T[0:8, :].astype(bf16)

    def own_row(r):
        out = dot(tok[r], weight[...], ((0,), (0,))).astype(bf16)
        compact[r] = dot(step_turned, tok[r], ((1,), (0,))).astype(bf16).astype(f32)
        for g in range(2):
            inner[r, g] = out[:, g * 128 : g * 128 + 128]
            raw = out[:, 256 + g * 128 : 384 + g * 128].astype(f32) + by_head(step_bias, g)
            steps[r, g] = softplus(raw)

    each_row(own_row, 8)

    head = lax.broadcasted_iota(jnp.int32, (8, LANES), 0)

    def head_rows(ref):
        return jnp.where(head == 0, ref[0], jnp.where(head == 1, ref[1], ref[2]))

    step = softplus(compact[...] + head_rows(step_bias))
    log_decay = (-jnp.exp(head_rows(decay_log)) * step).reshape(ROWS * 8, LANES)
    log_decay = jnp.concatenate(split(log_decay), axis=1)
    from_at = lax.broadcasted_iota(jnp.int32, (2 * COLS, COLS), 0) & (COLS - 1)
    to_at = lax.broadcasted_iota(jnp.int32, (2 * COLS, COLS), 1)
    later = jnp.where(from_at > to_at, 1.0, 0.0).astype(bf16)
    suffix = dot(log_decay, later, ((1,), (0,)))
    whole = dot(log_decay, jnp.ones((2 * COLS, COLS), bf16), ((1,), (0,)))
    compact[...] = step * jnp.exp(suffix).reshape(ROWS, 8, LANES)
    totals[...] = jnp.exp(whole).reshape(ROWS, 8, LANES)


def pack_kernel(tok, left, right, *outs):
    for out, r in zip(outs, (ROWS - 1, 0)):
        sides = [left[r : r + 1, :].astype(f32), right[r : r + 1, :].astype(f32)]
        sides = jnp.concatenate(sides + [jnp.zeros((14, WIDTH), f32)], axis=0)
        sides = jnp.concatenate([sides, jnp.zeros((16, LANES - WIDTH), f32)], axis=1)
        out[0:WIDTH, :] = tok[r]
        out[WIDTH:, :] = sides.astype(bf16)


def load_taps(conv_weight, conv_bias, taps):
    for k in range(10):
        v = conv_bias[...] if k == 9 else conv_weight[k // 3, k % 3 : k % 3 + 1, :]
        taps[0, k : k + 1, :] = v[:, 0:128]
        tail = [v[:, 128:192], v[:, 208:224], v[:, 208:224], v[:, 192:208]]
        taps[1, k : k + 1, :] = jnp.concatenate(tail + [jnp.zeros((1, 16), f32)], axis=1)


def conv_part(tokens, conv_w, dims):
    return dot(tokens, conv_w[...], dims).astype(bf16).astype(f32)


def put_sides(left, right, conv_w, proj, begins, first, count):
    for ref, at in ((left, 7), (right, 136)):
        out = conv_part(ref[...], conv_w, ((1,), (0,)))
        for g in range(2):
            proj[first : first + count, g, at, :] = out[
                begins : begins + count, g * 128 : g * 128 + 128
            ]


def conv_row(proj, taps, at):
    parts = []
    for g in range(2):
        acc = jnp.broadcast_to(taps[g, 9:10, :], (COLS, LANES))
        for a in range(3):
            for b in range(3):
                k = a * 3 + b
                acc = acc + taps[g, k : k + 1, :] * proj[at + a, g, 7 + b : 135 + b, :]
        parts.append(silu(acc).astype(bf16).astype(f32))
    return parts


def finish_row(parts, steps, compact, totals, xdt, act, bct, maps, ends):
    maps[...] = parts[1].astype(bf16)
    turned = parts[1].T
    chan_b = turned[96:112, :]
    bct[0:16, :] = chan_b
    bct[16:32, :] = turned[64:80, :]
    other = pltpu.roll(parts[1], HALF, 1)
    whole = [parts[0], jnp.where(low_lanes(COLS), parts[1], other)]
    for g in range(2):
        act[g] = whole[g].astype(bf16)
        xdt[g] = steps[g] * whole[g]
    weighted = [compact[h : h + 1, :] * chan_b for h in range(3)]
    weighted = jnp.concatenate(split(jnp.concatenate(weighted, axis=0)), axis=0)
    inner_x = jnp.concatenate(whole, axis=1).astype(bf16)
    state = dot(weighted, inner_x, ((1,), (0,)))
    state = state[0:48, :] + state[48:96, :]
    first = jnp.where(low_lanes(16), state[0:16, 0:128], state[16:32, 0:128])
    third = jnp.where(low_lanes(), state[32:40, 128:256], state[40:48, 128:256])
    total = jnp.where(low_lanes(1), totals[0:1, :], totals[1:2, :])
    rest = jnp.concatenate([total, totals[2:3, :], jnp.zeros((2, LANES), f32)], axis=0)
    ends[0] = jnp.concatenate([first[0:8, :], third[0:4, :], rest], axis=0)
    ends[1] = jnp.concatenate([first[8:16, :], third[4:8, :], rest], axis=0)


def inside_kernel(
    inner,
    left,
    right,
    steps,
    compact,
    totals,
    conv_w,
    taps,
    decay_log,
    xdt,
    decay,
    act,
    bct,
    maps,
    ends,
    proj,
):
    put_sides(left, right, conv_w, proj, 0, 0, ROWS)
    rate = [-jnp.exp(by_head(decay_log, g)) for g in range(2)]

    def own_row(r):
        for g in range(2):
            proj[r, g, 8:136, :] = inner[r, g].astype(f32)
            decay[r, g] = jnp.exp(rate[g] * steps[r, g])

    each_row(own_row, 4)

    def some(k, carry):
        for i in range(7):
            r = 1 + 7 * k + i
            parts = conv_row(proj, taps, r - 1)
            refs = [ref.at[r] for ref in (steps, compact, totals, xdt, act, bct, maps)]
            finish_row(parts, *refs, ends.at[pl.ds(2 * r, 2)])
        return carry

    lax.fori_loop(0, 2, some, 0)


def edge_kernel(
    inner,
    above,
    below,
    left,
    right,
    steps,
    compact,
    totals,
    conv_w,
    taps,
    ends,
    xdt,
    act,
    bct,
    maps,
    *refs,
):
    ends_out, (proj, held) = refs[:CHIPS], refs[CHIPS:]
    put_sides(left, right, conv_w, proj, 0, 1, 2)
    put_sides(left, right, conv_w, proj, ROWS - 2, 3, 2)
    for at, ref in ((0, above), (5, below)):
        out = conv_part(ref[0:WIDTH, :], conv_w, ((0,), (0,)))
        sides = conv_part(ref[WIDTH:, 0:WIDTH], conv_w, ((1,), (0,)))
        for g in range(2):
            proj[at, g, 8:136, :] = out[:, g * 128 : g * 128 + 128]
            proj[at, g, 7:8, :] = sides[0:1, g * 128 : g * 128 + 128]
            proj[at, g, 136:137, :] = sides[1:2, g * 128 : g * 128 + 128]
    for at, r in ((1, 0), (2, 1), (3, ROWS - 2), (4, ROWS - 1)):
        for g in range(2):
            proj[at, g, 8:136, :] = inner[r, g].astype(f32)
    held[...] = ends[...]
    for e, r in enumerate((0, ROWS - 1)):
        parts = conv_row(proj, taps, 3 * e)
        own = [ref.at[r] for ref in (steps, compact, totals)]
        mine = [ref.at[e] for ref in (xdt, act, bct, maps)]
        finish_row(parts, *own, *mine, held.at[pl.ds(2 * r, 2)])
    member, _ = line()
    for k, out in enumerate(ends_out):
        out[...] = held[pl.ds((member + k) % CHIPS * 8, 8)]


def cells_kernel(maps_in, maps_edge, cmap):
    for r in range(ROWS):
        cmap[:, r, :] = pltpu.roll(row_of((maps_in, maps_edge), r)[...].astype(f32), HALF, 1)


def row_of(pair, r):
    inside, edge = pair
    if r in (0, ROWS - 1):
        return edge.at[0 if r == 0 else 1]
    return inside.at[r]


def line():
    gx = lax.axis_index("gx")
    return gx % 4, gx // 4


def part_of(ref, i, at=None):
    box = ref if at is None else ref.at[at]
    return (box[i, 0:8, :], box[i, 8:16, :]), (box[i, 12:13, :], box[i, 13:14, :])


def put(ref, i, tiles, decays=None):
    ref[i, 0:8, :] = tiles[0]
    ref[i, 8:16, :] = tiles[1]
    if decays is not None:
        ref[i, 12:13, :] = decays[0]
        ref[i, 13:14, :] = decays[1]


def chain(tiles, step):
    return [d * a + b for a, b, d in zip(tiles, *step)]


def product(a, b):
    return [u * v for u, v in zip(a, b)]


def members_kernel(*refs):
    parts, (out, held) = refs[:CHIPS], refs[CHIPS:]
    member, _ = line()
    for k, part in enumerate(parts):
        held[(member + CHIPS - k) % CHIPS] = part[...]
    for i in range(8):
        tiles, decays = part_of(held, i, 0)
        for m in range(1, CHIPS):
            step = part_of(held, i, m)
            tiles, decays = chain(tiles, step), product(decays, step[1])
        put(out, i, tiles, decays)


def pair_kernel(mine, theirs, out):
    _, z = line()
    odd = z % 2 == 1
    for i in range(8):
        a, b = part_of(mine, i), part_of(theirs, i)
        after, before = chain(b[0], a), chain(a[0], b)
        tiles = [jnp.where(odd, u, v) for u, v in zip(after, before)]
        put(out, i, tiles, product(a[1], b[1]))


def carry_kernel(near, mid, far, theirs, *refs):
    parts, outs, held = refs[:CHIPS], refs[CHIPS : 2 * CHIPS], refs[-1]
    member, z = line()
    odd = z % 2 == 1
    for k, part in enumerate(parts):
        held[(member + CHIPS - k) % CHIPS] = part[...]
    for i in range(8):
        tiles = part_of(far, i)[0]
        for part in (mid, near):
            tiles = chain(tiles, part_of(part, i))
        tiles = [jnp.where(odd, u, v) for u, v in zip(chain(tiles, part_of(theirs, i)), tiles)]
        for m in range(CHIPS):
            step = part_of(held, i, m)
            put(held.at[m], i, tiles)
            tiles = chain(tiles, step)
    for k, out in enumerate(outs):
        out[...] = held[(member + k) % CHIPS]


def starts(carry, r):
    third = jnp.concatenate([carry[2 * r, 8:12, :], carry[2 * r + 1, 8:12, :]], axis=0)
    return [carry[2 * r, 0:8, :], carry[2 * r + 1, 0:8, :], third]


def bottom_kernel(xdt_in, xdt_edge, decay, bct_in, bct_edge, *refs, half):
    if half:
        state_in, bottom = refs
        begin = [state_in[i] for i in range(3 * ROWS)]
    else:
        bottom, state_out = refs
        begin = [jnp.zeros((8, LANES), f32)] * (3 * ROWS)
    low = low_lanes()
    xdt = [row_of((xdt_in, xdt_edge), r) for r in range(ROWS)]
    bct = [row_of((bct_in, bct_edge), r) for r in range(ROWS)]

    def block(k, state):
        state = list(state)
        base = pl.multiple_of((half * HALVED + k) * BLOCK, BLOCK)
        maps = [pltpu.roll(bct[r][0:16, :], COLS - base, 1) for r in range(ROWS)]
        for j in range(BLOCK):
            cols = [jnp.zeros((8, LANES), f32)] * 3
            for r in range(ROWS):
                wide = [spread(maps[r], q, j) for q in range(2)]
                wide.append(jnp.where(low, wide[0], wide[1]))
                x = [xdt[r][g, pl.ds(base + j, 8, stride=0), :] for g in range(2)]
                d = [decay[r, g, pl.ds(base + j, 8, stride=0), :] for g in range(2)]
                for q in range(3):
                    g = q // 2
                    state[3 * r + q] = d[g] * state[3 * r + q] + x[g] * wide[q]
                    cols[q] = d[g] * cols[q] + state[3 * r + q]
            for q in range(3):
                bottom[k, j * 24 + 8 * q : j * 24 + 8 * q + 8, :] = cols[q]
        for g in range(2):
            whole = decay[0, g, pl.ds(base, BLOCK), :]
            for r in range(1, ROWS):
                whole = whole * decay[r, g, pl.ds(base, BLOCK), :]
            bottom[k, 384 + 16 * g : 400 + 16 * g, :] = whole
        return tuple(state)

    state = lax.fori_loop(0, HALVED, block, tuple(begin))
    if not half:
        for i in range(3 * ROWS):
            state_out[i] = state[i]


def weight_kernel(steps, decay, decay_log, coef):
    row_at = lax.broadcasted_iota(jnp.int32, (COLS, 2 * COLS), 0)
    col_at = lax.broadcasted_iota(jnp.int32, (COLS, 2 * COLS), 1) & (COLS - 1)
    upto = jnp.where(col_at <= row_at, 1.0, 0.0).astype(bf16)
    rate = [-jnp.exp(by_head(decay_log, g)) for g in range(2)]
    rate = jnp.concatenate(rate, axis=1)

    def some(k, below):
        below = list(below)
        for i in range(4):
            r = ROWS - 1 - (k * 4 + i)
            along = rate * jnp.concatenate([steps[r, 0], steps[r, 1]], axis=1)
            along = dot(upto, jnp.concatenate(split(along), axis=0), ((1,), (0,)))
            along = jnp.exp(along)
            for g in range(2):
                coef[r, g] = along[:, g * 128 : g * 128 + 128] * below[g]
                below[g] = below[g] * decay[r, g]
        return tuple(below)

    lax.fori_loop(0, ROWS // 4, some, (jnp.ones((COLS, LANES), f32),) * 2)


def add_kernel(coef, left_half, right_half, *refs):
    parts, (mine, theirs, carry, hold) = refs[:CHIPS], refs[CHIPS:]
    core, _ = place()
    member, _ = line()
    for k, part in enumerate(parts):
        carry[pl.ds((member + CHIPS - k) % CHIPS * 8, 8)] = part[...]
    for r in range(ROWS):
        hold[3 * r], hold[3 * r + 1], hold[3 * r + 2] = starts(carry, r)

    def block(k, _, source, out, base):
        for at in range(0, BLOCK, 4):
            sums = [
                source[k, 24 * j + 8 * q : 24 * j + 8 * q + 8, :]
                for j in range(at, at + 4)
                for q in range(3)
            ]
            for r in range(ROWS):
                tiles = [hold[3 * r + q] for q in range(3)]
                for j in range(4):
                    c = base + k * BLOCK + at + j
                    w = [coef[r, g, pl.ds(c, 8, stride=0), :] for g in range(2)]
                    for q in range(3):
                        sums[3 * j + q] = sums[3 * j + q] + w[q // 2] * tiles[q]
            for j in range(4):
                for q in range(3):
                    row = 24 * (at + j) + 8 * q
                    out[k, row : row + 8, :] = sums[3 * j + q]
        out[k, 384:416, :] = source[k, 384:416, :]
        return 0

    def both(outs):
        for half, source in enumerate((left_half, right_half)):
            run = functools.partial(block, source=source, out=outs[half], base=half * HALF)
            lax.fori_loop(0, HALVED, run, 0)

    @pl.when(core == 0)
    def _():
        both((mine, theirs))

    @pl.when(core != 0)
    def _():
        both((theirs, mine))


def gating_kernel(decay, tok, in_weight, gating, reach, weight):
    source = in_weight[...].astype(f32)
    wide = [source[:, 0:INNER], jnp.zeros((WIDTH, HALF), f32)]
    weight[...] = jnp.concatenate(wide, axis=1).astype(bf16)

    def some(k, along):
        along = list(along)
        for i in range(4):
            r = k * 4 + i
            gate = dot(tok[r], weight[...], ((0,), (0,))).astype(bf16).astype(f32)
            for g in range(2):
                along[g] = along[g] * decay[r, g]
                gated = silu(gate[:, g * 128 : g * 128 + 128])
                gating[r, g] = gated
                reach[r, g] = along[g] * gated
        return tuple(along)

    lax.fori_loop(0, ROWS // 4, some, (jnp.ones((COLS, LANES), f32),) * 2)


def local_kernel(
    begins,
    xdt_in,
    xdt_edge,
    decay,
    bct_in,
    bct_edge,
    carry,
    act_in,
    act_edge,
    gating,
    skip_gain,
    *refs,
):
    if begins:
        track_in, gated, local = refs
    else:
        gated, track, local = refs
    low = low_lanes()
    xdt = [row_of((xdt_in, xdt_edge), r) for r in range(ROWS)]
    bct = [row_of((bct_in, bct_edge), r) for r in range(ROWS)]
    act = [row_of((act_in, act_edge), r) for r in range(ROWS)]
    count = ROWS // 2
    begin = []
    for i in range(count):
        begin += starts(carry, begins + i)

    def block(cb, state):
        state = list(state)
        base = cb * BLOCK
        maps = [pltpu.roll(bct[begins + i][...], COLS - base, 1) for i in range(count)]
        for j in range(BLOCK):
            if begins:
                cols = [track_in[cb, j * 24 + 8 * q : j * 24 + 8 * q + 8, :] for q in range(3)]
            else:
                cols = [jnp.zeros((8, LANES), f32)] * 3
            reads = []
            for i in range(count):
                r = begins + i
                wide = [spread(maps[i], q, j) for q in range(4)]
                b_all = [wide[0], wide[1], jnp.where(low, wide[0], wide[1])]
                x = [xdt[r][g, pl.ds(base + j, 8, stride=0), :] for g in range(2)]
                d = [decay[r, g, pl.ds(base + j, 8, stride=0), :] for g in range(2)]
                for q in range(3):
                    g = q // 2
                    state[3 * i + q] = d[g] * state[3 * i + q] + x[g] * b_all[q]
                    cols[q] = d[g] * cols[q] + state[3 * i + q]
                reads.append(wide[2] * cols[0] + wide[3] * cols[1])
                reads.append(jnp.where(low, wide[2], wide[3]) * cols[2])
            if not begins:
                for q in range(3):
                    track[cb, j * 24 + 8 * q : j * 24 + 8 * q + 8, :] = cols[q]
            for k in range(2):
                local[k, :, base + j, :] = fold_sublanes(reads[8 * k : 8 * k + 8])
        return tuple(state)

    lax.fori_loop(0, BLOCKS, block, tuple(begin))
    for i in range(count):
        r = begins + i
        for g in range(2):
            mixed = local[i // 4, (i % 4) * 2 + g]
            if g == 1:
                mixed = mixed + pltpu.roll(mixed, HALF, 1)
            mixed = mixed + by_head(skip_gain, g) * act[r][g].astype(f32)
            gated[i, g] = mixed * gating[r, g]


def place():
    gy = lax.axis_index("gy")
    return gy % 2, gy // 2


def rows_of(j, q):
    return pl.ds(pl.multiple_of(j * 24 + 8 * q, 8), 8)


def decay_of(j, q):
    return pl.ds(BLOCK * (24 + q // 2) + j, 8, stride=0)


def join_kernel(mine, theirs, *outs):
    core, chip = place()
    for k, out in enumerate(outs):
        piece = (chip + k) % CHIPS

        def column(j, _):
            for q in range(3):
                a, b = mine[piece, rows_of(j, q), :], theirs[piece, rows_of(j, q), :]
                da, db = mine[piece, decay_of(j, q), :], theirs[piece, decay_of(j, q), :]
                out[rows_of(j, q), :] = jnp.where(core == 0, db * a + b, da * b + a)
            return 0

        lax.fori_loop(0, BLOCK, column, 0, unroll=4)
        rest = pl.ds(BLOCK * 24, BLOCK * 2)
        out[rest, :] = mine[piece, rest, :] * theirs[piece, rest, :]


def col_prefix_kernel(*refs):
    parts, outs, held, ready = refs[:CHIPS], refs[CHIPS : 2 * CHIPS], refs[-2], refs[-1]
    _, chip = place()
    for k, part in enumerate(parts):
        held[(chip + CHIPS - k) % CHIPS] = part[...]

    def column(j, _):
        for q in range(3):
            state = jnp.zeros((8, LANES), f32)
            for s in range(CHIPS):
                ready[s, rows_of(j, q), :] = state
                state = held[s, decay_of(j, q), :] * state + held[s, rows_of(j, q), :]
        return 0

    lax.fori_loop(0, BLOCK, column, 0, unroll=4)
    for k, out in enumerate(outs):
        out[...] = ready[(chip + k) % CHIPS]


def share_kernel(*refs):
    parts, (mine, theirs, own, other) = refs[:CHIPS], refs[CHIPS:]
    core, chip = place()
    for k, part in enumerate(parts):
        piece = (chip + CHIPS - k) % CHIPS

        def column(j, _):
            for q in range(3):
                upper = part[rows_of(j, q), :]
                a, b = mine[piece, rows_of(j, q), :], theirs[piece, rows_of(j, q), :]
                da, db = mine[piece, decay_of(j, q), :], theirs[piece, decay_of(j, q), :]
                lower = jnp.where(core == 0, da * upper + a, db * upper + b)
                own[piece, rows_of(j, q), :] = jnp.where(core == 0, upper, lower)
                other[piece, rows_of(j, q), :] = jnp.where(core == 0, lower, upper)
            return 0

        lax.fori_loop(0, BLOCK, column, 0, unroll=4)


def reads_kernel(states, cmap, carried, *, half):
    low = low_lanes()
    core, _ = place()

    def block(k, _):
        for j in range(BLOCK):
            first, second, third = [
                states[k, j * 24 + 8 * q : j * 24 + 8 * q + 8, :] for q in range(3)
            ]
            turned = pltpu.roll(third, HALF, 1)
            right = [jnp.where(low, third, turned), jnp.where(low, turned, third)]
            whole = jnp.concatenate(
                [
                    jnp.concatenate([first, second], axis=0),
                    jnp.concatenate(right, axis=0),
                ],
                axis=1,
            )
            at = k * BLOCK + j
            reads = cmap[(core ^ half) * HALF + at][:, 0:32].astype(bf16)
            result = dot(reads, jnp.concatenate(split(whole), axis=0), ((1,), (0,)))
            for g in range(2):
                carried[:, g, at, :] = result[:, g * 128 : g * 128 + 128]
        return 0

    lax.fori_loop(0, HALVED, block, 0)


def exit_kernel(
    own, other, cmap, gated_a, gated_b, reach, norm_gain, out_weight, out, carried
):
    core, _ = place()
    reads_kernel(other, cmap, carried, half=1)
    turned = out_weight[...].astype(f32).T
    weight = jnp.concatenate([turned, jnp.zeros((WIDTH, HALF), f32)], axis=1).astype(bf16)
    pad = jnp.zeros((1, HALF), f32)
    gain = [norm_gain[:, 0:128], jnp.concatenate([norm_gain[:, 128:192], pad], axis=1)]

    def row(r, begins, gated):
        i = r - begins
        parts = []
        for g in range(2):
            a, b = own[r, g], carried[r, g]
            both = [jnp.where(core == 0, a, b), jnp.where(core == 0, b, a)]
            parts.append(gated[i, g] + reach[r, g] * jnp.concatenate(both, axis=0))
        total = jnp.sum(parts[0] * parts[0] + parts[1] * parts[1], axis=1, keepdims=True)
        scale = lax.rsqrt(total * (1.0 / INNER) + norm_eps)
        normed = [(parts[g] * scale * gain[g]).astype(bf16) for g in range(2)]
        result = dot(weight, jnp.concatenate(normed, axis=1), ((1,), (1,)))
        out[r] = result.astype(bf16)

    for begins, gated in ((0, gated_a), (ROWS // 2, gated_b)):

        def some(k, carry):
            for i in range(4):
                row(begins + 4 * k + i, begins, gated)
            return carry

        lax.fori_loop(0, ROWS // 8, some, 0)


def call(kernel, spaces, shapes, scratch, *operands, after=()):
    kinds = {"v": pltpu.VMEM, "s": pltpu.SMEM, "h": pl.ANY}
    first, waits = len(operands), len(after)
    spaces, operands = spaces + "h" * waits, operands + tuple(after)

    def inner(*refs):
        kernel(*refs[:first], *refs[first + waits :])

    return pl.pallas_call(
        inner,
        in_specs=[pl.BlockSpec(memory_space=kinds[k]) for k in spaces],
        out_specs=[pl.BlockSpec(memory_space=kinds[k]) for _, _, k in shapes],
        out_shape=[jax.ShapeDtypeStruct(s, t) for s, t, _ in shapes],
        scratch_shapes=scratch,
        compiler_params=pltpu.CompilerParams(vmem_limit_bytes=VMEM),
    )(*operands)


def steps(axis):
    count = lax.axis_size(axis)
    up = [(i, i + 1) for i in range(count - 1)]
    return up, [(j, i) for i, j in up]


def on_device(
    tokens,
    in_weight,
    conv_weight,
    conv_bias,
    step_bias,
    decay_log,
    skip_gain,
    norm_gain,
    out_weight,
):
    to_right, to_left = steps("gx")
    to_down, to_up = steps("gy")
    vmem = pltpu.VMEM
    last, first = tokens[:, :, COLS - 1], tokens[:, :, 0]
    left = lax.ppermute(last, "gx", to_right)
    right = lax.ppermute(first, "gx", to_left)
    rows8 = ((ROWS, 8, LANES), f32, "v")
    inner, step, compact, totals, conv_w, taps = call(
        project_kernel,
        "vvvvss",
        [(PLANE, bf16, "v"), (PLANE, f32, "v"), rows8, rows8]
        + [((WIDTH, 256), bf16, "v"), ((2, 16, LANES), f32, "v")],
        [vmem((WIDTH, 512), bf16)],
        tokens,
        in_weight,
        conv_weight,
        conv_bias.reshape(1, 224),
        step_bias,
        decay_log,
        after=(last, first),
    )
    edge_row = ((WIDTH + 16, LANES), bf16, "v")
    down_row, up_row = call(
        pack_kernel, "vvv", [edge_row] * 2, [], tokens, left, right, after=(conv_w,)
    )
    above = lax.ppermute(down_row, "gy", to_down)
    below = lax.ppermute(up_row, "gy", to_up)
    packet = ((8, 16, LANES), f32, "v")
    quarters = vmem((CHIPS,) + packet[0], f32)
    all_ends = ((2 * ROWS, 16, LANES), f32, "v")
    cells = ((COLS, ROWS, LANES), f32, "v")
    xdt, decay, act, bct, maps, ends = call(
        inside_kernel,
        "v" * 8 + "s",
        [
            (PLANE, f32, "v"),
            (PLANE, f32, "v"),
            (PLANE, bf16, "v"),
            ((ROWS, 32, COLS), f32, "v"),
            ((ROWS, COLS, LANES), bf16, "v"),
            all_ends,
        ],
        [vmem((ROWS, 2, 144, LANES), f32)],
        inner,
        left,
        right,
        step,
        compact,
        totals,
        conv_w,
        taps,
        decay_log,
        after=(up_row, down_row),
    )
    two = (2,) + PLANE[1:]
    xdt_edge, act_edge, bct_edge, maps_edge, *ends = call(
        edge_kernel,
        "v" * 11,
        [(two, f32, "v"), (two, bf16, "v"), ((2, 32, COLS), f32, "v")]
        + [((2, COLS, LANES), bf16, "v")]
        + [packet] * CHIPS,
        [vmem((6, 2, 144, LANES), f32), vmem(all_ends[0], f32)],
        inner,
        above,
        below,
        left,
        right,
        step,
        compact,
        totals,
        conv_w,
        taps,
        ends,
    )
    scanned = (xdt, xdt_edge, decay, bct, bct_edge)
    gx_count = lax.axis_size("gx")

    def members(pieces):
        moved = [pieces[0]] * CHIPS
        for k in (2, 1, 3):
            pairs = [(i, i // 4 * 4 + (i + k) % 4) for i in range(gx_count)]
            moved[k] = lax.ppermute(pieces[k], "gx", pairs)
        return moved

    piece, piece_out = (PIECE, f32, "v"), (PIECE_OUT, f32, "v")
    halves = ((HALVED,) + PIECE, f32, "v")
    tiles = ((3 * ROWS, 8, LANES), f32, "v")
    sent = ends[:1]
    left_half, middle = call(
        functools.partial(bottom_kernel, half=0),
        "vvvvv",
        [halves, tiles],
        [],
        *scanned,
        after=sent,
    )
    ends = members(ends)
    (whole,) = call(members_kernel, "vvvv", [packet], [quarters], *ends, after=(middle,))
    beside = lax.ppermute(whole, "gx", [(i, i ^ 4) for i in range(gx_count)])
    gating, reach = call(
        gating_kernel,
        "vvv",
        [(PLANE, f32, "v")] * 2,
        [vmem((WIDTH, 256), bf16)],
        decay,
        tokens,
        in_weight,
        after=(whole,),
    )
    (both,) = call(pair_kernel, "vv", [packet], [], whole, beside, after=(reach,))
    (right_half,) = call(
        functools.partial(bottom_kernel, half=1),
        "vvvvvv",
        [halves],
        [],
        *scanned,
        middle,
        after=(both,),
    )
    mid, near, far = [
        lax.ppermute(both, "gx", [(i, i + 8 * k) for i in range(gx_count - 8 * k)])
        for k in (2, 1, 3)
    ]
    carries = call(
        carry_kernel, "v" * 8, [packet] * CHIPS, [quarters], near, mid, far, beside, *ends,
        after=(right_half,),
    )
    (coef,) = call(
        weight_kernel, "vvs", [(PLANE, f32, "v")], [], step, decay, decay_log, after=carries[:1]
    )
    carries = members(carries)
    mine, theirs, carry = call(
        add_kernel,
        "v" * 7,
        [halves, halves, ((2 * ROWS, 16, LANES), f32, "v")],
        [vmem(tiles[0], f32)],
        coef,
        left_half,
        right_half,
        *carries,
    )
    gy_count = lax.axis_size("gy")
    swap = [(i, i ^ 1) for i in range(gy_count)]
    ahead = [[(i, (i + 2 * k) % gy_count) for i in range(gy_count)] for k in range(CHIPS)]

    def rotate(pieces):
        moved = [pieces[0]] * CHIPS
        for k in (2, 1, 3):
            moved[k] = lax.ppermute(pieces[k], "gy", ahead[k])
        return moved

    theirs = lax.ppermute(theirs, "gy", swap)
    joined = call(join_kernel, "vv", [piece] * CHIPS, [], mine, theirs)
    pieces = rotate(joined)
    half = ((ROWS // 2,) + PLANE[1:], f32, "v")
    local_scratch = vmem((2, 8, COLS, LANES), f32)
    inner = (*scanned, carry, act, act_edge, gating, skip_gain)
    gated_a, track = call(
        functools.partial(local_kernel, 0),
        "v" * 9 + "s",
        [half, ((BLOCKS,) + PIECE_OUT, f32, "v")],
        [local_scratch],
        *inner,
        after=joined[:1],
    )
    (cmap,) = call(cells_kernel, "vv", [cells], [], maps, maps_edge, after=joined[:1])
    pieces = call(
        col_prefix_kernel,
        "vvvv",
        [piece_out] * CHIPS,
        [vmem((CHIPS,) + PIECE, f32), vmem((CHIPS,) + PIECE_OUT, f32)],
        *pieces,
        after=(track, cmap),
    )
    above_chip = pieces[0]
    pieces = rotate(pieces)
    (gated_b,) = call(
        functools.partial(local_kernel, ROWS // 2),
        "v" * 9 + "sv",
        [half],
        [local_scratch],
        *inner,
        track,
        after=(above_chip,),
    )
    halves_out = ((HALVED,) + PIECE_OUT, f32, "v")
    own, other = call(
        share_kernel, "vvvvvv", [halves_out] * 2, [], *pieces, mine, theirs, after=(gated_b,)
    )
    sent = other
    other = lax.ppermute(sent, "gy", swap)
    half_plane = (ROWS, 2, HALF, LANES)
    (own,) = call(
        functools.partial(reads_kernel, half=0),
        "vv",
        [(half_plane, f32, "v")],
        [],
        own,
        cmap,
        after=(sent,),
    )
    (out,) = call(
        exit_kernel,
        "vvvvvvvv",
        [((ROWS, WIDTH, COLS), bf16, "v")],
        [vmem(half_plane, f32)],
        own,
        other,
        cmap,
        gated_a,
        gated_b,
        reach,
        norm_gain.reshape(1, INNER),
        out_weight,
    )
    return out


def solution(mesh):
    return jax.shard_map(
        on_device,
        mesh=mesh,
        in_specs=(P("gy", None, "gx"), P(), P(), P(), P(), P(), P(), P(), P()),
        out_specs=P("gy", None, "gx"),
        check_vma=False,
    )
```

```python
import functools

import jax
import jax.numpy as jnp
from jax import lax
from jax.experimental import pallas as pl
from jax.experimental.pallas import tpu as pltpu
from jax.sharding import PartitionSpec as P

f32, bf16 = jnp.float32, jnp.bfloat16
norm_eps = 1e-05
ROWS, COLS, WIDTH, LANES = 16, 128, 96, 128
INNER, STATE, HALF = 192, 16, 64
BLOCK, BLOCKS = 16, 8
HALVED, CHIPS = BLOCKS // 2, 4
PIECE, PIECE_OUT = (BLOCK * 26, LANES), (BLOCK * 24, LANES)
PLANE = (ROWS, 2, COLS, LANES)
VMEM = 12 * 1024 * 1024


def silu(v):
    return v / (1.0 + jnp.exp(-v))


def split(v):
    high = v.astype(bf16)
    return high, (v - high.astype(f32)).astype(bf16)


def dot(a, b, dims):
    return lax.dot_general(a, b, (dims, ((), ())), preferred_element_type=f32)


def low_lanes(rows=8):
    return lax.broadcasted_iota(jnp.int32, (rows, LANES), 1) < HALF


def by_head(values, g):
    if g == 1:
        return jnp.full((1, LANES), values[2], f32)
    return jnp.where(low_lanes(1), values[0], values[1])


def fold_sublanes(parts):
    place = lax.broadcasted_iota(jnp.int32, (8, LANES), 0)
    step = 1
    while len(parts) > 1:
        first = (place & step) == 0
        parts = [
            jnp.where(first, a, b) + pltpu.roll(jnp.where(first, b, a), 8 - step, 0)
            for a, b in zip(parts[0::2], parts[1::2])
        ]
        step *= 2
    return parts[0]


def each_row(body, together):
    def some(k, carry):
        for i in range(together):
            body(k * together + i)
        return carry

    lax.fori_loop(0, ROWS // together, some, 0)


def spread(values, q, j):
    return jnp.broadcast_to(values[8 * q : 8 * q + 8, j : j + 1], (8, LANES))


def softplus(v):
    return jnp.maximum(v, 0.0) + jnp.log1p(jnp.exp(-jnp.abs(v)))


def project_kernel(
    tok,
    in_weight,
    conv_weight,
    conv_bias,
    step_bias,
    decay_log,
    inner,
    steps,
    compact,
    totals,
    conv_w,
    taps,
    weight,
):
    load_taps(conv_weight, conv_bias, taps)
    source = in_weight[...].astype(f32)
    chan_b, chan_c = source[:, 384:400], source[:, 400:416]
    step_w = [jnp.broadcast_to(source[:, 416 + h : 417 + h], (WIDTH, HALF)) for h in range(3)]
    wide = [
        source[:, 192:384],
        chan_c,
        chan_c,
        chan_b,
        jnp.zeros((WIDTH, 16), f32),
        step_w[0],
        step_w[1],
        step_w[2],
        step_w[2],
    ]
    weight[...] = jnp.concatenate(wide, axis=1).astype(bf16)
    conv_w[...] = weight[:, 0:256]
    step_turned = jnp.concatenate([source[:, 416:419], jnp.zeros((WIDTH, 125), f32)], axis=1)
    step_turned = step_turned.T[0:8, :].astype(bf16)

    def own_row(r):
        out = dot(tok[r], weight[...], ((0,), (0,))).astype(bf16)
        compact[r] = dot(step_turned, tok[r], ((1,), (0,))).astype(bf16).astype(f32)
        for g in range(2):
            inner[r, g] = out[:, g * 128 : g * 128 + 128]
            raw = out[:, 256 + g * 128 : 384 + g * 128].astype(f32) + by_head(step_bias, g)
            steps[r, g] = softplus(raw)

    each_row(own_row, 16)

    head = lax.broadcasted_iota(jnp.int32, (8, LANES), 0)

    def head_rows(ref):
        return jnp.where(head == 0, ref[0], jnp.where(head == 1, ref[1], ref[2]))

    step = softplus(compact[...] + head_rows(step_bias))
    log_decay = (-jnp.exp(head_rows(decay_log)) * step).reshape(ROWS * 8, LANES)
    log_decay = jnp.concatenate(split(log_decay), axis=1)
    from_at = lax.broadcasted_iota(jnp.int32, (2 * COLS, COLS), 0) & (COLS - 1)
    to_at = lax.broadcasted_iota(jnp.int32, (2 * COLS, COLS), 1)
    later = jnp.where(from_at > to_at, 1.0, 0.0).astype(bf16)
    suffix = dot(log_decay, later, ((1,), (0,)))
    whole = dot(log_decay, jnp.ones((2 * COLS, COLS), bf16), ((1,), (0,)))
    compact[...] = step * jnp.exp(suffix).reshape(ROWS, 8, LANES)
    totals[...] = jnp.exp(whole).reshape(ROWS, 8, LANES)


def pack_kernel(tok, left, right, *outs):
    for out, r in zip(outs, (ROWS - 1, 0)):
        sides = [left[r : r + 1, :].astype(f32), right[r : r + 1, :].astype(f32)]
        sides = jnp.concatenate(sides + [jnp.zeros((14, WIDTH), f32)], axis=0)
        sides = jnp.concatenate([sides, jnp.zeros((16, LANES - WIDTH), f32)], axis=1)
        out[0:WIDTH, :] = tok[r]
        out[WIDTH:, :] = sides.astype(bf16)


def load_taps(conv_weight, conv_bias, taps):
    for k in range(10):
        v = conv_bias[...] if k == 9 else conv_weight[k // 3, k % 3 : k % 3 + 1, :]
        taps[0, k : k + 1, :] = v[:, 0:128]
        tail = [v[:, 128:192], v[:, 208:224], v[:, 208:224], v[:, 192:208]]
        taps[1, k : k + 1, :] = jnp.concatenate(tail + [jnp.zeros((1, 16), f32)], axis=1)


def conv_part(tokens, conv_w, dims):
    return dot(tokens, conv_w[...], dims).astype(bf16).astype(f32)


def put_sides(left, right, conv_w, proj, begins, first, count):
    for ref, at in ((left, 7), (right, 136)):
        out = conv_part(ref[...], conv_w, ((1,), (0,)))
        for g in range(2):
            proj[first : first + count, g, at, :] = out[
                begins : begins + count, g * 128 : g * 128 + 128
            ]


def conv_row(proj, taps, at):
    parts = []
    for g in range(2):
        acc = jnp.broadcast_to(taps[g, 9:10, :], (COLS, LANES))
        for a in range(3):
            for b in range(3):
                k = a * 3 + b
                acc = acc + taps[g, k : k + 1, :] * proj[at + a, g, 7 + b : 135 + b, :]
        parts.append(silu(acc).astype(bf16).astype(f32))
    return parts


def finish_row(parts, steps, compact, totals, xdt, act, bct, maps, ends):
    maps[...] = parts[1].astype(bf16)
    turned = parts[1].T
    chan_b = turned[96:112, :]
    bct[0:16, :] = chan_b
    bct[16:32, :] = turned[64:80, :]
    other = pltpu.roll(parts[1], HALF, 1)
    whole = [parts[0], jnp.where(low_lanes(COLS), parts[1], other)]
    for g in range(2):
        act[g] = whole[g].astype(bf16)
        xdt[g] = steps[g] * whole[g]
    weighted = [compact[h : h + 1, :] * chan_b for h in range(3)]
    weighted = jnp.concatenate(split(jnp.concatenate(weighted, axis=0)), axis=0)
    inner_x = jnp.concatenate(whole, axis=1).astype(bf16)
    state = dot(weighted, inner_x, ((1,), (0,)))
    state = state[0:48, :] + state[48:96, :]
    first = jnp.where(low_lanes(16), state[0:16, 0:128], state[16:32, 0:128])
    third = jnp.where(low_lanes(), state[32:40, 128:256], state[40:48, 128:256])
    total = jnp.where(low_lanes(1), totals[0:1, :], totals[1:2, :])
    rest = jnp.concatenate([total, totals[2:3, :], jnp.zeros((2, LANES), f32)], axis=0)
    ends[0] = jnp.concatenate([first[0:8, :], third[0:4, :], rest], axis=0)
    ends[1] = jnp.concatenate([first[8:16, :], third[4:8, :], rest], axis=0)


def inside_kernel(
    inner,
    left,
    right,
    steps,
    compact,
    totals,
    conv_w,
    taps,
    decay_log,
    xdt,
    decay,
    act,
    bct,
    maps,
    ends,
    proj,
):
    put_sides(left, right, conv_w, proj, 0, 0, ROWS)
    rate = [-jnp.exp(by_head(decay_log, g)) for g in range(2)]

    def own_row(r):
        for g in range(2):
            proj[r, g, 8:136, :] = inner[r, g].astype(f32)
            decay[r, g] = jnp.exp(rate[g] * steps[r, g])

    each_row(own_row, 4)

    def some(k, carry):
        for i in range(7):
            r = 1 + 7 * k + i
            parts = conv_row(proj, taps, r - 1)
            refs = [ref.at[r] for ref in (steps, compact, totals, xdt, act, bct, maps)]
            finish_row(parts, *refs, ends.at[pl.ds(2 * r, 2)])
        return carry

    lax.fori_loop(0, 2, some, 0)


def edge_kernel(
    inner,
    above,
    below,
    left,
    right,
    steps,
    compact,
    totals,
    conv_w,
    taps,
    ends,
    xdt,
    act,
    bct,
    maps,
    *refs,
):
    ends_out, (proj, held) = refs[:CHIPS], refs[CHIPS:]
    put_sides(left, right, conv_w, proj, 0, 1, 2)
    put_sides(left, right, conv_w, proj, ROWS - 2, 3, 2)
    for at, ref in ((0, above), (5, below)):
        out = conv_part(ref[0:WIDTH, :], conv_w, ((0,), (0,)))
        sides = conv_part(ref[WIDTH:, 0:WIDTH], conv_w, ((1,), (0,)))
        for g in range(2):
            proj[at, g, 8:136, :] = out[:, g * 128 : g * 128 + 128]
            proj[at, g, 7:8, :] = sides[0:1, g * 128 : g * 128 + 128]
            proj[at, g, 136:137, :] = sides[1:2, g * 128 : g * 128 + 128]
    for at, r in ((1, 0), (2, 1), (3, ROWS - 2), (4, ROWS - 1)):
        for g in range(2):
            proj[at, g, 8:136, :] = inner[r, g].astype(f32)
    held[...] = ends[...]
    for e, r in enumerate((0, ROWS - 1)):
        parts = conv_row(proj, taps, 3 * e)
        own = [ref.at[r] for ref in (steps, compact, totals)]
        mine = [ref.at[e] for ref in (xdt, act, bct, maps)]
        finish_row(parts, *own, *mine, held.at[pl.ds(2 * r, 2)])
    member, _ = line()
    for k, out in enumerate(ends_out):
        out[...] = held[pl.ds((member + k) % CHIPS * 8, 8)]


def cells_kernel(maps_in, maps_edge, cmap):
    for r in range(ROWS):
        cmap[:, r, :] = pltpu.roll(row_of((maps_in, maps_edge), r)[...].astype(f32), HALF, 1)


def row_of(pair, r):
    inside, edge = pair
    if r in (0, ROWS - 1):
        return edge.at[0 if r == 0 else 1]
    return inside.at[r]


def line():
    gx = lax.axis_index("gx")
    return gx % 4, gx // 4


def part_of(ref, i, at=None):
    box = ref if at is None else ref.at[at]
    return (box[i, 0:8, :], box[i, 8:16, :]), (box[i, 12:13, :], box[i, 13:14, :])


def put(ref, i, tiles, decays=None):
    ref[i, 0:8, :] = tiles[0]
    ref[i, 8:16, :] = tiles[1]
    if decays is not None:
        ref[i, 12:13, :] = decays[0]
        ref[i, 13:14, :] = decays[1]


def chain(tiles, step):
    return [d * a + b for a, b, d in zip(tiles, *step)]


def product(a, b):
    return [u * v for u, v in zip(a, b)]


def members_kernel(*refs):
    parts, (out, held) = refs[:CHIPS], refs[CHIPS:]
    member, _ = line()
    for k, part in enumerate(parts):
        held[(member + CHIPS - k) % CHIPS] = part[...]
    for i in range(8):
        tiles, decays = part_of(held, i, 0)
        for m in range(1, CHIPS):
            step = part_of(held, i, m)
            tiles, decays = chain(tiles, step), product(decays, step[1])
        put(out, i, tiles, decays)


def pair_kernel(mine, theirs, out):
    _, z = line()
    odd = z % 2 == 1
    for i in range(8):
        a, b = part_of(mine, i), part_of(theirs, i)
        after, before = chain(b[0], a), chain(a[0], b)
        tiles = [jnp.where(odd, u, v) for u, v in zip(after, before)]
        put(out, i, tiles, product(a[1], b[1]))


def carry_kernel(near, mid, far, theirs, *refs):
    parts, outs, held = refs[:CHIPS], refs[CHIPS : 2 * CHIPS], refs[-1]
    member, z = line()
    odd = z % 2 == 1
    for k, part in enumerate(parts):
        held[(member + CHIPS - k) % CHIPS] = part[...]
    for i in range(8):
        tiles = part_of(far, i)[0]
        for part in (mid, near):
            tiles = chain(tiles, part_of(part, i))
        tiles = [jnp.where(odd, u, v) for u, v in zip(chain(tiles, part_of(theirs, i)), tiles)]
        for m in range(CHIPS):
            step = part_of(held, i, m)
            put(held.at[m], i, tiles)
            tiles = chain(tiles, step)
    for k, out in enumerate(outs):
        out[...] = held[(member + k) % CHIPS]


def starts(carry, r):
    third = jnp.concatenate([carry[2 * r, 8:12, :], carry[2 * r + 1, 8:12, :]], axis=0)
    return [carry[2 * r, 0:8, :], carry[2 * r + 1, 0:8, :], third]


def bottom_kernel(xdt_in, xdt_edge, decay, bct_in, bct_edge, *refs, half):
    if half:
        state_in, bottom = refs
        begin = [state_in[i] for i in range(3 * ROWS)]
    else:
        bottom, state_out = refs
        begin = [jnp.zeros((8, LANES), f32)] * (3 * ROWS)
    low = low_lanes()
    xdt = [row_of((xdt_in, xdt_edge), r) for r in range(ROWS)]
    bct = [row_of((bct_in, bct_edge), r) for r in range(ROWS)]

    def block(k, state):
        state = list(state)
        base = pl.multiple_of((half * HALVED + k) * BLOCK, BLOCK)
        maps = [pltpu.roll(bct[r][0:16, :], COLS - base, 1) for r in range(ROWS)]
        for j in range(BLOCK):
            cols = [jnp.zeros((8, LANES), f32)] * 3
            for r in range(ROWS):
                wide = [spread(maps[r], q, j) for q in range(2)]
                wide.append(jnp.where(low, wide[0], wide[1]))
                x = [xdt[r][g, pl.ds(base + j, 8, stride=0), :] for g in range(2)]
                d = [decay[r, g, pl.ds(base + j, 8, stride=0), :] for g in range(2)]
                for q in range(3):
                    g = q // 2
                    state[3 * r + q] = d[g] * state[3 * r + q] + x[g] * wide[q]
                    cols[q] = d[g] * cols[q] + state[3 * r + q]
            for q in range(3):
                bottom[k, j * 24 + 8 * q : j * 24 + 8 * q + 8, :] = cols[q]
        for g in range(2):
            whole = decay[0, g, pl.ds(base, BLOCK), :]
            for r in range(1, ROWS):
                whole = whole * decay[r, g, pl.ds(base, BLOCK), :]
            bottom[k, 384 + 16 * g : 400 + 16 * g, :] = whole
        return tuple(state)

    state = lax.fori_loop(0, HALVED, block, tuple(begin))
    if not half:
        for i in range(3 * ROWS):
            state_out[i] = state[i]


def weight_kernel(steps, decay, decay_log, coef):
    row_at = lax.broadcasted_iota(jnp.int32, (COLS, 2 * COLS), 0)
    col_at = lax.broadcasted_iota(jnp.int32, (COLS, 2 * COLS), 1) & (COLS - 1)
    upto = jnp.where(col_at <= row_at, 1.0, 0.0).astype(bf16)
    rate = [-jnp.exp(by_head(decay_log, g)) for g in range(2)]
    rate = jnp.concatenate(rate, axis=1)

    def some(k, below):
        below = list(below)
        for i in range(4):
            r = ROWS - 1 - (k * 4 + i)
            along = rate * jnp.concatenate([steps[r, 0], steps[r, 1]], axis=1)
            along = dot(upto, jnp.concatenate(split(along), axis=0), ((1,), (0,)))
            along = jnp.exp(along)
            for g in range(2):
                coef[r, g] = along[:, g * 128 : g * 128 + 128] * below[g]
                below[g] = below[g] * decay[r, g]
        return tuple(below)

    lax.fori_loop(0, ROWS // 4, some, (jnp.ones((COLS, LANES), f32),) * 2)


def add_kernel(coef, left_half, right_half, *refs):
    parts, (mine, theirs, carry, hold) = refs[:CHIPS], refs[CHIPS:]
    core, _ = place()
    member, _ = line()
    for k, part in enumerate(parts):
        carry[pl.ds((member + CHIPS - k) % CHIPS * 8, 8)] = part[...]
    for r in range(ROWS):
        hold[3 * r], hold[3 * r + 1], hold[3 * r + 2] = starts(carry, r)

    def block(k, _, source, out, base):
        for at in range(0, BLOCK, 4):
            sums = [
                source[k, 24 * j + 8 * q : 24 * j + 8 * q + 8, :]
                for j in range(at, at + 4)
                for q in range(3)
            ]
            for r in range(ROWS):
                tiles = [hold[3 * r + q] for q in range(3)]
                for j in range(4):
                    c = base + k * BLOCK + at + j
                    w = [coef[r, g, pl.ds(c, 8, stride=0), :] for g in range(2)]
                    for q in range(3):
                        sums[3 * j + q] = sums[3 * j + q] + w[q // 2] * tiles[q]
            for j in range(4):
                for q in range(3):
                    row = 24 * (at + j) + 8 * q
                    out[k, row : row + 8, :] = sums[3 * j + q]
        out[k, 384:416, :] = source[k, 384:416, :]
        return 0

    def both(outs):
        for half, source in enumerate((left_half, right_half)):
            run = functools.partial(block, source=source, out=outs[half], base=half * HALF)
            lax.fori_loop(0, HALVED, run, 0)

    @pl.when(core == 0)
    def _():
        both((mine, theirs))

    @pl.when(core != 0)
    def _():
        both((theirs, mine))


def gating_kernel(decay, tok, in_weight, gating, reach, weight):
    source = in_weight[...].astype(f32)
    wide = [source[:, 0:INNER], jnp.zeros((WIDTH, HALF), f32)]
    weight[...] = jnp.concatenate(wide, axis=1).astype(bf16)

    def some(k, along):
        along = list(along)
        for i in range(4):
            r = k * 4 + i
            gate = dot(tok[r], weight[...], ((0,), (0,))).astype(bf16).astype(f32)
            for g in range(2):
                along[g] = along[g] * decay[r, g]
                gated = silu(gate[:, g * 128 : g * 128 + 128])
                gating[r, g] = gated
                reach[r, g] = along[g] * gated
        return tuple(along)

    lax.fori_loop(0, ROWS // 4, some, (jnp.ones((COLS, LANES), f32),) * 2)


def local_kernel(
    begins,
    xdt_in,
    xdt_edge,
    decay,
    bct_in,
    bct_edge,
    carry,
    act_in,
    act_edge,
    gating,
    skip_gain,
    *refs,
):
    if begins:
        track_in, gated, local = refs
    else:
        gated, track, local = refs
    low = low_lanes()
    xdt = [row_of((xdt_in, xdt_edge), r) for r in range(ROWS)]
    bct = [row_of((bct_in, bct_edge), r) for r in range(ROWS)]
    act = [row_of((act_in, act_edge), r) for r in range(ROWS)]
    count = ROWS // 2
    begin = []
    for i in range(count):
        begin += starts(carry, begins + i)

    def block(cb, state):
        state = list(state)
        base = cb * BLOCK
        maps = [pltpu.roll(bct[begins + i][...], COLS - base, 1) for i in range(count)]
        for j in range(BLOCK):
            if begins:
                cols = [track_in[cb, j * 24 + 8 * q : j * 24 + 8 * q + 8, :] for q in range(3)]
            else:
                cols = [jnp.zeros((8, LANES), f32)] * 3
            reads = []
            for i in range(count):
                r = begins + i
                wide = [spread(maps[i], q, j) for q in range(4)]
                b_all = [wide[0], wide[1], jnp.where(low, wide[0], wide[1])]
                x = [xdt[r][g, pl.ds(base + j, 8, stride=0), :] for g in range(2)]
                d = [decay[r, g, pl.ds(base + j, 8, stride=0), :] for g in range(2)]
                for q in range(3):
                    g = q // 2
                    state[3 * i + q] = d[g] * state[3 * i + q] + x[g] * b_all[q]
                    cols[q] = d[g] * cols[q] + state[3 * i + q]
                reads.append(wide[2] * cols[0] + wide[3] * cols[1])
                reads.append(jnp.where(low, wide[2], wide[3]) * cols[2])
            if not begins:
                for q in range(3):
                    track[cb, j * 24 + 8 * q : j * 24 + 8 * q + 8, :] = cols[q]
            for k in range(2):
                local[k, :, base + j, :] = fold_sublanes(reads[8 * k : 8 * k + 8])
        return tuple(state)

    lax.fori_loop(0, BLOCKS, block, tuple(begin))
    for i in range(count):
        r = begins + i
        for g in range(2):
            mixed = local[i // 4, (i % 4) * 2 + g]
            if g == 1:
                mixed = mixed + pltpu.roll(mixed, HALF, 1)
            mixed = mixed + by_head(skip_gain, g) * act[r][g].astype(f32)
            gated[i, g] = mixed * gating[r, g]


def place():
    gy = lax.axis_index("gy")
    return gy % 2, gy // 2


def rows_of(j, q):
    return pl.ds(pl.multiple_of(j * 24 + 8 * q, 8), 8)


def decay_of(j, q):
    return pl.ds(BLOCK * (24 + q // 2) + j, 8, stride=0)


def join_kernel(mine, theirs, *outs):
    core, chip = place()
    for k, out in enumerate(outs):
        piece = (chip + k) % CHIPS

        def column(j, _):
            for q in range(3):
                a, b = mine[piece, rows_of(j, q), :], theirs[piece, rows_of(j, q), :]
                da, db = mine[piece, decay_of(j, q), :], theirs[piece, decay_of(j, q), :]
                out[rows_of(j, q), :] = jnp.where(core == 0, db * a + b, da * b + a)
            return 0

        lax.fori_loop(0, BLOCK, column, 0, unroll=4)
        rest = pl.ds(BLOCK * 24, BLOCK * 2)
        out[rest, :] = mine[piece, rest, :] * theirs[piece, rest, :]


def col_prefix_kernel(*refs):
    parts, outs, held, ready = refs[:CHIPS], refs[CHIPS : 2 * CHIPS], refs[-2], refs[-1]
    _, chip = place()
    for k, part in enumerate(parts):
        held[(chip + CHIPS - k) % CHIPS] = part[...]

    def column(j, _):
        for q in range(3):
            state = jnp.zeros((8, LANES), f32)
            for s in range(CHIPS):
                ready[s, rows_of(j, q), :] = state
                state = held[s, decay_of(j, q), :] * state + held[s, rows_of(j, q), :]
        return 0

    lax.fori_loop(0, BLOCK, column, 0, unroll=4)
    for k, out in enumerate(outs):
        out[...] = ready[(chip + k) % CHIPS]


def share_kernel(*refs):
    parts, (mine, theirs, own, other) = refs[:CHIPS], refs[CHIPS:]
    core, chip = place()
    for k, part in enumerate(parts):
        piece = (chip + CHIPS - k) % CHIPS

        def column(j, _):
            for q in range(3):
                upper = part[rows_of(j, q), :]
                a, b = mine[piece, rows_of(j, q), :], theirs[piece, rows_of(j, q), :]
                da, db = mine[piece, decay_of(j, q), :], theirs[piece, decay_of(j, q), :]
                lower = jnp.where(core == 0, da * upper + a, db * upper + b)
                own[piece, rows_of(j, q), :] = jnp.where(core == 0, upper, lower)
                other[piece, rows_of(j, q), :] = jnp.where(core == 0, lower, upper)
            return 0

        lax.fori_loop(0, BLOCK, column, 0, unroll=4)


def reads_kernel(states, cmap, carried, *, half):
    low = low_lanes()
    core, _ = place()

    def block(k, _):
        for j in range(BLOCK):
            first, second, third = [
                states[k, j * 24 + 8 * q : j * 24 + 8 * q + 8, :] for q in range(3)
            ]
            turned = pltpu.roll(third, HALF, 1)
            right = [jnp.where(low, third, turned), jnp.where(low, turned, third)]
            whole = jnp.concatenate(
                [
                    jnp.concatenate([first, second], axis=0),
                    jnp.concatenate(right, axis=0),
                ],
                axis=1,
            )
            at = k * BLOCK + j
            reads = cmap[(core ^ half) * HALF + at][:, 0:32].astype(bf16)
            result = dot(reads, jnp.concatenate(split(whole), axis=0), ((1,), (0,)))
            for g in range(2):
                carried[:, g, at, :] = result[:, g * 128 : g * 128 + 128]
        return 0

    lax.fori_loop(0, HALVED, block, 0, unroll=HALVED)


def exit_kernel(
    own, other, cmap, gated_a, gated_b, reach, norm_gain, out_weight, out, carried
):
    core, _ = place()
    reads_kernel(other, cmap, carried, half=1)
    turned = out_weight[...].astype(f32).T
    weight = jnp.concatenate([turned, jnp.zeros((WIDTH, HALF), f32)], axis=1).astype(bf16)
    pad = jnp.zeros((1, HALF), f32)
    gain = [norm_gain[:, 0:128], jnp.concatenate([norm_gain[:, 128:192], pad], axis=1)]

    def row(r, begins, gated):
        i = r - begins
        parts = []
        for g in range(2):
            a, b = own[r, g], carried[r, g]
            both = [jnp.where(core == 0, a, b), jnp.where(core == 0, b, a)]
            parts.append(gated[i, g] + reach[r, g] * jnp.concatenate(both, axis=0))
        total = jnp.sum(parts[0] * parts[0] + parts[1] * parts[1], axis=1, keepdims=True)
        scale = lax.rsqrt(total * (1.0 / INNER) + norm_eps)
        normed = [(parts[g] * scale * gain[g]).astype(bf16) for g in range(2)]
        result = dot(weight, jnp.concatenate(normed, axis=1), ((1,), (1,)))
        out[r] = result.astype(bf16)

    for begins, gated in ((0, gated_a), (ROWS // 2, gated_b)):
        for i in range(ROWS // 2):
            row(begins + i, begins, gated)


def call(kernel, spaces, shapes, scratch, *operands, after=()):
    kinds = {"v": pltpu.VMEM, "s": pltpu.SMEM, "h": pl.ANY}
    first, waits = len(operands), len(after)
    spaces, operands = spaces + "h" * waits, operands + tuple(after)

    def inner(*refs):
        kernel(*refs[:first], *refs[first + waits :])

    return pl.pallas_call(
        inner,
        in_specs=[pl.BlockSpec(memory_space=kinds[k]) for k in spaces],
        out_specs=[pl.BlockSpec(memory_space=kinds[k]) for _, _, k in shapes],
        out_shape=[jax.ShapeDtypeStruct(s, t) for s, t, _ in shapes],
        scratch_shapes=scratch,
        compiler_params=pltpu.CompilerParams(vmem_limit_bytes=VMEM),
    )(*operands)


def steps(axis):
    count = lax.axis_size(axis)
    up = [(i, i + 1) for i in range(count - 1)]
    return up, [(j, i) for i, j in up]


def on_device(
    tokens,
    in_weight,
    conv_weight,
    conv_bias,
    step_bias,
    decay_log,
    skip_gain,
    norm_gain,
    out_weight,
):
    to_right, to_left = steps("gx")
    to_down, to_up = steps("gy")
    vmem = pltpu.VMEM
    last, first = tokens[:, :, COLS - 1], tokens[:, :, 0]
    left = lax.ppermute(last, "gx", to_right)
    right = lax.ppermute(first, "gx", to_left)
    rows8 = ((ROWS, 8, LANES), f32, "v")
    inner, step, compact, totals, conv_w, taps = call(
        project_kernel,
        "vvvvss",
        [(PLANE, bf16, "v"), (PLANE, f32, "v"), rows8, rows8]
        + [((WIDTH, 256), bf16, "v"), ((2, 16, LANES), f32, "v")],
        [vmem((WIDTH, 512), bf16)],
        tokens,
        in_weight,
        conv_weight,
        conv_bias.reshape(1, 224),
        step_bias,
        decay_log,
        after=(last, first),
    )
    edge_row = ((WIDTH + 16, LANES), bf16, "v")
    down_row, up_row = call(
        pack_kernel, "vvv", [edge_row] * 2, [], tokens, left, right, after=(conv_w,)
    )
    above = lax.ppermute(down_row, "gy", to_down)
    below = lax.ppermute(up_row, "gy", to_up)
    packet = ((8, 16, LANES), f32, "v")
    quarters = vmem((CHIPS,) + packet[0], f32)
    all_ends = ((2 * ROWS, 16, LANES), f32, "v")
    cells = ((COLS, ROWS, LANES), f32, "v")
    xdt, decay, act, bct, maps, ends = call(
        inside_kernel,
        "v" * 8 + "s",
        [
            (PLANE, f32, "v"),
            (PLANE, f32, "v"),
            (PLANE, bf16, "v"),
            ((ROWS, 32, COLS), f32, "v"),
            ((ROWS, COLS, LANES), bf16, "v"),
            all_ends,
        ],
        [vmem((ROWS, 2, 144, LANES), f32)],
        inner,
        left,
        right,
        step,
        compact,
        totals,
        conv_w,
        taps,
        decay_log,
        after=(up_row, down_row),
    )
    two = (2,) + PLANE[1:]
    xdt_edge, act_edge, bct_edge, maps_edge, *ends = call(
        edge_kernel,
        "v" * 11,
        [(two, f32, "v"), (two, bf16, "v"), ((2, 32, COLS), f32, "v")]
        + [((2, COLS, LANES), bf16, "v")]
        + [packet] * CHIPS,
        [vmem((6, 2, 144, LANES), f32), vmem(all_ends[0], f32)],
        inner,
        above,
        below,
        left,
        right,
        step,
        compact,
        totals,
        conv_w,
        taps,
        ends,
    )
    scanned = (xdt, xdt_edge, decay, bct, bct_edge)
    gx_count = lax.axis_size("gx")

    def members(pieces):
        moved = [pieces[0]] * CHIPS
        for k in (2, 1, 3):
            pairs = [(i, i // 4 * 4 + (i + k) % 4) for i in range(gx_count)]
            moved[k] = lax.ppermute(pieces[k], "gx", pairs)
        return moved

    piece, piece_out = (PIECE, f32, "v"), (PIECE_OUT, f32, "v")
    halves = ((HALVED,) + PIECE, f32, "v")
    tiles = ((3 * ROWS, 8, LANES), f32, "v")
    sent = ends[:1]
    left_half, middle = call(
        functools.partial(bottom_kernel, half=0),
        "vvvvv",
        [halves, tiles],
        [],
        *scanned,
        after=sent,
    )
    ends = members(ends)
    (whole,) = call(members_kernel, "vvvv", [packet], [quarters], *ends, after=(middle,))
    beside = lax.ppermute(whole, "gx", [(i, i ^ 4) for i in range(gx_count)])
    gating, reach = call(
        gating_kernel,
        "vvv",
        [(PLANE, f32, "v")] * 2,
        [vmem((WIDTH, 256), bf16)],
        decay,
        tokens,
        in_weight,
        after=(whole,),
    )
    (both,) = call(pair_kernel, "vv", [packet], [], whole, beside, after=(reach,))
    (right_half,) = call(
        functools.partial(bottom_kernel, half=1),
        "vvvvvv",
        [halves],
        [],
        *scanned,
        middle,
        after=(both,),
    )
    mid, near, far = [
        lax.ppermute(both, "gx", [(i, i + 8 * k) for i in range(gx_count - 8 * k)])
        for k in (2, 1, 3)
    ]
    carries = call(
        carry_kernel, "v" * 8, [packet] * CHIPS, [quarters], near, mid, far, beside, *ends,
        after=(right_half,),
    )
    (coef,) = call(
        weight_kernel, "vvs", [(PLANE, f32, "v")], [], step, decay, decay_log, after=carries[:1]
    )
    carries = members(carries)
    mine, theirs, carry = call(
        add_kernel,
        "v" * 7,
        [halves, halves, ((2 * ROWS, 16, LANES), f32, "v")],
        [vmem(tiles[0], f32)],
        coef,
        left_half,
        right_half,
        *carries,
    )
    gy_count = lax.axis_size("gy")
    swap = [(i, i ^ 1) for i in range(gy_count)]
    ahead = [[(i, (i + 2 * k) % gy_count) for i in range(gy_count)] for k in range(CHIPS)]

    def rotate(pieces):
        moved = [pieces[0]] * CHIPS
        for k in (2, 1, 3):
            moved[k] = lax.ppermute(pieces[k], "gy", ahead[k])
        return moved

    theirs = lax.ppermute(theirs, "gy", swap)
    joined = call(join_kernel, "vv", [piece] * CHIPS, [], mine, theirs)
    pieces = rotate(joined)
    half = ((ROWS // 2,) + PLANE[1:], f32, "v")
    local_scratch = vmem((2, 8, COLS, LANES), f32)
    inner = (*scanned, carry, act, act_edge, gating, skip_gain)
    gated_a, track = call(
        functools.partial(local_kernel, 0),
        "v" * 9 + "s",
        [half, ((BLOCKS,) + PIECE_OUT, f32, "v")],
        [local_scratch],
        *inner,
        after=joined[:1],
    )
    (cmap,) = call(cells_kernel, "vv", [cells], [], maps, maps_edge, after=joined[:1])
    pieces = call(
        col_prefix_kernel,
        "vvvv",
        [piece_out] * CHIPS,
        [vmem((CHIPS,) + PIECE, f32), vmem((CHIPS,) + PIECE_OUT, f32)],
        *pieces,
        after=(track, cmap),
    )
    above_chip = pieces[0]
    pieces = rotate(pieces)
    (gated_b,) = call(
        functools.partial(local_kernel, ROWS // 2),
        "v" * 9 + "sv",
        [half],
        [local_scratch],
        *inner,
        track,
        after=(above_chip,),
    )
    halves_out = ((HALVED,) + PIECE_OUT, f32, "v")
    own, other = call(
        share_kernel, "vvvvvv", [halves_out] * 2, [], *pieces, mine, theirs, after=(gated_b,)
    )
    sent = other
    other = lax.ppermute(sent, "gy", swap)
    half_plane = (ROWS, 2, HALF, LANES)
    (own,) = call(
        functools.partial(reads_kernel, half=0),
        "vv",
        [(half_plane, f32, "v")],
        [],
        own,
        cmap,
        after=(sent,),
    )
    (out,) = call(
        exit_kernel,
        "vvvvvvvv",
        [((ROWS, WIDTH, COLS), bf16, "v")],
        [vmem(half_plane, f32)],
        own,
        other,
        cmap,
        gated_a,
        gated_b,
        reach,
        norm_gain.reshape(1, INNER),
        out_weight,
    )
    return out


def solution(mesh):
    return jax.shard_map(
        on_device,
        mesh=mesh,
        in_specs=(P("gy", None, "gx"), P(), P(), P(), P(), P(), P(), P(), P()),
        out_specs=P("gy", None, "gx"),
        check_vma=False,
    )
```

```python
import functools

import jax
import jax.numpy as jnp
from jax import lax
from jax.experimental import pallas as pl
from jax.experimental.pallas import tpu as pltpu
from jax.sharding import PartitionSpec as P

f32, bf16 = jnp.float32, jnp.bfloat16
norm_eps = 1e-05
ROWS, COLS, WIDTH, LANES = 16, 128, 96, 128
INNER, STATE, HALF = 192, 16, 64
BLOCK, BLOCKS = 16, 8
HALVED, CHIPS = BLOCKS // 2, 4
PIECE, PIECE_OUT = (BLOCK * 26, LANES), (BLOCK * 24, LANES)
PLANE = (ROWS, 2, COLS, LANES)
VMEM = 12 * 1024 * 1024


def silu(v):
    return v / (1.0 + jnp.exp(-v))


def split(v):
    high = v.astype(bf16)
    return high, (v - high.astype(f32)).astype(bf16)


def dot(a, b, dims):
    return lax.dot_general(a, b, (dims, ((), ())), preferred_element_type=f32)


def low_lanes(rows=8):
    return lax.broadcasted_iota(jnp.int32, (rows, LANES), 1) < HALF


def by_head(values, g):
    if g == 1:
        return jnp.full((1, LANES), values[2], f32)
    return jnp.where(low_lanes(1), values[0], values[1])


def fold_sublanes(parts):
    place = lax.broadcasted_iota(jnp.int32, (8, LANES), 0)
    step = 1
    while len(parts) > 1:
        first = (place & step) == 0
        parts = [
            jnp.where(first, a, b) + pltpu.roll(jnp.where(first, b, a), 8 - step, 0)
            for a, b in zip(parts[0::2], parts[1::2])
        ]
        step *= 2
    return parts[0]


def each_row(body, together):
    def some(k, carry):
        for i in range(together):
            body(k * together + i)
        return carry

    lax.fori_loop(0, ROWS // together, some, 0)


def spread(values, q, j):
    return jnp.broadcast_to(values[8 * q : 8 * q + 8, j : j + 1], (8, LANES))


def softplus(v):
    return jnp.maximum(v, 0.0) + jnp.log1p(jnp.exp(-jnp.abs(v)))


def project_kernel(
    tok,
    in_weight,
    conv_weight,
    conv_bias,
    step_bias,
    decay_log,
    inner,
    steps,
    decay,
    compact,
    totals,
    conv_w,
    taps,
    weight,
):
    rate = [-jnp.exp(by_head(decay_log, g)) for g in range(2)]
    load_taps(conv_weight, conv_bias, taps)
    source = in_weight[...].astype(f32)
    chan_b, chan_c = source[:, 384:400], source[:, 400:416]
    step_w = [jnp.broadcast_to(source[:, 416 + h : 417 + h], (WIDTH, HALF)) for h in range(3)]
    wide = [
        source[:, 192:384],
        chan_c,
        chan_c,
        chan_b,
        jnp.zeros((WIDTH, 16), f32),
        step_w[0],
        step_w[1],
        step_w[2],
        step_w[2],
    ]
    weight[...] = jnp.concatenate(wide, axis=1).astype(bf16)
    conv_w[...] = weight[:, 0:256]
    step_turned = jnp.concatenate([source[:, 416:419], jnp.zeros((WIDTH, 125), f32)], axis=1)
    step_turned = step_turned.T[0:8, :].astype(bf16)

    def own_row(r):
        out = dot(tok[r], weight[...], ((0,), (0,))).astype(bf16)
        compact[r] = dot(step_turned, tok[r], ((1,), (0,))).astype(bf16).astype(f32)
        for g in range(2):
            inner[r, g] = out[:, g * 128 : g * 128 + 128]
            raw = out[:, 256 + g * 128 : 384 + g * 128].astype(f32) + by_head(step_bias, g)
            steps[r, g] = softplus(raw)
            decay[r, g] = jnp.exp(rate[g] * steps[r, g])

    each_row(own_row, 16)

    head = lax.broadcasted_iota(jnp.int32, (8, LANES), 0)

    def head_rows(ref):
        return jnp.where(head == 0, ref[0], jnp.where(head == 1, ref[1], ref[2]))

    step = softplus(compact[...] + head_rows(step_bias))
    log_decay = (-jnp.exp(head_rows(decay_log)) * step).reshape(ROWS * 8, LANES)
    log_decay = jnp.concatenate(split(log_decay), axis=1)
    from_at = lax.broadcasted_iota(jnp.int32, (2 * COLS, COLS), 0) & (COLS - 1)
    to_at = lax.broadcasted_iota(jnp.int32, (2 * COLS, COLS), 1)
    later = jnp.where(from_at > to_at, 1.0, 0.0).astype(bf16)
    suffix = dot(log_decay, later, ((1,), (0,)))
    whole = dot(log_decay, jnp.ones((2 * COLS, COLS), bf16), ((1,), (0,)))
    compact[...] = step * jnp.exp(suffix).reshape(ROWS, 8, LANES)
    totals[...] = jnp.exp(whole).reshape(ROWS, 8, LANES)


def pack_kernel(tok, left, right, *outs):
    for out, r in zip(outs, (ROWS - 1, 0)):
        sides = [left[r : r + 1, :].astype(f32), right[r : r + 1, :].astype(f32)]
        sides = jnp.concatenate(sides + [jnp.zeros((14, WIDTH), f32)], axis=0)
        sides = jnp.concatenate([sides, jnp.zeros((16, LANES - WIDTH), f32)], axis=1)
        out[0:WIDTH, :] = tok[r]
        out[WIDTH:, :] = sides.astype(bf16)


def load_taps(conv_weight, conv_bias, taps):
    for k in range(10):
        v = conv_bias[...] if k == 9 else conv_weight[k // 3, k % 3 : k % 3 + 1, :]
        taps[0, k : k + 1, :] = v[:, 0:128]
        tail = [v[:, 128:192], v[:, 208:224], v[:, 208:224], v[:, 192:208]]
        taps[1, k : k + 1, :] = jnp.concatenate(tail + [jnp.zeros((1, 16), f32)], axis=1)


def conv_part(tokens, conv_w, dims):
    return dot(tokens, conv_w[...], dims).astype(bf16).astype(f32)


def put_sides(left, right, conv_w, proj, begins, first, count):
    for ref, at in ((left, 7), (right, 136)):
        out = conv_part(ref[...], conv_w, ((1,), (0,)))
        for g in range(2):
            proj[first : first + count, g, at, :] = out[
                begins : begins + count, g * 128 : g * 128 + 128
            ]


def conv_row(proj, taps, at):
    parts = []
    for g in range(2):
        acc = jnp.broadcast_to(taps[g, 9:10, :], (COLS, LANES))
        for a in range(3):
            for b in range(3):
                k = a * 3 + b
                acc = acc + taps[g, k : k + 1, :] * proj[at + a, g, 7 + b : 135 + b, :]
        parts.append(silu(acc).astype(bf16).astype(f32))
    return parts


def finish_row(parts, steps, compact, totals, xdt, act, bct, maps, ends):
    maps[...] = parts[1].astype(bf16)
    turned = parts[1].T
    chan_b = turned[96:112, :]
    bct[0:16, :] = chan_b
    bct[16:32, :] = turned[64:80, :]
    other = pltpu.roll(parts[1], HALF, 1)
    whole = [parts[0], jnp.where(low_lanes(COLS), parts[1], other)]
    for g in range(2):
        act[g] = whole[g].astype(bf16)
        xdt[g] = steps[g] * whole[g]
    weighted = [compact[h : h + 1, :] * chan_b for h in range(3)]
    weighted = jnp.concatenate(split(jnp.concatenate(weighted, axis=0)), axis=0)
    inner_x = jnp.concatenate(whole, axis=1).astype(bf16)
    state = dot(weighted, inner_x, ((1,), (0,)))
    state = state[0:48, :] + state[48:96, :]
    first = jnp.where(low_lanes(16), state[0:16, 0:128], state[16:32, 0:128])
    third = jnp.where(low_lanes(), state[32:40, 128:256], state[40:48, 128:256])
    total = jnp.where(low_lanes(1), totals[0:1, :], totals[1:2, :])
    rest = jnp.concatenate([total, totals[2:3, :], jnp.zeros((2, LANES), f32)], axis=0)
    ends[0] = jnp.concatenate([first[0:8, :], third[0:4, :], rest], axis=0)
    ends[1] = jnp.concatenate([first[8:16, :], third[4:8, :], rest], axis=0)


def inside_kernel(
    inner,
    left,
    right,
    steps,
    compact,
    totals,
    conv_w,
    taps,
    xdt,
    act,
    bct,
    maps,
    ends,
    proj,
):
    put_sides(left, right, conv_w, proj, 0, 0, ROWS)

    def own_row(r):
        for g in range(2):
            proj[r, g, 8:136, :] = inner[r, g].astype(f32)

    each_row(own_row, 4)

    def some(k, carry):
        for i in range(7):
            r = 1 + 7 * k + i
            parts = conv_row(proj, taps, r - 1)
            refs = [ref.at[r] for ref in (steps, compact, totals, xdt, act, bct, maps)]
            finish_row(parts, *refs, ends.at[pl.ds(2 * r, 2)])
        return carry

    lax.fori_loop(0, 2, some, 0, unroll=2)


def edge_kernel(
    inner,
    above,
    below,
    left,
    right,
    steps,
    compact,
    totals,
    conv_w,
    taps,
    ends,
    xdt,
    act,
    bct,
    maps,
    *refs,
):
    ends_out, (proj, held) = refs[:CHIPS], refs[CHIPS:]
    put_sides(left, right, conv_w, proj, 0, 1, 2)
    put_sides(left, right, conv_w, proj, ROWS - 2, 3, 2)
    for at, ref in ((0, above), (5, below)):
        out = conv_part(ref[0:WIDTH, :], conv_w, ((0,), (0,)))
        sides = conv_part(ref[WIDTH:, 0:WIDTH], conv_w, ((1,), (0,)))
        for g in range(2):
            proj[at, g, 8:136, :] = out[:, g * 128 : g * 128 + 128]
            proj[at, g, 7:8, :] = sides[0:1, g * 128 : g * 128 + 128]
            proj[at, g, 136:137, :] = sides[1:2, g * 128 : g * 128 + 128]
    for at, r in ((1, 0), (2, 1), (3, ROWS - 2), (4, ROWS - 1)):
        for g in range(2):
            proj[at, g, 8:136, :] = inner[r, g].astype(f32)
    held[...] = ends[...]
    for e, r in enumerate((0, ROWS - 1)):
        parts = conv_row(proj, taps, 3 * e)
        own = [ref.at[r] for ref in (steps, compact, totals)]
        mine = [ref.at[e] for ref in (xdt, act, bct, maps)]
        finish_row(parts, *own, *mine, held.at[pl.ds(2 * r, 2)])
    member, _ = line()
    for k, out in enumerate(ends_out):
        out[...] = held[pl.ds((member + k) % CHIPS * 8, 8)]


def cells_kernel(maps_in, maps_edge, cmap):
    for r in range(ROWS):
        cmap[:, r, :] = pltpu.roll(row_of((maps_in, maps_edge), r)[...].astype(f32), HALF, 1)


def row_of(pair, r):
    inside, edge = pair
    if r in (0, ROWS - 1):
        return edge.at[0 if r == 0 else 1]
    return inside.at[r]


def line():
    gx = lax.axis_index("gx")
    return gx % 4, gx // 4


def part_of(ref, i, at=None):
    box = ref if at is None else ref.at[at]
    return (box[i, 0:8, :], box[i, 8:16, :]), (box[i, 12:13, :], box[i, 13:14, :])


def put(ref, i, tiles, decays=None):
    ref[i, 0:8, :] = tiles[0]
    ref[i, 8:16, :] = tiles[1]
    if decays is not None:
        ref[i, 12:13, :] = decays[0]
        ref[i, 13:14, :] = decays[1]


def chain(tiles, step):
    return [d * a + b for a, b, d in zip(tiles, *step)]


def product(a, b):
    return [u * v for u, v in zip(a, b)]


def members_kernel(*refs):
    parts, (out, held) = refs[:CHIPS], refs[CHIPS:]
    member, _ = line()
    for k, part in enumerate(parts):
        held[(member + CHIPS - k) % CHIPS] = part[...]
    for i in range(8):
        tiles, decays = part_of(held, i, 0)
        for m in range(1, CHIPS):
            step = part_of(held, i, m)
            tiles, decays = chain(tiles, step), product(decays, step[1])
        put(out, i, tiles, decays)


def pair_kernel(mine, theirs, out):
    _, z = line()
    odd = z % 2 == 1
    for i in range(8):
        a, b = part_of(mine, i), part_of(theirs, i)
        after, before = chain(b[0], a), chain(a[0], b)
        tiles = [jnp.where(odd, u, v) for u, v in zip(after, before)]
        put(out, i, tiles, product(a[1], b[1]))


def carry_kernel(near, mid, far, theirs, *refs):
    parts, outs, held = refs[:CHIPS], refs[CHIPS : 2 * CHIPS], refs[-1]
    member, z = line()
    odd = z % 2 == 1
    for k, part in enumerate(parts):
        held[(member + CHIPS - k) % CHIPS] = part[...]
    for i in range(8):
        tiles = part_of(far, i)[0]
        for part in (mid, near):
            tiles = chain(tiles, part_of(part, i))
        tiles = [jnp.where(odd, u, v) for u, v in zip(chain(tiles, part_of(theirs, i)), tiles)]
        for m in range(CHIPS):
            step = part_of(held, i, m)
            put(held.at[m], i, tiles)
            tiles = chain(tiles, step)
    for k, out in enumerate(outs):
        out[...] = held[(member + k) % CHIPS]


def starts(carry, r):
    third = jnp.concatenate([carry[2 * r, 8:12, :], carry[2 * r + 1, 8:12, :]], axis=0)
    return [carry[2 * r, 0:8, :], carry[2 * r + 1, 0:8, :], third]


def bottom_kernel(xdt_in, xdt_edge, decay, bct_in, bct_edge, *refs, half):
    if half:
        state_in, bottom = refs
        begin = [state_in[i] for i in range(3 * ROWS)]
    else:
        bottom, state_out = refs
        begin = [jnp.zeros((8, LANES), f32)] * (3 * ROWS)
    low = low_lanes()
    xdt = [row_of((xdt_in, xdt_edge), r) for r in range(ROWS)]
    bct = [row_of((bct_in, bct_edge), r) for r in range(ROWS)]

    def block(k, state):
        state = list(state)
        base = pl.multiple_of((half * HALVED + k) * BLOCK, BLOCK)
        maps = [pltpu.roll(bct[r][0:16, :], COLS - base, 1) for r in range(ROWS)]
        for j in range(BLOCK):
            cols = [jnp.zeros((8, LANES), f32)] * 3
            for r in range(ROWS):
                wide = [spread(maps[r], q, j) for q in range(2)]
                wide.append(jnp.where(low, wide[0], wide[1]))
                x = [xdt[r][g, pl.ds(base + j, 8, stride=0), :] for g in range(2)]
                d = [decay[r, g, pl.ds(base + j, 8, stride=0), :] for g in range(2)]
                for q in range(3):
                    g = q // 2
                    state[3 * r + q] = d[g] * state[3 * r + q] + x[g] * wide[q]
                    cols[q] = d[g] * cols[q] + state[3 * r + q]
            for q in range(3):
                bottom[k, j * 24 + 8 * q : j * 24 + 8 * q + 8, :] = cols[q]
        for g in range(2):
            whole = decay[0, g, pl.ds(base, BLOCK), :]
            for r in range(1, ROWS):
                whole = whole * decay[r, g, pl.ds(base, BLOCK), :]
            bottom[k, 384 + 16 * g : 400 + 16 * g, :] = whole
        return tuple(state)

    state = lax.fori_loop(0, HALVED, block, tuple(begin))
    if not half:
        for i in range(3 * ROWS):
            state_out[i] = state[i]


def weight_kernel(steps, decay, decay_log, coef):
    row_at = lax.broadcasted_iota(jnp.int32, (COLS, 2 * COLS), 0)
    col_at = lax.broadcasted_iota(jnp.int32, (COLS, 2 * COLS), 1) & (COLS - 1)
    upto = jnp.where(col_at <= row_at, 1.0, 0.0).astype(bf16)
    rate = [-jnp.exp(by_head(decay_log, g)) for g in range(2)]
    rate = jnp.concatenate(rate, axis=1)

    def some(k, below):
        below = list(below)
        for i in range(4):
            r = ROWS - 1 - (k * 4 + i)
            along = rate * jnp.concatenate([steps[r, 0], steps[r, 1]], axis=1)
            along = dot(upto, jnp.concatenate(split(along), axis=0), ((1,), (0,)))
            along = jnp.exp(along)
            for g in range(2):
                coef[r, g] = along[:, g * 128 : g * 128 + 128] * below[g]
                below[g] = below[g] * decay[r, g]
        return tuple(below)

    lax.fori_loop(0, ROWS // 4, some, (jnp.ones((COLS, LANES), f32),) * 2)


def add_kernel(coef, left_half, right_half, *refs):
    parts, (mine, theirs, carry, hold) = refs[:CHIPS], refs[CHIPS:]
    core, _ = place()
    member, _ = line()
    for k, part in enumerate(parts):
        carry[pl.ds((member + CHIPS - k) % CHIPS * 8, 8)] = part[...]
    for r in range(ROWS):
        hold[3 * r], hold[3 * r + 1], hold[3 * r + 2] = starts(carry, r)

    def block(k, _, source, out, base):
        for at in range(0, BLOCK, 4):
            sums = [
                source[k, 24 * j + 8 * q : 24 * j + 8 * q + 8, :]
                for j in range(at, at + 4)
                for q in range(3)
            ]
            for r in range(ROWS):
                tiles = [hold[3 * r + q] for q in range(3)]
                for j in range(4):
                    c = base + k * BLOCK + at + j
                    w = [coef[r, g, pl.ds(c, 8, stride=0), :] for g in range(2)]
                    for q in range(3):
                        sums[3 * j + q] = sums[3 * j + q] + w[q // 2] * tiles[q]
            for j in range(4):
                for q in range(3):
                    row = 24 * (at + j) + 8 * q
                    out[k, row : row + 8, :] = sums[3 * j + q]
        out[k, 384:416, :] = source[k, 384:416, :]
        return 0

    def both(outs):
        for half, source in enumerate((left_half, right_half)):
            run = functools.partial(block, source=source, out=outs[half], base=half * HALF)
            lax.fori_loop(0, HALVED, run, 0)

    @pl.when(core == 0)
    def _():
        both((mine, theirs))

    @pl.when(core != 0)
    def _():
        both((theirs, mine))


def gating_kernel(decay, tok, in_weight, gating, reach, weight):
    source = in_weight[...].astype(f32)
    wide = [source[:, 0:INNER], jnp.zeros((WIDTH, HALF), f32)]
    weight[...] = jnp.concatenate(wide, axis=1).astype(bf16)

    def some(k, along):
        along = list(along)
        for i in range(4):
            r = k * 4 + i
            gate = dot(tok[r], weight[...], ((0,), (0,))).astype(bf16).astype(f32)
            for g in range(2):
                along[g] = along[g] * decay[r, g]
                gated = silu(gate[:, g * 128 : g * 128 + 128])
                gating[r, g] = gated
                reach[r, g] = along[g] * gated
        return tuple(along)

    lax.fori_loop(0, ROWS // 4, some, (jnp.ones((COLS, LANES), f32),) * 2)


def local_kernel(
    begins,
    xdt_in,
    xdt_edge,
    decay,
    bct_in,
    bct_edge,
    carry,
    act_in,
    act_edge,
    gating,
    skip_gain,
    *refs,
):
    if begins:
        track_in, gated, local = refs
    else:
        gated, track, local = refs
    low = low_lanes()
    xdt = [row_of((xdt_in, xdt_edge), r) for r in range(ROWS)]
    bct = [row_of((bct_in, bct_edge), r) for r in range(ROWS)]
    act = [row_of((act_in, act_edge), r) for r in range(ROWS)]
    count = ROWS // 2
    begin = []
    for i in range(count):
        begin += starts(carry, begins + i)

    def block(cb, state):
        state = list(state)
        base = cb * BLOCK
        maps = [pltpu.roll(bct[begins + i][...], COLS - base, 1) for i in range(count)]
        for j in range(BLOCK):
            if begins:
                cols = [track_in[cb, j * 24 + 8 * q : j * 24 + 8 * q + 8, :] for q in range(3)]
            else:
                cols = [jnp.zeros((8, LANES), f32)] * 3
            reads = []
            for i in range(count):
                r = begins + i
                wide = [spread(maps[i], q, j) for q in range(4)]
                b_all = [wide[0], wide[1], jnp.where(low, wide[0], wide[1])]
                x = [xdt[r][g, pl.ds(base + j, 8, stride=0), :] for g in range(2)]
                d = [decay[r, g, pl.ds(base + j, 8, stride=0), :] for g in range(2)]
                for q in range(3):
                    g = q // 2
                    state[3 * i + q] = d[g] * state[3 * i + q] + x[g] * b_all[q]
                    cols[q] = d[g] * cols[q] + state[3 * i + q]
                reads.append(wide[2] * cols[0] + wide[3] * cols[1])
                reads.append(jnp.where(low, wide[2], wide[3]) * cols[2])
            if not begins:
                for q in range(3):
                    track[cb, j * 24 + 8 * q : j * 24 + 8 * q + 8, :] = cols[q]
            for k in range(2):
                local[k, :, base + j, :] = fold_sublanes(reads[8 * k : 8 * k + 8])
        return tuple(state)

    lax.fori_loop(0, BLOCKS, block, tuple(begin))
    for i in range(count):
        r = begins + i
        for g in range(2):
            mixed = local[i // 4, (i % 4) * 2 + g]
            if g == 1:
                mixed = mixed + pltpu.roll(mixed, HALF, 1)
            mixed = mixed + by_head(skip_gain, g) * act[r][g].astype(f32)
            gated[i, g] = mixed * gating[r, g]


def place():
    gy = lax.axis_index("gy")
    return gy % 2, gy // 2


def rows_of(j, q):
    return pl.ds(pl.multiple_of(j * 24 + 8 * q, 8), 8)


def decay_of(j, q):
    return pl.ds(BLOCK * (24 + q // 2) + j, 8, stride=0)


def join_kernel(mine, theirs, *outs):
    core, chip = place()
    for k, out in enumerate(outs):
        piece = (chip + k) % CHIPS

        def column(j, _):
            for q in range(3):
                a, b = mine[piece, rows_of(j, q), :], theirs[piece, rows_of(j, q), :]
                da, db = mine[piece, decay_of(j, q), :], theirs[piece, decay_of(j, q), :]
                out[rows_of(j, q), :] = jnp.where(core == 0, db * a + b, da * b + a)
            return 0

        lax.fori_loop(0, BLOCK, column, 0, unroll=4)
        rest = pl.ds(BLOCK * 24, BLOCK * 2)
        out[rest, :] = mine[piece, rest, :] * theirs[piece, rest, :]


def col_prefix_kernel(*refs):
    parts, outs, held, ready = refs[:CHIPS], refs[CHIPS : 2 * CHIPS], refs[-2], refs[-1]
    _, chip = place()
    for k, part in enumerate(parts):
        held[(chip + CHIPS - k) % CHIPS] = part[...]

    def column(j, _):
        for q in range(3):
            state = jnp.zeros((8, LANES), f32)
            for s in range(CHIPS):
                ready[s, rows_of(j, q), :] = state
                state = held[s, decay_of(j, q), :] * state + held[s, rows_of(j, q), :]
        return 0

    lax.fori_loop(0, BLOCK, column, 0, unroll=4)
    for k, out in enumerate(outs):
        out[...] = ready[(chip + k) % CHIPS]


def share_kernel(*refs):
    parts, (mine, theirs, own, other) = refs[:CHIPS], refs[CHIPS:]
    core, chip = place()
    for k, part in enumerate(parts):
        piece = (chip + CHIPS - k) % CHIPS

        def column(j, _):
            for q in range(3):
                upper = part[rows_of(j, q), :]
                a, b = mine[piece, rows_of(j, q), :], theirs[piece, rows_of(j, q), :]
                da, db = mine[piece, decay_of(j, q), :], theirs[piece, decay_of(j, q), :]
                lower = jnp.where(core == 0, da * upper + a, db * upper + b)
                own[piece, rows_of(j, q), :] = jnp.where(core == 0, upper, lower)
                other[piece, rows_of(j, q), :] = jnp.where(core == 0, lower, upper)
            return 0

        lax.fori_loop(0, BLOCK, column, 0, unroll=4)


def reads_kernel(states, cmap, carried, *, half):
    low = low_lanes()
    core, _ = place()

    def block(k, _):
        for j in range(BLOCK):
            first, second, third = [
                states[k, j * 24 + 8 * q : j * 24 + 8 * q + 8, :] for q in range(3)
            ]
            turned = pltpu.roll(third, HALF, 1)
            right = [jnp.where(low, third, turned), jnp.where(low, turned, third)]
            whole = jnp.concatenate(
                [
                    jnp.concatenate([first, second], axis=0),
                    jnp.concatenate(right, axis=0),
                ],
                axis=1,
            )
            at = k * BLOCK + j
            reads = cmap[(core ^ half) * HALF + at][:, 0:32].astype(bf16)
            result = dot(reads, jnp.concatenate(split(whole), axis=0), ((1,), (0,)))
            for g in range(2):
                carried[:, g, at, :] = result[:, g * 128 : g * 128 + 128]
        return 0

    lax.fori_loop(0, HALVED, block, 0, unroll=HALVED)


def exit_kernel(
    own, other, cmap, gated_a, gated_b, reach, norm_gain, out_weight, out, carried
):
    core, _ = place()
    reads_kernel(other, cmap, carried, half=1)
    turned = out_weight[...].astype(f32).T
    weight = jnp.concatenate([turned, jnp.zeros((WIDTH, HALF), f32)], axis=1).astype(bf16)
    pad = jnp.zeros((1, HALF), f32)
    gain = [norm_gain[:, 0:128], jnp.concatenate([norm_gain[:, 128:192], pad], axis=1)]

    def row(r, begins, gated):
        i = r - begins
        parts = []
        for g in range(2):
            a, b = own[r, g], carried[r, g]
            both = [jnp.where(core == 0, a, b), jnp.where(core == 0, b, a)]
            parts.append(gated[i, g] + reach[r, g] * jnp.concatenate(both, axis=0))
        total = jnp.sum(parts[0] * parts[0] + parts[1] * parts[1], axis=1, keepdims=True)
        scale = lax.rsqrt(total * (1.0 / INNER) + norm_eps)
        normed = [(parts[g] * scale * gain[g]).astype(bf16) for g in range(2)]
        result = dot(weight, jnp.concatenate(normed, axis=1), ((1,), (1,)))
        out[r] = result.astype(bf16)

    for begins, gated in ((0, gated_a), (ROWS // 2, gated_b)):
        for i in range(ROWS // 2):
            row(begins + i, begins, gated)


def call(kernel, spaces, shapes, scratch, *operands, after=()):
    kinds = {"v": pltpu.VMEM, "s": pltpu.SMEM, "h": pl.ANY}
    first, waits = len(operands), len(after)
    spaces, operands = spaces + "h" * waits, operands + tuple(after)

    def inner(*refs):
        kernel(*refs[:first], *refs[first + waits :])

    return pl.pallas_call(
        inner,
        in_specs=[pl.BlockSpec(memory_space=kinds[k]) for k in spaces],
        out_specs=[pl.BlockSpec(memory_space=kinds[k]) for _, _, k in shapes],
        out_shape=[jax.ShapeDtypeStruct(s, t) for s, t, _ in shapes],
        scratch_shapes=scratch,
        compiler_params=pltpu.CompilerParams(vmem_limit_bytes=VMEM),
    )(*operands)


def steps(axis):
    count = lax.axis_size(axis)
    up = [(i, i + 1) for i in range(count - 1)]
    return up, [(j, i) for i, j in up]


def on_device(
    tokens,
    in_weight,
    conv_weight,
    conv_bias,
    step_bias,
    decay_log,
    skip_gain,
    norm_gain,
    out_weight,
):
    to_right, to_left = steps("gx")
    to_down, to_up = steps("gy")
    vmem = pltpu.VMEM
    last, first = tokens[:, :, COLS - 1], tokens[:, :, 0]
    left = lax.ppermute(last, "gx", to_right)
    right = lax.ppermute(first, "gx", to_left)
    rows8 = ((ROWS, 8, LANES), f32, "v")
    inner, step, decay, compact, totals, conv_w, taps = call(
        project_kernel,
        "vvvvss",
        [(PLANE, bf16, "v"), (PLANE, f32, "v"), (PLANE, f32, "v"), rows8, rows8]
        + [((WIDTH, 256), bf16, "v"), ((2, 16, LANES), f32, "v")],
        [vmem((WIDTH, 512), bf16)],
        tokens,
        in_weight,
        conv_weight,
        conv_bias.reshape(1, 224),
        step_bias,
        decay_log,
        after=(last, first),
    )
    edge_row = ((WIDTH + 16, LANES), bf16, "v")
    down_row, up_row = call(
        pack_kernel, "vvv", [edge_row] * 2, [], tokens, left, right, after=(conv_w,)
    )
    above = lax.ppermute(down_row, "gy", to_down)
    below = lax.ppermute(up_row, "gy", to_up)
    packet = ((8, 16, LANES), f32, "v")
    quarters = vmem((CHIPS,) + packet[0], f32)
    all_ends = ((2 * ROWS, 16, LANES), f32, "v")
    cells = ((COLS, ROWS, LANES), f32, "v")
    xdt, act, bct, maps, ends = call(
        inside_kernel,
        "v" * 8,
        [
            (PLANE, f32, "v"),
            (PLANE, bf16, "v"),
            ((ROWS, 32, COLS), f32, "v"),
            ((ROWS, COLS, LANES), bf16, "v"),
            all_ends,
        ],
        [vmem((ROWS, 2, 144, LANES), f32)],
        inner,
        left,
        right,
        step,
        compact,
        totals,
        conv_w,
        taps,
        after=(up_row, down_row),
    )
    two = (2,) + PLANE[1:]
    xdt_edge, act_edge, bct_edge, maps_edge, *ends = call(
        edge_kernel,
        "v" * 11,
        [(two, f32, "v"), (two, bf16, "v"), ((2, 32, COLS), f32, "v")]
        + [((2, COLS, LANES), bf16, "v")]
        + [packet] * CHIPS,
        [vmem((6, 2, 144, LANES), f32), vmem(all_ends[0], f32)],
        inner,
        above,
        below,
        left,
        right,
        step,
        compact,
        totals,
        conv_w,
        taps,
        ends,
    )
    scanned = (xdt, xdt_edge, decay, bct, bct_edge)
    gx_count = lax.axis_size("gx")

    def members(pieces):
        moved = [pieces[0]] * CHIPS
        for k in (2, 1, 3):
            pairs = [(i, i // 4 * 4 + (i + k) % 4) for i in range(gx_count)]
            moved[k] = lax.ppermute(pieces[k], "gx", pairs)
        return moved

    piece, piece_out = (PIECE, f32, "v"), (PIECE_OUT, f32, "v")
    halves = ((HALVED,) + PIECE, f32, "v")
    tiles = ((3 * ROWS, 8, LANES), f32, "v")
    sent = ends[:1]
    left_half, middle = call(
        functools.partial(bottom_kernel, half=0),
        "vvvvv",
        [halves, tiles],
        [],
        *scanned,
        after=sent,
    )
    ends = members(ends)
    (whole,) = call(members_kernel, "vvvv", [packet], [quarters], *ends, after=(middle,))
    beside = lax.ppermute(whole, "gx", [(i, i ^ 4) for i in range(gx_count)])
    gating, reach = call(
        gating_kernel,
        "vvv",
        [(PLANE, f32, "v")] * 2,
        [vmem((WIDTH, 256), bf16)],
        decay,
        tokens,
        in_weight,
        after=(whole,),
    )
    (both,) = call(pair_kernel, "vv", [packet], [], whole, beside, after=(reach,))
    (right_half,) = call(
        functools.partial(bottom_kernel, half=1),
        "vvvvvv",
        [halves],
        [],
        *scanned,
        middle,
        after=(both,),
    )
    mid, near, far = [
        lax.ppermute(both, "gx", [(i, i + 8 * k) for i in range(gx_count - 8 * k)])
        for k in (2, 1, 3)
    ]
    carries = call(
        carry_kernel, "v" * 8, [packet] * CHIPS, [quarters], near, mid, far, beside, *ends,
        after=(right_half,),
    )
    (coef,) = call(
        weight_kernel, "vvs", [(PLANE, f32, "v")], [], step, decay, decay_log, after=carries[:1]
    )
    carries = members(carries)
    mine, theirs, carry = call(
        add_kernel,
        "v" * 7,
        [halves, halves, ((2 * ROWS, 16, LANES), f32, "v")],
        [vmem(tiles[0], f32)],
        coef,
        left_half,
        right_half,
        *carries,
    )
    gy_count = lax.axis_size("gy")
    swap = [(i, i ^ 1) for i in range(gy_count)]
    ahead = [[(i, (i + 2 * k) % gy_count) for i in range(gy_count)] for k in range(CHIPS)]

    def rotate(pieces):
        moved = [pieces[0]] * CHIPS
        for k in (2, 1, 3):
            moved[k] = lax.ppermute(pieces[k], "gy", ahead[k])
        return moved

    theirs = lax.ppermute(theirs, "gy", swap)
    joined = call(join_kernel, "vv", [piece] * CHIPS, [], mine, theirs)
    pieces = rotate(joined)
    half = ((ROWS // 2,) + PLANE[1:], f32, "v")
    local_scratch = vmem((2, 8, COLS, LANES), f32)
    inner = (*scanned, carry, act, act_edge, gating, skip_gain)
    gated_a, track = call(
        functools.partial(local_kernel, 0),
        "v" * 9 + "s",
        [half, ((BLOCKS,) + PIECE_OUT, f32, "v")],
        [local_scratch],
        *inner,
        after=joined[:1],
    )
    (cmap,) = call(cells_kernel, "vv", [cells], [], maps, maps_edge, after=joined[:1])
    pieces = call(
        col_prefix_kernel,
        "vvvv",
        [piece_out] * CHIPS,
        [vmem((CHIPS,) + PIECE, f32), vmem((CHIPS,) + PIECE_OUT, f32)],
        *pieces,
        after=(track, cmap),
    )
    above_chip = pieces[0]
    pieces = rotate(pieces)
    (gated_b,) = call(
        functools.partial(local_kernel, ROWS // 2),
        "v" * 9 + "sv",
        [half],
        [local_scratch],
        *inner,
        track,
        after=(above_chip,),
    )
    halves_out = ((HALVED,) + PIECE_OUT, f32, "v")
    own, other = call(
        share_kernel, "vvvvvv", [halves_out] * 2, [], *pieces, mine, theirs, after=(gated_b,)
    )
    sent = other
    other = lax.ppermute(sent, "gy", swap)
    half_plane = (ROWS, 2, HALF, LANES)
    (own,) = call(
        functools.partial(reads_kernel, half=0),
        "vv",
        [(half_plane, f32, "v")],
        [],
        own,
        cmap,
        after=(sent,),
    )
    (out,) = call(
        exit_kernel,
        "vvvvvvvv",
        [((ROWS, WIDTH, COLS), bf16, "v")],
        [vmem(half_plane, f32)],
        own,
        other,
        cmap,
        gated_a,
        gated_b,
        reach,
        norm_gain.reshape(1, INNER),
        out_weight,
    )
    return out


def solution(mesh):
    return jax.shard_map(
        on_device,
        mesh=mesh,
        in_specs=(P("gy", None, "gx"), P(), P(), P(), P(), P(), P(), P(), P()),
        out_specs=P("gy", None, "gx"),
        check_vma=False,
    )
```
